256 devices in a mesh: cfg: 2 (over core), seq: 16 (over x_hi, z), fsdp: 8 (over y, x_lo).
Axes of the slice: x: 4 (x_hi: 2, x_lo: 2; x = x_hi * 2 + x_lo), y: 4, z: 8, core: 2. Of those that a mesh axis runs over, the one named last changes fastest.
Arguments:
- queries: bfloat16 [2, 1024, 4096], P('cfg', None, 'seq'), may hold values from -6 to 6
- key_vectors: bfloat16 [2, 16384, 4096], P('cfg', ('seq', 'fsdp')), may hold values from -6 to 6
- value_vectors: bfloat16 [2, 16384, 4096], P('cfg', ('seq', 'fsdp')), may hold values from -6 to 6
- cotangent: bfloat16 [1024, 5120], P(None, 'fsdp'), may hold values from -600 to 600
- out_weight: bfloat16 [4096, 5120], P('seq', 'fsdp'), may hold values from -0.09375 to 0.09375
- frame_valid: int32 [5], replicated, may hold values from 0 to 1, as said below
- group_offset: int32 [1], replicated, may hold values from 0 to 15360
- guide_index: int32 [1], replicated, may hold values from 0 to 4096
Outputs:
- query_grad: bfloat16 [2, 1024, 4096], P('cfg', 'fsdp', 'seq')
- key_grad: bfloat16 [2, 16384, 4096], P('cfg', ('seq', 'fsdp'))
- value_grad: bfloat16 [2, 16384, 4096], P('cfg', ('seq', 'fsdp'))
- weight_grad: float32 [4096, 5120], P('seq', 'fsdp')
The draws below stay inside these ranges and needn't reach their ends.
Inputs may be any that keep to these rules, and one draw needn't show every extreme that they name: `frame_valid`: at least one frame is valid and at least one frame is not.
All inputs are finite; a program needn't handle non-finite values.
Results may differ from the reference program's by a relative error of at most 0.03.
Values may be sent and summed in bfloat16 or wider, within the bound.
No kernel may reach another device: no remote copies, remote signals or barrier semaphores. Data moves between devices by JAX's collectives and lax.ppermute only.
A program may use at most 128 MiB of HBM per device.

```python
import math
import jax
import jax.numpy as jnp
from jax import lax

D = 5120
HEAD_DIM = 128
HEADS = 32
QC = 1024
FRAME_TOK = 3600
INNER = 4096
KEYS = 16384
FRAMES = 5


def scaled_noise(key, shape, low_scale, high_scale):
    noise_key, scale_key = jax.random.split(key)
    row_scale = jnp.exp(jax.random.uniform(scale_key, (shape[0], shape[1], 1), jnp.float32, math.log(low_scale), math.log(high_scale)))
    base = jax.random.truncated_normal(noise_key, -3.0, 3.0, shape, jnp.float32)
    return base * row_scale


def draw_queries(key, part):
    key = jax.random.fold_in(key, 5)
    return scaled_noise(key, (2, QC, HEADS * HEAD_DIM), 0.5, 2.0).astype(jnp.bfloat16)


def draw_key_vectors(key, part):
    key = jax.random.fold_in(key, 7)
    return scaled_noise(key, (2, KEYS, HEADS * HEAD_DIM), 0.5, 2.0).astype(jnp.bfloat16)


def draw_frame_valid(key, part):
    key = jax.random.fold_in(key, 9)
    coin_key, keep_key, drop_key = jax.random.split(key, 3)
    coin_flips = jax.random.randint(coin_key, (FRAMES,), 0, 10)
    keep_frame = jax.random.randint(keep_key, (), 0, FRAMES)
    drop_frame = (keep_frame + jax.random.randint(drop_key, (), 1, FRAMES)) % FRAMES
    frame_ids = jnp.arange(FRAMES)
    chosen = jnp.where(coin_flips < 7, 1, 0)
    chosen = jnp.where(frame_ids == keep_frame, 1, chosen)
    return jnp.where(frame_ids == drop_frame, 0, chosen).astype(jnp.int32)


def block_scale(own_key, dims, shards, smallest, top_value):
    factor_of, own = 1.0, jax.random.fold_in(own_key, 6)
    for dim, blocks in shards:
        heights = jnp.exp(jax.random.uniform(jax.random.fold_in(own, dim), (blocks,), jnp.float32, smallest / len(shards), top_value / len(shards)))
        factor_of = factor_of * jnp.repeat(heights, dims[dim] // blocks).reshape([-1 if axis == dim else 1 for axis in range(len(dims))])
    return factor_of


def bell_draw(own_key, extent, width, reach, cuts=(), kind=jnp.bfloat16):
    drawn = jax.random.normal(own_key, extent, jnp.float32) * width
    if len(cuts) > 0:
        drawn = block_scale(own_key, extent, cuts, -0.22, 0.18) * drawn
    return jnp.clip(drawn, min=-reach, max=reach).astype(kind)


def setup_inputs(seed: int = 0) -> dict:
    key_list = jax.random.split(jax.random.key(seed), 9)
    return {
        "queries": draw_queries(jax.random.fold_in(key_list[8], 71), 0),
        "key_vectors": draw_key_vectors(jax.random.fold_in(key_list[8], 71), 0),
        "value_vectors": bell_draw(key_list[2], (2, KEYS, INNER), 1.0, 6.0, ((0, 2), (1, 128))),
        "cotangent": bell_draw(key_list[3], (QC, D), 100.0, 600.0, ((1, 8),)),
        "out_weight": bell_draw(key_list[4], (INNER, D), INNER ** -0.5, 0.09375, ((0, 16), (1, 8))),
        "frame_valid": draw_frame_valid(jax.random.fold_in(key_list[8], 71), 0),
        "group_offset": jax.random.randint(key_list[6], (1,), 0, KEYS - QC + 1).astype(jnp.int32),
        "guide_index": jax.random.randint(key_list[7], (1,), 0, 4097).astype(jnp.int32),
    }


NEG_LARGE = -1e+30
LOSS_SCALE = 128.0

def rotate_back(gradient, positions, head_dim):
    row_count = gradient.shape[0]
    full_width = gradient.shape[1]
    half_dim = head_dim // 2
    shaped = gradient.reshape(row_count, full_width // head_dim, head_dim)
    frequency = 10000.0 ** (-jnp.arange(half_dim, dtype=jnp.float32) / half_dim)
    angles = positions.astype(jnp.float32)[:, None] * frequency[None, :]
    cosine = jnp.cos(angles)[:, None, :]
    sine_part = jnp.sin(angles)[:, None, :]
    first_half = shaped[:, :, :half_dim]
    second = shaped[:, :, half_dim:]
    turned = jnp.concatenate([first_half * cosine + second * sine_part, second * cosine - first_half * sine_part], axis=2)
    return turned.reshape(row_count, full_width)

def head_backward(query_head, key_head, value_head, upstream_head, key_valid, query_positions, key_positions):
    scale_factor = 1.0 / math.sqrt(HEAD_DIM)
    scores = jnp.dot(query_head, key_head.T, preferred_element_type=jnp.float32) * scale_factor
    masked = jnp.where(key_valid[None, :], scores, NEG_LARGE)
    row_max = lax.optimization_barrier(jnp.max(masked, axis=1, keepdims=True))
    exponent = jnp.where(key_valid[None, :], jnp.exp(masked - row_max), 0.0)
    row_sum = lax.optimization_barrier(jnp.sum(exponent, axis=1, keepdims=True))
    attn_out = (jnp.dot(exponent.astype(jnp.bfloat16), value_head, preferred_element_type=jnp.float32) / row_sum).astype(jnp.bfloat16)
    probability = exponent / row_sum
    row_delta = lax.optimization_barrier(jnp.sum(upstream_head.astype(jnp.float32) * attn_out.astype(jnp.float32), axis=1, keepdims=True))
    value_grad = jnp.dot(probability.astype(jnp.bfloat16).T, upstream_head, preferred_element_type=jnp.float32).astype(jnp.bfloat16)
    prob_grad = jnp.dot(upstream_head, value_head.T, preferred_element_type=jnp.float32)
    score_grad = (probability * (prob_grad - row_delta) * scale_factor).astype(jnp.bfloat16)
    query_sum = jnp.dot(score_grad, key_head, preferred_element_type=jnp.float32)
    query_grad = rotate_back(query_sum, query_positions, HEAD_DIM).astype(jnp.bfloat16)
    key_sum = jnp.dot(score_grad.T, query_head, preferred_element_type=jnp.float32)
    key_grad = rotate_back(key_sum, key_positions, HEAD_DIM).astype(jnp.bfloat16)
    return (attn_out, query_grad, key_grad, value_grad)

def by_heads(stacked):
    row_total = stacked.shape[1]
    return stacked.reshape(2, row_total, HEADS, HEAD_DIM).transpose(0, 2, 1, 3).reshape(2 * HEADS, row_total, HEAD_DIM)

def from_heads(stacked):
    row_total = stacked.shape[1]
    return stacked.reshape(2, HEADS, row_total, HEAD_DIM).transpose(0, 2, 1, 3).reshape(2, row_total, HEADS * HEAD_DIM)

def reference(queries, key_vectors, value_vectors, cotangent, out_weight, frame_valid, group_offset, guide_index):
    guide_scale = 1.5 + guide_index[0].astype(jnp.float32) / 1024.0
    guide_weight = jnp.stack([guide_scale, 1.0 - guide_scale])
    base_upstream = jnp.dot(cotangent, out_weight.T, preferred_element_type=jnp.float32)
    upstream = (guide_weight[:, None, None] * base_upstream[None]).astype(jnp.bfloat16)
    key_total = key_vectors.shape[1]
    key_index = jnp.arange(key_total, dtype=jnp.int32)
    key_valid = frame_valid[(key_index // FRAME_TOK).astype(jnp.int32)] == 1
    query_positions = group_offset[0] + jnp.arange(QC, dtype=jnp.int32)

    def one_head(operands):
        return head_backward(operands[0], operands[1], operands[2], operands[3], key_valid, query_positions, key_index)
    results = lax.map(one_head, (by_heads(queries), by_heads(key_vectors), by_heads(value_vectors), by_heads(upstream)))
    attn_out = from_heads(results[0])
    query_grad = from_heads(results[1])
    key_grad = from_heads(results[2])
    value_grad = from_heads(results[3])
    first_term = guide_weight[0] * jnp.dot(attn_out[0].T, cotangent, preferred_element_type=jnp.float32)
    second_term = guide_weight[1] * jnp.dot(attn_out[1].T, cotangent, preferred_element_type=jnp.float32)
    weight_grad = (first_term + second_term) / LOSS_SCALE
    return (query_grad, key_grad, value_grad, weight_grad)
```

```python
import math

import jax
import jax.numpy as jnp
from jax import lax
from jax.experimental import pallas as pl
from jax.experimental.pallas import tpu as pltpu
from jax.sharding import PartitionSpec as P

HEAD_DIM = 128
FRAME_TOK = 3600
NEG_LARGE = -1e30
NEG_FLOOR = -1e29
LOSS_SCALE = 128.0
SCALE = 1.0 / math.sqrt(HEAD_DIM)
EXP2_SCALE = SCALE * math.log2(math.e)
BF16 = jnp.bfloat16
F32 = jnp.float32
MIB = 1024 * 1024

NT = (((1,), (1,)), ((), ()))
TN = (((0,), (0,)), ((), ()))


def matmul(a, b, dims=(((1,), (0,)), ((), ()))):
    return lax.dot_general(a, b, dims, preferred_element_type=F32)


def params(mib):
    return pltpu.CompilerParams(vmem_limit_bytes=mib * MIB)


def pack_blocks(keys, values, parts):
    rows, width = keys.shape[1], keys.shape[2] // parts

    def kernel(k_ref, v_ref, out_ref, sems):
        copies = []
        for which, ref in enumerate((k_ref, v_ref)):
            for part in range(parts):
                copies.append(
                    pltpu.make_async_copy(
                        ref.at[0, :, pl.ds(part * width, width)],
                        out_ref.at[part, which],
                        sems.at[which, part],
                    )
                )
        for copy in copies:
            copy.start()
        for copy in copies:
            copy.wait()

    return pl.pallas_call(
        kernel,
        out_shape=jax.ShapeDtypeStruct((parts, 2, rows, width), keys.dtype),
        in_specs=[pl.BlockSpec(memory_space=pl.ANY)] * 2,
        out_specs=pl.BlockSpec(memory_space=pl.ANY),
        scratch_shapes=[pltpu.SemaphoreType.DMA((2, parts))],
        cost_estimate=pl.CostEstimate(flops=0, bytes_accessed=8 * MIB, transcendentals=0),
    )(keys, values)


def unpack_blocks(packed):
    parts, _, rows, width = packed.shape

    def kernel(in_ref, k_ref, v_ref, sems):
        copies = []
        for which, ref in enumerate((k_ref, v_ref)):
            for part in range(parts):
                copies.append(
                    pltpu.make_async_copy(
                        in_ref.at[part, which],
                        ref.at[0, :, pl.ds(part * width, width)],
                        sems.at[which, part],
                    )
                )
        for copy in copies:
            copy.start()
        for copy in copies:
            copy.wait()

    shape = jax.ShapeDtypeStruct((1, rows, parts * width), packed.dtype)
    return pl.pallas_call(
        kernel,
        out_shape=(shape, shape),
        in_specs=[pl.BlockSpec(memory_space=pl.ANY)],
        out_specs=(pl.BlockSpec(memory_space=pl.ANY),) * 2,
        scratch_shapes=[pltpu.SemaphoreType.DMA((2, parts))],
    )(packed)


def forward_kernel(kv_ref, qu_ref, bias_ref, exp_ref, out_ref, stat_ref):
    key_rows = kv_ref.shape[0] * kv_ref.shape[2]
    query_rows = qu_ref.shape[0] * qu_ref.shape[2]
    heads = kv_ref.shape[3] // HEAD_DIM
    bias = jnp.concatenate([bias_ref[...]] * (query_rows // 128), axis=1)
    rows = []
    for head in range(heads):
        lanes = slice(head * HEAD_DIM, (head + 1) * HEAD_DIM)
        keys = kv_ref[:, 0, :, lanes].reshape(key_rows, HEAD_DIM)
        values = kv_ref[:, 1, :, lanes].reshape(key_rows, HEAD_DIM)
        query = qu_ref[:, 0, :, lanes].reshape(query_rows, HEAD_DIM)
        upstream = qu_ref[:, 1, :, lanes].reshape(query_rows, HEAD_DIM)
        scores = matmul(keys, query, NT) * EXP2_SCALE + bias
        top = jnp.maximum(jnp.max(scores, axis=0, keepdims=True), NEG_FLOOR)
        exponent = jnp.exp2(scores - top)
        total = jnp.sum(exponent, axis=0, keepdims=True)
        exponent_bf = exponent.astype(BF16)
        exp_ref[head] = exponent_bf
        output = matmul(values, exponent_bf, TN)
        delta = jnp.sum(upstream.astype(F32).T * output, axis=0, keepdims=True)
        rows += [top, total, delta]
        for part in range(query_rows // 128):
            out_ref[part, lanes, :] = output[:, part * 128 : (part + 1) * 128].astype(BF16)
    rows.append(jnp.zeros((8 - len(rows), query_rows), F32))
    stat_ref[...] = jnp.concatenate(rows, axis=0)


def forward(kv, qu, bias):
    blocks, _, block_rows, width = kv.shape
    key_rows = blocks * block_rows
    slices, _, slice_rows, _ = qu.shape
    queries = slices * slice_rows
    heads = width // HEAD_DIM
    step = 256
    per = step // slice_rows
    return pl.pallas_call(
        forward_kernel,
        grid=(queries // step,),
        in_specs=[
            pl.BlockSpec((blocks, 2, block_rows, width), lambda i: (0, 0, 0, 0)),
            pl.BlockSpec((per, 2, slice_rows, width), lambda i: (i, 0, 0, 0)),
            pl.BlockSpec((key_rows, 128), lambda i: (0, 0)),
        ],
        out_specs=(
            pl.BlockSpec((heads, key_rows, step), lambda i: (0, 0, i)),
            pl.BlockSpec((per, width, slice_rows), lambda i: (i, 0, 0)),
            pl.BlockSpec((8, step), lambda i: (0, i)),
        ),
        out_shape=(
            jax.ShapeDtypeStruct((heads, key_rows, queries), BF16),
            jax.ShapeDtypeStruct((slices, width, slice_rows), BF16),
            jax.ShapeDtypeStruct((8, queries), F32),
        ),
        compiler_params=params(48),
        cost_estimate=pl.CostEstimate(
            flops=4 * heads * queries * key_rows * HEAD_DIM,
            bytes_accessed=12 * MIB,
            transcendentals=heads * queries * key_rows,
        ),
    )(kv, qu, bias)


def merged_stats(stats, head):
    tops = stats[:, 3 * head, :]
    totals = stats[:, 3 * head + 1, :]
    deltas = stats[:, 3 * head + 2, :]
    top = jnp.max(tops, axis=0, keepdims=True)
    factors = jnp.exp2(tops - top)
    inverse = 1.0 / jnp.sum(totals * factors, axis=0, keepdims=True)
    delta = jnp.sum(deltas * factors, axis=0, keepdims=True) * inverse
    return top, factors, inverse, delta


def backward_kernel(
    kv_ref, qu_ref, exp_ref, stats_ref, own_ref, cos_block, sin_block, cos_row, sin_row, grad_ref, query_ref, acc_ref
):
    step = pl.program_id(0)
    blocks, block_rows = kv_ref.shape[0], kv_ref.shape[2]
    key_rows = blocks * block_rows
    query_rows = qu_ref.shape[0] * qu_ref.shape[2]
    heads = kv_ref.shape[3] // HEAD_DIM
    stats = stats_ref[...]
    for head in range(heads):
        lanes = slice(head * HEAD_DIM, (head + 1) * HEAD_DIM)
        top, _, inverse, delta = merged_stats(stats, head)
        factor = jnp.exp2(own_ref[3 * head : 3 * head + 1, :] - top) * inverse
        keys = kv_ref[:, 0, :, lanes].reshape(key_rows, HEAD_DIM)
        values = kv_ref[:, 1, :, lanes].reshape(key_rows, HEAD_DIM)
        query = qu_ref[:, 0, :, lanes].reshape(query_rows, HEAD_DIM)
        upstream = qu_ref[:, 1, :, lanes].reshape(query_rows, HEAD_DIM)
        probability = exp_ref[head].astype(F32) * factor
        value_grad = matmul(probability.astype(BF16), upstream)
        prob_grad = matmul(values, upstream, NT)
        score_grad = (probability * (prob_grad - delta)).astype(BF16)
        key_grad = matmul(score_grad, query) * SCALE
        query_part = matmul(keys, score_grad, TN)
        for block in range(blocks):
            part = key_grad[block * block_rows : (block + 1) * block_rows, :]
            cos_a = cos_block[block]
            sin_a = sin_block[block]
            cosine = cos_a * cos_row[...] - sin_a * sin_row[...]
            sine = sin_a * cos_row[...] + cos_a * sin_row[...]
            signed = jnp.where(
                lax.broadcasted_iota(jnp.int32, sine.shape, 1) < HEAD_DIM // 2, sine, -sine
            )
            turned = part * cosine + pltpu.roll(part, HEAD_DIM // 2, 1) * signed
            grad_ref[block, 0, :, lanes] = turned.astype(BF16)
            grad_ref[block, 1, :, lanes] = value_grad[
                block * block_rows : (block + 1) * block_rows, :
            ].astype(BF16)

        @pl.when(step == 0)
        def _():
            acc_ref[lanes, :] = query_part

        @pl.when(step > 0)
        def _():
            acc_ref[lanes, :] += query_part

    @pl.when(step == pl.num_programs(0) - 1)
    def _():
        for part in range(query_ref.shape[0]):
            query_ref[part] = (acc_ref[:, part * 128 : (part + 1) * 128] * SCALE).astype(BF16)


def backward(kv, qu, exponent, stats, own, tables):
    blocks, _, block_rows, width = kv.shape
    slices, _, slice_rows, _ = qu.shape
    queries = slices * slice_rows
    heads = width // HEAD_DIM
    per = 4
    key_rows = blocks * block_rows
    whole = lambda shape: pl.BlockSpec(shape, lambda i: (0,) * len(shape))
    return pl.pallas_call(
        backward_kernel,
        grid=(blocks // per,),
        in_specs=[
            pl.BlockSpec((per, 2, block_rows, width), lambda i: (i, 0, 0, 0)),
            whole(qu.shape),
            pl.BlockSpec((heads, per * block_rows, queries), lambda i: (0, i, 0)),
            whole(stats.shape),
            whole(own.shape),
            pl.BlockSpec((per, 1, HEAD_DIM), lambda i: (i, 0, 0)),
            pl.BlockSpec((per, 1, HEAD_DIM), lambda i: (i, 0, 0)),
            whole((block_rows, HEAD_DIM)),
            whole((block_rows, HEAD_DIM)),
        ],
        out_specs=(
            pl.BlockSpec((per, 2, block_rows, width), lambda i: (i, 0, 0, 0)),
            whole((slices, width, slice_rows)),
        ),
        out_shape=(
            jax.ShapeDtypeStruct((blocks, 2, block_rows, width), BF16),
            jax.ShapeDtypeStruct((slices, width, slice_rows), BF16),
        ),
        scratch_shapes=[pltpu.VMEM((width, queries), F32)],
        compiler_params=params(48),
        cost_estimate=pl.CostEstimate(
            flops=8 * heads * queries * key_rows * HEAD_DIM,
            bytes_accessed=14 * MIB,
            transcendentals=0,
        ),
    )(kv, qu, exponent, stats, own, *tables)


def merge_output(parts, stats):
    def kernel(parts_ref, stats_ref, out_ref):
        for head in range(parts_ref.shape[1] // HEAD_DIM):
            lanes = slice(head * HEAD_DIM, (head + 1) * HEAD_DIM)
            _, factors, inverse, _ = merged_stats(stats_ref[...], head)
            weights = factors * inverse
            total = parts_ref[0, lanes, :].astype(F32) * weights[0:1, :]
            for block in range(1, parts_ref.shape[0]):
                total += parts_ref[block, lanes, :].astype(F32) * weights[block : block + 1, :]
            out_ref[lanes, :] = total.astype(BF16)

    return pl.pallas_call(
        kernel, out_shape=jax.ShapeDtypeStruct(parts.shape[1:], BF16), compiler_params=params(16)
    )(parts, stats)


def merge_query_grad(parts, cosine, sine):
    def kernel(parts_ref, cos_ref, sin_ref, out_ref):
        total = jnp.sum(parts_ref[...].astype(F32), axis=0)
        half = HEAD_DIM // 2
        turned = []
        for head in range(parts_ref.shape[1] // HEAD_DIM):
            first = total[head * HEAD_DIM : head * HEAD_DIM + half, :]
            second = total[head * HEAD_DIM + half : (head + 1) * HEAD_DIM, :]
            turned.append(first * cos_ref[...] + second * sin_ref[...])
            turned.append(second * cos_ref[...] - first * sin_ref[...])
        out_ref[...] = jnp.concatenate(turned, axis=0).T.astype(BF16)

    return pl.pallas_call(
        kernel,
        out_shape=jax.ShapeDtypeStruct((parts.shape[2], parts.shape[1]), BF16),
        compiler_params=params(16),
    )(parts, cosine, sine)


def projection_grad(parts, cotangent):
    def kernel(parts_ref, cot_ref, out_ref):
        joined = jnp.concatenate([parts_ref[part] for part in range(parts_ref.shape[0])], axis=1)
        out_ref[...] = matmul(joined, cot_ref[...]) * (1.0 / LOSS_SCALE)

    return pl.pallas_call(
        kernel,
        out_shape=jax.ShapeDtypeStruct((parts.shape[1], cotangent.shape[1]), F32),
        compiler_params=params(32),
    )(parts, cotangent)


def upstream_part(cotangent, out_weight):
    def kernel(cot_ref, weight_ref, out_ref):
        out_ref[...] = matmul(cot_ref[...], weight_ref[...], NT).astype(BF16)

    return pl.pallas_call(
        kernel,
        out_shape=jax.ShapeDtypeStruct((cotangent.shape[0], out_weight.shape[0]), BF16),
        compiler_params=params(32),
    )(cotangent, out_weight)


def per_device(
    queries, key_vectors, value_vectors, cotangent, out_weight, frame_valid, group_offset, guide_index
):
    seq_count, fsdp_count = lax.axis_size("seq"), lax.axis_size("fsdp")
    z_count = fsdp_count
    x_count = seq_count // z_count
    seq_index, fsdp_index = lax.axis_index("seq"), lax.axis_index("fsdp")
    z_index = seq_index % z_count
    cfg_index = lax.axis_index("cfg")
    block_rows = key_vectors.shape[1]
    group_rows, width = queries.shape[1], queries.shape[2]
    slice_rows = group_rows // z_count

    def place(x, z, f):
        return (x * z_count + z) * fsdp_count + f

    spots = [
        (x, z, f) for x in range(x_count) for z in range(z_count) for f in range(fsdp_count)
    ]
    plane_groups = [
        [place(x, z, f) for x in range(x_count) for f in range(fsdp_count)] for z in range(z_count)
    ]
    column_groups = [[x * z_count + z for z in range(z_count)] for x in range(x_count)]
    turn = [(place(x, z, f), place(x, f, z)) for x, z, f in spots]
    cfg_stride = seq_count * fsdp_count
    turn_across = [
        (c * cfg_stride + s, (1 - c) * cfg_stride + d) for c in range(2) for s, d in turn
    ]

    def over_plane(x):
        return lax.all_to_all(x, ("seq", "fsdp"), 0, 0, axis_index_groups=plane_groups, tiled=True)

    def over_column(x):
        return lax.all_to_all(x, "seq", 0, 0, axis_index_groups=column_groups, tiled=True)

    def over_fsdp(x):
        return lax.all_to_all(x, "fsdp", 0, 0, tiled=True)

    def copies(x, count):
        return jnp.broadcast_to(x[None], (count,) + x.shape)

    guide = 1.5 + guide_index[0].astype(F32) / 1024.0
    own_weight = jnp.where(cfg_index == 0, guide, 1.0 - guide)

    kv = over_plane(pack_blocks(key_vectors, value_vectors, x_count * fsdp_count))

    partial = upstream_part(cotangent, out_weight).reshape(fsdp_count, slice_rows, width)
    summed = jnp.sum(over_fsdp(partial).astype(F32), axis=0)
    upstream_rows = (own_weight * summed).astype(BF16)
    query_rows = lax.dynamic_slice(
        queries[0], (fsdp_index * slice_rows, 0), (slice_rows, width)
    )
    both = lax.ppermute(jnp.stack([query_rows, upstream_rows]), ("seq", "fsdp"), turn)
    qu = over_column(copies(both, z_count))

    block_ids = jnp.arange(x_count * fsdp_count, dtype=jnp.int32)
    block_start = place(block_ids // fsdp_count, z_index, block_ids % fsdp_count) * block_rows
    row_ids = jnp.arange(block_rows, dtype=jnp.int32)
    positions = (block_start[:, None] + row_ids[None, :]).reshape(-1)
    frame_match = (positions // FRAME_TOK)[:, None] == jnp.arange(
        frame_valid.shape[0], dtype=jnp.int32
    )[None, :]
    valid = jnp.sum(jnp.where(frame_match, frame_valid[None, :], 0), axis=1) == 1
    bias = jnp.broadcast_to(
        jnp.where(valid, 0.0, NEG_LARGE).astype(F32)[:, None], (positions.shape[0], 128)
    )
    frequency = 10000.0 ** (-jnp.arange(HEAD_DIM // 2, dtype=F32) / (HEAD_DIM // 2))
    twice = jnp.concatenate([frequency, frequency])
    block_angle = (block_start.astype(F32)[:, None] * twice[None, :])[:, None, :]
    row_angle = row_ids.astype(F32)[:, None] * twice[None, :]
    tables = (jnp.cos(block_angle), jnp.sin(block_angle), jnp.cos(row_angle), jnp.sin(row_angle))

    exponent, out_parts, own_stats = forward(kv, qu, bias)
    stats = over_column(copies(own_stats, z_count))
    grads, query_parts = backward(kv, qu, exponent, stats, own_stats, tables)
    key_grad, value_grad = unpack_blocks(over_plane(grads))

    out_slices = over_column(out_parts)
    slice_stats = lax.dynamic_slice_in_dim(stats, z_index * slice_rows, slice_rows, axis=2)
    attn_rows = merge_output(out_slices, slice_stats)
    own_rows = lax.ppermute(attn_rows, ("seq", "fsdp"), turn)
    other_rows = lax.ppermute(attn_rows, ("cfg", "seq", "fsdp"), turn_across)
    mixed = own_weight * own_rows.astype(F32) + (1.0 - own_weight) * other_rows.astype(F32)
    weight_grad = projection_grad(over_fsdp(copies(mixed.astype(BF16), fsdp_count)), cotangent)

    query_positions = (
        group_offset[0] + z_index * slice_rows + jnp.arange(slice_rows, dtype=jnp.int32)
    )
    query_angle = query_positions.astype(F32)[None, :] * frequency[:, None]
    query_slice = merge_query_grad(
        over_column(query_parts), jnp.cos(query_angle), jnp.sin(query_angle)
    )
    query_grad = lax.ppermute(query_slice, ("seq", "fsdp"), turn)[None]
    return (query_grad, key_grad, value_grad, weight_grad)


def solution(mesh):
    placed = (
        P("cfg", None, "seq"),
        P("cfg", ("seq", "fsdp"), None),
        P("cfg", ("seq", "fsdp"), None),
        P(None, "fsdp"),
        P("seq", "fsdp"),
        P(),
        P(),
        P(),
    )
    return jax.shard_map(
        per_device,
        mesh=mesh,
        in_specs=placed,
        out_specs=(
            P("cfg", "fsdp", "seq"),
            P("cfg", ("seq", "fsdp"), None),
            P("cfg", ("seq", "fsdp"), None),
            P("seq", "fsdp"),
        ),
        check_vma=False,
    )
```

```python
import math

import jax
import jax.numpy as jnp
from jax import lax
from jax.experimental import pallas as pl
from jax.experimental.pallas import tpu as pltpu
from jax.sharding import PartitionSpec as P

HEAD_DIM = 128
FRAME_TOK = 3600
NEG_LARGE = -1e30
NEG_FLOOR = -1e29
LOSS_SCALE = 128.0
SCALE = 1.0 / math.sqrt(HEAD_DIM)
EXP2_SCALE = SCALE * math.log2(math.e)
BF16 = jnp.bfloat16
F32 = jnp.float32
MIB = 1024 * 1024

PATH = (0, 4, 2, 6, 1, 5, 3, 7)
NT = (((1,), (1,)), ((), ()))
TN = (((0,), (0,)), ((), ()))


def matmul(a, b, dims=(((1,), (0,)), ((), ()))):
    return lax.dot_general(a, b, dims, preferred_element_type=F32)


def params(mib):
    return pltpu.CompilerParams(vmem_limit_bytes=mib * MIB)


def pack_blocks(keys, values, parts):
    rows, width = keys.shape[1], keys.shape[2] // parts
    per = 4

    def kernel(k_ref, v_ref, out_ref):
        for which, ref in enumerate((k_ref, v_ref)):
            for part in range(per):
                out_ref[part, which] = ref[0, :, part * width : (part + 1) * width]

    return pl.pallas_call(
        kernel,
        grid=(parts // per,),
        out_shape=jax.ShapeDtypeStruct((parts, 2, rows, width), keys.dtype),
        in_specs=[pl.BlockSpec((1, rows, per * width), lambda i: (0, 0, i))] * 2,
        out_specs=pl.BlockSpec((per, 2, rows, width), lambda i: (i, 0, 0, 0)),
        compiler_params=params(16),
    )(keys, values)


def unpack_blocks(packed):
    parts, _, rows, width = packed.shape
    per = 4

    def kernel(in_ref, k_ref, v_ref):
        for which, ref in enumerate((k_ref, v_ref)):
            for part in range(per):
                ref[0, :, part * width : (part + 1) * width] = in_ref[part, which]

    shape = jax.ShapeDtypeStruct((1, rows, parts * width), packed.dtype)
    return pl.pallas_call(
        kernel,
        grid=(parts // per,),
        out_shape=(shape, shape),
        in_specs=[pl.BlockSpec((per, 2, rows, width), lambda i: (i, 0, 0, 0))],
        out_specs=(pl.BlockSpec((1, rows, per * width), lambda i: (0, 0, i)),) * 2,
        compiler_params=params(16),
    )(packed)


def forward_kernel(kv_ref, qu_ref, bias_ref, exp_ref, out_ref, stat_ref, top_ref):
    key_rows = kv_ref.shape[0] * kv_ref.shape[2]
    query_rows = qu_ref.shape[0] * qu_ref.shape[2]
    heads = kv_ref.shape[3] // HEAD_DIM
    bias = jnp.concatenate([bias_ref[...]] * (query_rows // 128), axis=1)
    rows, tops = [], []
    for head in range(heads):
        lanes = slice(head * HEAD_DIM, (head + 1) * HEAD_DIM)
        keys = kv_ref[:, 0, :, lanes].reshape(key_rows, HEAD_DIM)
        values = kv_ref[:, 1, :, lanes].reshape(key_rows, HEAD_DIM)
        query = qu_ref[:, 0, :, lanes].reshape(query_rows, HEAD_DIM)
        upstream = qu_ref[:, 1, :, lanes].reshape(query_rows, HEAD_DIM)
        scores = matmul(keys, query, NT) * EXP2_SCALE + bias
        top = jnp.maximum(jnp.max(scores, axis=0, keepdims=True), NEG_FLOOR)
        exponent = jnp.exp2(scores - top)
        total = jnp.sum(exponent, axis=0, keepdims=True)
        exponent_bf = exponent.astype(BF16)
        exp_ref[head] = exponent_bf
        safe = jnp.maximum(total, 1e-30)
        output = matmul(values, exponent_bf, TN) * (1.0 / safe)
        delta = jnp.sum(upstream.astype(F32).T * output, axis=0, keepdims=True)
        rows += [jnp.where(total > 0.0, top + jnp.log2(safe), NEG_FLOOR), delta]
        tops.append(top)
        for part in range(query_rows // 128):
            out_ref[part, lanes, :] = output[:, part * 128 : (part + 1) * 128].astype(BF16)
    stat_ref[...] = jnp.concatenate(rows, axis=0)
    top_ref[...] = jnp.concatenate(tops, axis=0)


def forward(kv, qu, bias):
    blocks, _, block_rows, width = kv.shape
    key_rows = blocks * block_rows
    slices, _, slice_rows, _ = qu.shape
    queries = slices * slice_rows
    heads = width // HEAD_DIM
    step = 256
    per = step // slice_rows
    return pl.pallas_call(
        forward_kernel,
        grid=(queries // step,),
        in_specs=[
            pl.BlockSpec((blocks, 2, block_rows, width), lambda i: (0, 0, 0, 0)),
            pl.BlockSpec((per, 2, slice_rows, width), lambda i: (i, 0, 0, 0)),
            pl.BlockSpec((key_rows, 128), lambda i: (0, 0)),
        ],
        out_specs=(
            pl.BlockSpec((heads, key_rows, step), lambda i: (0, 0, i)),
            pl.BlockSpec((per, width, slice_rows), lambda i: (i, 0, 0)),
            pl.BlockSpec((2 * heads, step), lambda i: (0, i)),
            pl.BlockSpec((heads, step), lambda i: (0, i)),
        ),
        out_shape=(
            jax.ShapeDtypeStruct((heads, key_rows, queries), BF16),
            jax.ShapeDtypeStruct((slices, width, slice_rows), BF16),
            jax.ShapeDtypeStruct((2 * heads, queries), F32),
            jax.ShapeDtypeStruct((heads, queries), F32),
        ),
        compiler_params=params(48),
        cost_estimate=pl.CostEstimate(
            flops=4 * heads * queries * key_rows * HEAD_DIM,
            bytes_accessed=12 * MIB,
            transcendentals=heads * queries * key_rows,
        ),
    )(kv, qu, bias)


def merged_stats(stats, head):
    logs = stats[:, 2 * head, :]
    deltas = stats[:, 2 * head + 1, :]
    top = jnp.max(logs, axis=0, keepdims=True)
    shares = jnp.exp2(logs - top)
    total = jnp.sum(shares, axis=0, keepdims=True)
    shares = shares / total
    return top + jnp.log2(total), shares, jnp.sum(deltas * shares, axis=0, keepdims=True)


def backward_kernel(
    spot_ref,
    kv_ref,
    qu_ref,
    exp_ref,
    stats_ref,
    own_ref,
    cos_block,
    sin_block,
    cos_row,
    sin_row,
    grad_ref,
    keep_ref,
    send_ref,
    acc_ref,
):
    step = pl.program_id(0)
    blocks, block_rows = kv_ref.shape[0], kv_ref.shape[2]
    key_rows = blocks * block_rows
    query_rows = qu_ref.shape[0] * qu_ref.shape[2]
    heads = kv_ref.shape[3] // HEAD_DIM
    stats = stats_ref[...]
    for head in range(heads):
        lanes = slice(head * HEAD_DIM, (head + 1) * HEAD_DIM)
        log_total, _, delta = merged_stats(stats, head)
        factor = jnp.exp2(own_ref[head : head + 1, :] - log_total)
        keys = kv_ref[:, 0, :, lanes].reshape(key_rows, HEAD_DIM)
        values = kv_ref[:, 1, :, lanes].reshape(key_rows, HEAD_DIM)
        query = qu_ref[:, 0, :, lanes].reshape(query_rows, HEAD_DIM)
        upstream = qu_ref[:, 1, :, lanes].reshape(query_rows, HEAD_DIM)
        probability = exp_ref[head].astype(F32) * factor
        value_grad = matmul(probability.astype(BF16), upstream)
        prob_grad = matmul(values, upstream, NT)
        score_grad = (probability * (prob_grad - delta)).astype(BF16)
        key_grad = matmul(score_grad, query) * SCALE
        query_part = matmul(keys, score_grad, TN)
        for block in range(blocks):
            part = key_grad[block * block_rows : (block + 1) * block_rows, :]
            cos_a = cos_block[block]
            sin_a = sin_block[block]
            cosine = cos_a * cos_row[...] - sin_a * sin_row[...]
            sine = sin_a * cos_row[...] + cos_a * sin_row[...]
            signed = jnp.where(
                lax.broadcasted_iota(jnp.int32, sine.shape, 1) < HEAD_DIM // 2, sine, -sine
            )
            turned = part * cosine + pltpu.roll(part, HEAD_DIM // 2, 1) * signed
            grad_ref[block, 0, :, lanes] = turned.astype(BF16)
            grad_ref[block, 1, :, lanes] = value_grad[
                block * block_rows : (block + 1) * block_rows, :
            ].astype(BF16)

        @pl.when(step == 0)
        def _():
            acc_ref[lanes, :] = query_part

        @pl.when(step > 0)
        def _():
            acc_ref[lanes, :] += query_part

    @pl.when(step == pl.num_programs(0) - 1)
    def _():
        half = keep_ref.shape[0]
        for slot in range(2 * half):
            first = pl.multiple_of(lax.bitwise_xor(spot_ref[0], PATH[slot]) * 128, 128)
            part = (acc_ref[:, pl.ds(first, 128)] * SCALE).astype(BF16)
            if slot < half:
                keep_ref[slot] = part
            else:
                send_ref[slot - half] = part


def backward(spot, kv, qu, exponent, stats, own, tables):
    blocks, _, block_rows, width = kv.shape
    slices, _, slice_rows, _ = qu.shape
    queries = slices * slice_rows
    heads = width // HEAD_DIM
    per = 4
    key_rows = blocks * block_rows
    whole = lambda shape: pl.BlockSpec(shape, lambda i, s: (0,) * len(shape))
    half = jax.ShapeDtypeStruct((slices // 2, width, slice_rows), BF16)
    return pl.pallas_call(
        backward_kernel,
        grid_spec=pltpu.PrefetchScalarGridSpec(
            num_scalar_prefetch=1,
            grid=(blocks // per,),
            in_specs=[
                pl.BlockSpec((per, 2, block_rows, width), lambda i, s: (i, 0, 0, 0)),
                whole(qu.shape),
                pl.BlockSpec((heads, per * block_rows, queries), lambda i, s: (0, i, 0)),
                whole(stats.shape),
                whole(own.shape),
                pl.BlockSpec((per, 1, HEAD_DIM), lambda i, s: (i, 0, 0)),
                pl.BlockSpec((per, 1, HEAD_DIM), lambda i, s: (i, 0, 0)),
                whole((block_rows, HEAD_DIM)),
                whole((block_rows, HEAD_DIM)),
            ],
            out_specs=(
                pl.BlockSpec((per, 2, block_rows, width), lambda i, s: (i, 0, 0, 0)),
                whole(half.shape),
                whole(half.shape),
            ),
            scratch_shapes=[pltpu.VMEM((width, queries), F32)],
        ),
        out_shape=(jax.ShapeDtypeStruct((blocks, 2, block_rows, width), BF16), half, half),
        compiler_params=params(48),
        cost_estimate=pl.CostEstimate(
            flops=8 * heads * queries * key_rows * HEAD_DIM,
            bytes_accessed=14 * MIB,
            transcendentals=0,
        ),
    )(spot, kv, qu, exponent, stats, own, *tables)


def merge_output(parts, stats):
    def kernel(parts_ref, stats_ref, out_ref):
        for head in range(parts_ref.shape[1] // HEAD_DIM):
            lanes = slice(head * HEAD_DIM, (head + 1) * HEAD_DIM)
            _, shares, _ = merged_stats(stats_ref[...], head)
            total = jnp.zeros((HEAD_DIM, parts_ref.shape[2]), F32)
            for block in range(parts_ref.shape[0]):
                total += parts_ref[block, lanes, :].astype(F32) * shares[block : block + 1, :]
            out_ref[lanes, :] = total.astype(BF16)

    return pl.pallas_call(
        kernel, out_shape=jax.ShapeDtypeStruct(parts.shape[1:], BF16), compiler_params=params(8)
    )(parts, stats)


def merge_query_grad(kept, arrived, cosine, sine):
    def kernel(kept_ref, arrived_ref, cos_ref, sin_ref, out_ref):
        total = kept_ref[0].astype(F32) + arrived_ref[0].astype(F32)
        half = HEAD_DIM // 2
        turned = []
        for head in range(total.shape[0] // HEAD_DIM):
            first = total[head * HEAD_DIM : head * HEAD_DIM + half, :]
            second = total[head * HEAD_DIM + half : (head + 1) * HEAD_DIM, :]
            turned.append(first * cos_ref[...] + second * sin_ref[...])
            turned.append(second * cos_ref[...] - first * sin_ref[...])
        out_ref[...] = jnp.concatenate(turned, axis=0).T.astype(BF16)

    return pl.pallas_call(
        kernel,
        out_shape=jax.ShapeDtypeStruct((kept.shape[2], kept.shape[1]), BF16),
        compiler_params=params(8),
    )(kept, arrived, cosine, sine)


def projection_grad(spot, near, far, cotangent):
    count = 2 * near.shape[0]

    def kernel(spot_ref, near_ref, far_ref, cot_ref, out_ref, joined_ref):
        for slot in range(count):
            first = pl.multiple_of(lax.bitwise_xor(spot_ref[0], PATH[slot]) * 128, 128)
            ref = near_ref if slot < count // 2 else far_ref
            joined_ref[:, pl.ds(first, 128)] = ref[slot % (count // 2)]
        out_ref[...] = matmul(joined_ref[...], cot_ref[...]) * (1.0 / LOSS_SCALE)

    vmem = pl.BlockSpec(memory_space=pltpu.VMEM)
    return pl.pallas_call(
        kernel,
        out_shape=jax.ShapeDtypeStruct((near.shape[1], cotangent.shape[1]), F32),
        in_specs=[pl.BlockSpec(memory_space=pltpu.SMEM), vmem, vmem, vmem],
        out_specs=vmem,
        scratch_shapes=[pltpu.VMEM((near.shape[1], count * 128), BF16)],
        compiler_params=params(16),
    )(spot, near, far, cotangent)


def assemble(spot, query_near, query_far, upstream_near, upstream_far):
    count = 2 * query_near.shape[0]

    def kernel(spot_ref, q_near, q_far, u_near, u_far, out_ref):
        for slot in range(count):
            place = lax.bitwise_xor(spot_ref[0], PATH[slot])
            out_ref[place, 0] = (q_near if slot < count // 2 else q_far)[slot % (count // 2)]
            out_ref[place, 1] = (u_near if slot < count // 2 else u_far)[slot % (count // 2)]

    vmem = pl.BlockSpec(memory_space=pltpu.VMEM)
    return pl.pallas_call(
        kernel,
        out_shape=jax.ShapeDtypeStruct((count, 2) + query_near.shape[1:], BF16),
        in_specs=[pl.BlockSpec(memory_space=pltpu.SMEM)] + [vmem] * 4,
        out_specs=vmem,
        compiler_params=params(16),
    )(spot, query_near, query_far, upstream_near, upstream_far)


def upstream_part(cotangent, out_weight):
    def kernel(cot_ref, weight_ref, out_ref):
        out_ref[...] = matmul(cot_ref[...], weight_ref[...], NT).astype(BF16)

    return pl.pallas_call(
        kernel,
        out_shape=jax.ShapeDtypeStruct((cotangent.shape[0], out_weight.shape[0]), BF16),
        compiler_params=params(32),
    )(cotangent, out_weight)


def per_device(
    queries, key_vectors, value_vectors, cotangent, out_weight, frame_valid, group_offset, guide_index
):
    seq_count, fsdp_count = lax.axis_size("seq"), lax.axis_size("fsdp")
    z_count = fsdp_count
    x_count = seq_count // z_count
    seq_index, fsdp_index = lax.axis_index("seq"), lax.axis_index("fsdp")
    z_index = seq_index % z_count
    cfg_index = lax.axis_index("cfg")
    block_rows = key_vectors.shape[1]
    group_rows, width = queries.shape[1], queries.shape[2]
    slice_rows = group_rows // z_count

    def place(x, z, f):
        return (x * z_count + z) * fsdp_count + f

    spots = [
        (x, z, f) for x in range(x_count) for z in range(z_count) for f in range(fsdp_count)
    ]
    plane_groups = [
        [place(x, z, f) for x in range(x_count) for f in range(fsdp_count)] for z in range(z_count)
    ]
    column_groups = [[x * z_count + z for z in range(z_count)] for x in range(x_count)]
    turn = [(place(x, z, f), place(x, (f + z) % z_count, z)) for x, z, f in spots]
    back = [(d, s) for s, d in turn]
    cfg_stride = seq_count * fsdp_count
    back_across = [
        (c * cfg_stride + s, (1 - c) * cfg_stride + d) for c in range(2) for s, d in back
    ]

    def over_plane(x):
        return lax.all_to_all(x, ("seq", "fsdp"), 0, 0, axis_index_groups=plane_groups, tiled=True)

    def over_column(x):
        return lax.all_to_all(x, "seq", 0, 0, axis_index_groups=column_groups, tiled=True)

    def over_fsdp(x):
        return lax.all_to_all(x, "fsdp", 0, 0, tiled=True)

    def z_partner(x, bit):
        return lax.ppermute(x, "seq", [(s, s ^ bit) for s in range(seq_count)])

    def fsdp_partner(x, bit):
        return lax.ppermute(x, "fsdp", [(s, s ^ bit) for s in range(fsdp_count)])

    def doubled(x, partner):
        near = x[None]
        for bit in (4, 2):
            near = jnp.concatenate([near, partner(near, bit)])
        return near, partner(near, 1)

    def tied(first, second):
        return lax.optimization_barrier((first, second))

    z_spot = z_index.astype(jnp.int32)[None]
    fsdp_spot = fsdp_index.astype(jnp.int32)[None]
    guide = 1.5 + guide_index[0].astype(F32) / 1024.0
    own_weight = jnp.where(cfg_index == 0, guide, 1.0 - guide)

    query_rows = lax.dynamic_slice(
        queries[0], (fsdp_index * slice_rows, 0), (slice_rows, width)
    )
    query_near, query_far = doubled(
        lax.ppermute(query_rows, ("seq", "fsdp"), turn), z_partner
    )
    partial = upstream_part(cotangent, out_weight).reshape(fsdp_count, slice_rows, width)
    partial = over_fsdp(partial)
    packed = pack_blocks(key_vectors, value_vectors, x_count * fsdp_count)
    partial, packed = tied(partial, packed)
    kv = over_plane(packed)

    summed = jnp.sum(partial.astype(F32), axis=0)
    upstream_rows = (own_weight * summed).astype(BF16)
    upstream_near, upstream_far = doubled(
        lax.ppermute(upstream_rows, ("seq", "fsdp"), turn), z_partner
    )
    qu = assemble(z_spot, query_near, query_far, upstream_near, upstream_far)

    block_ids = jnp.arange(x_count * fsdp_count, dtype=jnp.int32)
    block_start = place(block_ids // fsdp_count, z_index, block_ids % fsdp_count) * block_rows
    row_ids = jnp.arange(block_rows, dtype=jnp.int32)
    positions = (block_start[:, None] + row_ids[None, :]).reshape(-1)
    frame_match = (positions // FRAME_TOK)[:, None] == jnp.arange(
        frame_valid.shape[0], dtype=jnp.int32
    )[None, :]
    valid = jnp.sum(jnp.where(frame_match, frame_valid[None, :], 0), axis=1) == 1
    bias = jnp.broadcast_to(
        jnp.where(valid, 0.0, NEG_LARGE).astype(F32)[:, None], (positions.shape[0], 128)
    )
    frequency = 10000.0 ** (-jnp.arange(HEAD_DIM // 2, dtype=F32) / (HEAD_DIM // 2))
    twice = jnp.concatenate([frequency, frequency])
    block_angle = (block_start.astype(F32)[:, None] * twice[None, :])[:, None, :]
    row_angle = row_ids.astype(F32)[:, None] * twice[None, :]
    tables = (jnp.cos(block_angle), jnp.sin(block_angle), jnp.cos(row_angle), jnp.sin(row_angle))
    slice_id = (z_index - fsdp_index) % z_count
    query_positions = (
        group_offset[0] + slice_id * slice_rows + jnp.arange(slice_rows, dtype=jnp.int32)
    )
    query_angle = query_positions.astype(F32)[None, :] * frequency[:, None]

    exponent, out_parts, own_stats, own_top = forward(kv, qu, bias)
    stats = over_column(jnp.broadcast_to(own_stats[None], (z_count,) + own_stats.shape))
    stats, out_parts = tied(stats, out_parts)
    out_slices = over_column(out_parts)
    grads, query_keep, query_send = backward(z_spot, kv, qu, exponent, stats, own_top, tables)
    grads, out_slices, query_send = lax.optimization_barrier((grads, out_slices, query_send))
    key_grad, value_grad = unpack_blocks(over_plane(grads))

    for bit in (1, 2):
        arrived = z_partner(query_send, bit)
        total = (query_keep.astype(F32) + arrived.astype(F32)).astype(BF16)
        half = total.shape[0] // 2
        query_keep, query_send = total[:half], total[half:]
    arrived = z_partner(query_send, 4)
    query_slice = merge_query_grad(query_keep, arrived, jnp.cos(query_angle), jnp.sin(query_angle))
    query_grad = lax.ppermute(query_slice, ("seq", "fsdp"), back)[None]

    slice_stats = lax.dynamic_slice_in_dim(stats, z_index * slice_rows, slice_rows, axis=2)
    attn_rows = merge_output(out_slices, slice_stats)
    own_rows = lax.ppermute(attn_rows, ("seq", "fsdp"), back)
    other_rows = lax.ppermute(attn_rows, ("cfg", "seq", "fsdp"), back_across)
    mixed = own_weight * own_rows.astype(F32) + (1.0 - own_weight) * other_rows.astype(F32)
    mixed_near, mixed_far = doubled(mixed.astype(BF16), fsdp_partner)
    weight_grad = projection_grad(fsdp_spot, mixed_near, mixed_far, cotangent)
    return (query_grad, key_grad, value_grad, weight_grad)


def solution(mesh):
    placed = (
        P("cfg", None, "seq"),
        P("cfg", ("seq", "fsdp"), None),
        P("cfg", ("seq", "fsdp"), None),
        P(None, "fsdp"),
        P("seq", "fsdp"),
        P(),
        P(),
        P(),
    )
    return jax.shard_map(
        per_device,
        mesh=mesh,
        in_specs=placed,
        out_specs=(
            P("cfg", "fsdp", "seq"),
            P("cfg", ("seq", "fsdp"), None),
            P("cfg", ("seq", "fsdp"), None),
            P("seq", "fsdp"),
        ),
        check_vma=False,
    )
```

```python
import math

import jax
import jax.numpy as jnp
from jax import lax
from jax.experimental import pallas as pl
from jax.experimental.pallas import tpu as pltpu
from jax.sharding import PartitionSpec as P

HEAD_DIM = 128
FRAME_TOK = 3600
NEG_LARGE = -1e30
NEG_FLOOR = -1e29
LOSS_SCALE = 128.0
SCALE = 1.0 / math.sqrt(HEAD_DIM)
EXP2_SCALE = SCALE * math.log2(math.e)
BF16 = jnp.bfloat16
F32 = jnp.float32
MIB = 1024 * 1024

PATH = (0, 4, 2, 6, 1, 5, 3, 7)
NT = (((1,), (1,)), ((), ()))
TN = (((0,), (0,)), ((), ()))


def matmul(a, b, dims=(((1,), (0,)), ((), ()))):
    return lax.dot_general(a, b, dims, preferred_element_type=F32)


def params(mib):
    return pltpu.CompilerParams(vmem_limit_bytes=mib * MIB)


def pack_blocks(keys, values, parts):
    rows, width = keys.shape[1], keys.shape[2] // parts
    per = 4

    def kernel(k_ref, v_ref, out_ref):
        for which, ref in enumerate((k_ref, v_ref)):
            for part in range(per):
                out_ref[part, which] = ref[0, :, part * width : (part + 1) * width]

    return pl.pallas_call(
        kernel,
        grid=(parts // per,),
        out_shape=jax.ShapeDtypeStruct((parts, 2, rows, width), keys.dtype),
        in_specs=[pl.BlockSpec((1, rows, per * width), lambda i: (0, 0, i))] * 2,
        out_specs=pl.BlockSpec((per, 2, rows, width), lambda i: (i, 0, 0, 0)),
        compiler_params=params(16),
    )(keys, values)


def unpack_blocks(packed):
    parts, _, rows, width = packed.shape
    per = 4

    def kernel(in_ref, k_ref, v_ref):
        for which, ref in enumerate((k_ref, v_ref)):
            for part in range(per):
                ref[0, :, part * width : (part + 1) * width] = in_ref[part, which]

    shape = jax.ShapeDtypeStruct((1, rows, parts * width), packed.dtype)
    return pl.pallas_call(
        kernel,
        grid=(parts // per,),
        out_shape=(shape, shape),
        in_specs=[pl.BlockSpec((per, 2, rows, width), lambda i: (i, 0, 0, 0))],
        out_specs=(pl.BlockSpec((1, rows, per * width), lambda i: (0, 0, i)),) * 2,
        compiler_params=params(16),
    )(packed)


def forward_kernel(spot_ref, kv_ref, query_ref, bias_ref, exp_ref, out_ref, log_ref, top_ref):
    key_rows = kv_ref.shape[0] * kv_ref.shape[2]
    per, slice_rows = query_ref.shape[0], query_ref.shape[1]
    query_rows = per * slice_rows
    slices = out_ref.shape[0]
    heads = kv_ref.shape[3] // HEAD_DIM
    bias = jnp.concatenate([bias_ref[...]] * (query_rows // 128), axis=1)
    logs, tops = [], []
    for head in range(heads):
        lanes = slice(head * HEAD_DIM, (head + 1) * HEAD_DIM)
        keys = kv_ref[:, 0, :, lanes].reshape(key_rows, HEAD_DIM)
        values = kv_ref[:, 1, :, lanes].reshape(key_rows, HEAD_DIM)
        query = query_ref[:, :, lanes].reshape(query_rows, HEAD_DIM)
        scores = matmul(keys, query, NT) * EXP2_SCALE + bias
        top = jnp.maximum(jnp.max(scores, axis=0, keepdims=True), NEG_FLOOR)
        exponent = jnp.exp2(scores - top)
        total = jnp.sum(exponent, axis=0, keepdims=True)
        exponent_bf = exponent.astype(BF16)
        exp_ref[head] = exponent_bf
        safe = jnp.maximum(total, 1e-30)
        output = (matmul(values, exponent_bf, TN) * (1.0 / safe)).astype(BF16)
        logs.append(jnp.where(total > 0.0, top + jnp.log2(safe), NEG_FLOOR))
        tops.append(top)
        for part in range(per):
            place = lax.rem(pl.program_id(0) * per + part + spot_ref[1], slices)
            out_ref[place, lanes, :] = output[:, part * slice_rows : (part + 1) * slice_rows]
    log_ref[...] = jnp.concatenate(logs, axis=0)
    top_ref[...] = jnp.concatenate(tops, axis=0)


def forward(spot, kv, query, bias):
    blocks, _, block_rows, width = kv.shape
    key_rows = blocks * block_rows
    slices, slice_rows, _ = query.shape
    queries = slices * slice_rows
    heads = width // HEAD_DIM
    step = 256
    per = step // slice_rows
    return pl.pallas_call(
        forward_kernel,
        grid_spec=pltpu.PrefetchScalarGridSpec(
            num_scalar_prefetch=1,
            grid=(queries // step,),
            in_specs=[
                pl.BlockSpec((blocks, 2, block_rows, width), lambda i, s: (0, 0, 0, 0)),
                pl.BlockSpec((per, slice_rows, width), lambda i, s: (i, 0, 0)),
                pl.BlockSpec((key_rows, 128), lambda i, s: (0, 0)),
            ],
            out_specs=(
                pl.BlockSpec((heads, key_rows, step), lambda i, s: (0, 0, i)),
                pl.BlockSpec((slices, width, slice_rows), lambda i, s: (0, 0, 0)),
                pl.BlockSpec((heads, step), lambda i, s: (0, i)),
                pl.BlockSpec((heads, step), lambda i, s: (0, i)),
            ),
        ),
        out_shape=(
            jax.ShapeDtypeStruct((heads, key_rows, queries), BF16),
            jax.ShapeDtypeStruct((slices, width, slice_rows), BF16),
            jax.ShapeDtypeStruct((heads, queries), F32),
            jax.ShapeDtypeStruct((heads, queries), F32),
        ),
        compiler_params=params(48),
        cost_estimate=pl.CostEstimate(
            flops=4 * heads * queries * key_rows * HEAD_DIM,
            bytes_accessed=12 * MIB,
            transcendentals=heads * queries * key_rows,
        ),
    )(spot, kv, query, bias)


def local_stats(spot, upstream, parts, logs):
    slices, slice_rows, width = upstream.shape
    heads = width // HEAD_DIM

    def kernel(spot_ref, up_ref, parts_ref, log_ref, out_ref):
        deltas = []
        for part in range(slices):
            place = lax.rem(part + spot_ref[1], slices)
            product = up_ref[part].astype(F32).T * parts_ref[place].astype(F32)
            deltas.append(
                [
                    jnp.sum(product[head * HEAD_DIM : (head + 1) * HEAD_DIM], axis=0, keepdims=True)
                    for head in range(heads)
                ]
            )
        rows = []
        for head in range(heads):
            rows.append(log_ref[head : head + 1, :])
            rows.append(jnp.concatenate([delta[head] for delta in deltas], axis=1))
        stats = jnp.concatenate(rows, axis=0)
        for copy in range(slices):
            out_ref[copy] = stats

    vmem = pl.BlockSpec(memory_space=pltpu.VMEM)
    return pl.pallas_call(
        kernel,
        out_shape=jax.ShapeDtypeStruct((slices, 2 * heads, slices * slice_rows), F32),
        in_specs=[pl.BlockSpec(memory_space=pltpu.SMEM), vmem, vmem, vmem],
        out_specs=vmem,
        compiler_params=params(16),
    )(spot, upstream, parts, logs)


def merged_stats(stats, head):
    logs = stats[:, 2 * head, :]
    deltas = stats[:, 2 * head + 1, :]
    top = jnp.max(logs, axis=0, keepdims=True)
    shares = jnp.exp2(logs - top)
    total = jnp.sum(shares, axis=0, keepdims=True)
    shares = shares / total
    return top + jnp.log2(total), shares, jnp.sum(deltas * shares, axis=0, keepdims=True)


def backward_kernel(
    spot_ref,
    kv_ref,
    query_ref,
    up_ref,
    exp_ref,
    stats_ref,
    own_ref,
    cos_block,
    sin_block,
    cos_row,
    sin_row,
    grad_ref,
    keep_ref,
    send_ref,
    acc_ref,
):
    step = pl.program_id(0)
    blocks, block_rows = kv_ref.shape[0], kv_ref.shape[2]
    key_rows = blocks * block_rows
    query_rows = query_ref.shape[0] * query_ref.shape[1]
    heads = kv_ref.shape[3] // HEAD_DIM
    stats = stats_ref[...]
    for head in range(heads):
        lanes = slice(head * HEAD_DIM, (head + 1) * HEAD_DIM)
        log_total, _, delta = merged_stats(stats, head)
        factor = jnp.exp2(own_ref[head : head + 1, :] - log_total)
        keys = kv_ref[:, 0, :, lanes].reshape(key_rows, HEAD_DIM)
        values = kv_ref[:, 1, :, lanes].reshape(key_rows, HEAD_DIM)
        query = query_ref[:, :, lanes].reshape(query_rows, HEAD_DIM)
        upstream = up_ref[:, :, lanes].reshape(query_rows, HEAD_DIM)
        probability = exp_ref[head].astype(F32) * factor
        value_grad = matmul(probability.astype(BF16), upstream)
        prob_grad = matmul(values, upstream, NT)
        score_grad = (probability * (prob_grad - delta)).astype(BF16)
        key_grad = matmul(score_grad, query) * SCALE
        query_part = matmul(keys, score_grad, TN)
        for block in range(blocks):
            part = key_grad[block * block_rows : (block + 1) * block_rows, :]
            cos_a = cos_block[block]
            sin_a = sin_block[block]
            cosine = cos_a * cos_row[...] - sin_a * sin_row[...]
            sine = sin_a * cos_row[...] + cos_a * sin_row[...]
            signed = jnp.where(
                lax.broadcasted_iota(jnp.int32, sine.shape, 1) < HEAD_DIM // 2, sine, -sine
            )
            turned = part * cosine + pltpu.roll(part, HEAD_DIM // 2, 1) * signed
            grad_ref[block, 0, :, lanes] = turned.astype(BF16)
            grad_ref[block, 1, :, lanes] = value_grad[
                block * block_rows : (block + 1) * block_rows, :
            ].astype(BF16)

        @pl.when(step == 0)
        def _():
            acc_ref[lanes, :] = query_part

        @pl.when(step > 0)
        def _():
            acc_ref[lanes, :] += query_part

    @pl.when(step == pl.num_programs(0) - 1)
    def _():
        half = keep_ref.shape[0]
        for slot in range(2 * half):
            place = lax.bitwise_xor(spot_ref[0], PATH[slot]) + 2 * half - spot_ref[1]
            first = pl.multiple_of(lax.rem(place, 2 * half) * 128, 128)
            part = (acc_ref[:, pl.ds(first, 128)] * SCALE).astype(BF16)
            if slot < half:
                keep_ref[slot] = part
            else:
                send_ref[slot - half] = part


def backward(spot, kv, query, upstream, exponent, stats, own, tables):
    blocks, _, block_rows, width = kv.shape
    slices, slice_rows, _ = query.shape
    queries = slices * slice_rows
    heads = width // HEAD_DIM
    per = 4
    key_rows = blocks * block_rows
    whole = lambda shape: pl.BlockSpec(shape, lambda i, s: (0,) * len(shape))
    half = jax.ShapeDtypeStruct((slices // 2, width, slice_rows), BF16)
    return pl.pallas_call(
        backward_kernel,
        grid_spec=pltpu.PrefetchScalarGridSpec(
            num_scalar_prefetch=1,
            grid=(blocks // per,),
            in_specs=[
                pl.BlockSpec((per, 2, block_rows, width), lambda i, s: (i, 0, 0, 0)),
                whole(query.shape),
                whole(query.shape),
                pl.BlockSpec((heads, per * block_rows, queries), lambda i, s: (0, i, 0)),
                whole(stats.shape),
                whole(own.shape),
                pl.BlockSpec((per, 1, HEAD_DIM), lambda i, s: (i, 0, 0)),
                pl.BlockSpec((per, 1, HEAD_DIM), lambda i, s: (i, 0, 0)),
                whole((block_rows, HEAD_DIM)),
                whole((block_rows, HEAD_DIM)),
            ],
            out_specs=(
                pl.BlockSpec((per, 2, block_rows, width), lambda i, s: (i, 0, 0, 0)),
                whole(half.shape),
                whole(half.shape),
            ),
            scratch_shapes=[pltpu.VMEM((width, queries), F32)],
        ),
        out_shape=(jax.ShapeDtypeStruct((blocks, 2, block_rows, width), BF16), half, half),
        compiler_params=params(48),
        cost_estimate=pl.CostEstimate(
            flops=8 * heads * queries * key_rows * HEAD_DIM,
            bytes_accessed=14 * MIB,
            transcendentals=0,
        ),
    )(spot, kv, query, upstream, exponent, stats, own, *tables)


def merge_output(parts, stats):
    def kernel(parts_ref, stats_ref, out_ref):
        for head in range(parts_ref.shape[1] // HEAD_DIM):
            lanes = slice(head * HEAD_DIM, (head + 1) * HEAD_DIM)
            _, shares, _ = merged_stats(stats_ref[...], head)
            total = jnp.zeros((HEAD_DIM, parts_ref.shape[2]), F32)
            for block in range(parts_ref.shape[0]):
                total += parts_ref[block, lanes, :].astype(F32) * shares[block : block + 1, :]
            out_ref[lanes, :] = total.astype(BF16)

    return pl.pallas_call(
        kernel, out_shape=jax.ShapeDtypeStruct(parts.shape[1:], BF16), compiler_params=params(8)
    )(parts, stats)


def merge_query_grad(kept, arrived, cosine, sine):
    def kernel(kept_ref, arrived_ref, cos_ref, sin_ref, out_ref):
        total = kept_ref[0].astype(F32) + arrived_ref[0].astype(F32)
        half = HEAD_DIM // 2
        turned = []
        for head in range(total.shape[0] // HEAD_DIM):
            first = total[head * HEAD_DIM : head * HEAD_DIM + half, :]
            second = total[head * HEAD_DIM + half : (head + 1) * HEAD_DIM, :]
            turned.append(first * cos_ref[...] + second * sin_ref[...])
            turned.append(second * cos_ref[...] - first * sin_ref[...])
        out_ref[...] = jnp.concatenate(turned, axis=0).T.astype(BF16)

    return pl.pallas_call(
        kernel,
        out_shape=jax.ShapeDtypeStruct((kept.shape[2], kept.shape[1]), BF16),
        compiler_params=params(8),
    )(kept, arrived, cosine, sine)


def projection_grad(spot, parts, cotangent):
    count = len(parts)

    def kernel(spot_ref, *refs):
        cot_ref, out_ref, joined_ref = refs[count:]
        for k in range(count):
            place = lax.rem(spot_ref[1] - spot_ref[0] + 2 * count - k, count)
            joined_ref[:, pl.ds(pl.multiple_of(place * 128, 128), 128)] = refs[k][...]
        out_ref[...] = matmul(joined_ref[...], cot_ref[...]) * (1.0 / LOSS_SCALE)

    vmem = pl.BlockSpec(memory_space=pltpu.VMEM)
    width = parts[0].shape[0]
    return pl.pallas_call(
        kernel,
        out_shape=jax.ShapeDtypeStruct((width, cotangent.shape[1]), F32),
        in_specs=[pl.BlockSpec(memory_space=pltpu.SMEM)] + [vmem] * (count + 1),
        out_specs=vmem,
        scratch_shapes=[pltpu.VMEM((width, count * 128), BF16)],
        compiler_params=params(16),
    )(spot, *parts, cotangent)


def assemble(spot, near, far, shifted):
    count = 2 * near.shape[0]

    def kernel(spot_ref, near_ref, far_ref, out_ref):
        for slot in range(count):
            place = lax.bitwise_xor(spot_ref[0], PATH[slot])
            if shifted:
                place = lax.rem(place + count - spot_ref[1], count)
            out_ref[place] = (near_ref if slot < count // 2 else far_ref)[slot % (count // 2)]

    vmem = pl.BlockSpec(memory_space=pltpu.VMEM)
    return pl.pallas_call(
        kernel,
        out_shape=jax.ShapeDtypeStruct((count,) + near.shape[1:], BF16),
        in_specs=[pl.BlockSpec(memory_space=pltpu.SMEM), vmem, vmem],
        out_specs=vmem,
        compiler_params=params(16),
    )(spot, near, far)


def upstream_part(cotangent, out_weight):
    def kernel(cot_ref, weight_ref, out_ref):
        out_ref[...] = matmul(cot_ref[...], weight_ref[...], NT).astype(BF16)

    return pl.pallas_call(
        kernel,
        out_shape=jax.ShapeDtypeStruct((cotangent.shape[0], out_weight.shape[0]), BF16),
        compiler_params=params(32),
    )(cotangent, out_weight)


def per_device(
    queries, key_vectors, value_vectors, cotangent, out_weight, frame_valid, group_offset, guide_index
):
    seq_count, fsdp_count = lax.axis_size("seq"), lax.axis_size("fsdp")
    z_count = fsdp_count
    x_count = seq_count // z_count
    seq_index, fsdp_index = lax.axis_index("seq"), lax.axis_index("fsdp")
    z_index = seq_index % z_count
    cfg_index = lax.axis_index("cfg")
    block_rows = key_vectors.shape[1]
    group_rows, width = queries.shape[1], queries.shape[2]
    slice_rows = group_rows // z_count

    def place(x, z, f):
        return (x * z_count + z) * fsdp_count + f

    spots = [
        (x, z, f) for x in range(x_count) for z in range(z_count) for f in range(fsdp_count)
    ]
    plane_groups = [
        [place(x, z, f) for x in range(x_count) for f in range(fsdp_count)] for z in range(z_count)
    ]
    column_groups = [[x * z_count + z for z in range(z_count)] for x in range(x_count)]
    turn = [(place(x, z, f), place(x, (f + z) % z_count, z)) for x, z, f in spots]
    back = [(d, s) for s, d in turn]
    spread = [
        [(place(x, z, f), place(x, f, (z + k) % fsdp_count)) for x, z, f in spots]
        for k in range(fsdp_count)
    ]

    def over_plane(x):
        return lax.all_to_all(x, ("seq", "fsdp"), 0, 0, axis_index_groups=plane_groups, tiled=True)

    def over_column(x):
        return lax.all_to_all(x, "seq", 0, 0, axis_index_groups=column_groups, tiled=True)

    def over_fsdp(x):
        return lax.all_to_all(x, "fsdp", 0, 0, tiled=True)

    def z_partner(x, bit):
        return lax.ppermute(x, "seq", [(s, s ^ bit) for s in range(seq_count)])

    def doubled(x, partner):
        near = x[None]
        for bit in (4, 2):
            near = jnp.concatenate([near, partner(near, bit)])
        return near, partner(near, 1)

    tied = lax.optimization_barrier
    spot = jnp.stack([z_index, fsdp_index]).astype(jnp.int32)
    guide = 1.5 + guide_index[0].astype(F32) / 1024.0
    own_weight = jnp.where(cfg_index == 0, guide, 1.0 - guide)

    query_rows = lax.dynamic_slice(
        queries[0], (fsdp_index * slice_rows, 0), (slice_rows, width)
    )
    query_rows = lax.ppermute(query_rows, ("seq", "fsdp"), turn)
    partial = upstream_part(cotangent, out_weight).reshape(fsdp_count, slice_rows, width)
    partial = over_fsdp(partial)
    packed = pack_blocks(key_vectors, value_vectors, x_count * fsdp_count)
    query_rows, partial, packed = tied((query_rows, partial, packed))

    kv = over_plane(packed)
    summed = jnp.sum(partial.astype(F32), axis=0)
    upstream_rows = (own_weight * summed).astype(BF16)
    query = assemble(spot, *doubled(query_rows, z_partner), True)
    upstream_heads = assemble(spot, *doubled(upstream_rows, z_partner), False)

    block_ids = jnp.arange(x_count * fsdp_count, dtype=jnp.int32)
    block_start = place(block_ids // fsdp_count, z_index, block_ids % fsdp_count) * block_rows
    row_ids = jnp.arange(block_rows, dtype=jnp.int32)
    positions = (block_start[:, None] + row_ids[None, :]).reshape(-1)
    frame_match = (positions // FRAME_TOK)[:, None] == jnp.arange(
        frame_valid.shape[0], dtype=jnp.int32
    )[None, :]
    valid = jnp.sum(jnp.where(frame_match, frame_valid[None, :], 0), axis=1) == 1
    bias = jnp.broadcast_to(
        jnp.where(valid, 0.0, NEG_LARGE).astype(F32)[:, None], (positions.shape[0], 128)
    )
    frequency = 10000.0 ** (-jnp.arange(HEAD_DIM // 2, dtype=F32) / (HEAD_DIM // 2))
    twice = jnp.concatenate([frequency, frequency])
    block_angle = (block_start.astype(F32)[:, None] * twice[None, :])[:, None, :]
    row_angle = row_ids.astype(F32)[:, None] * twice[None, :]
    tables = (jnp.cos(block_angle), jnp.sin(block_angle), jnp.cos(row_angle), jnp.sin(row_angle))
    slice_id = (z_index - fsdp_index) % z_count
    query_positions = (
        group_offset[0] + slice_id * slice_rows + jnp.arange(slice_rows, dtype=jnp.int32)
    )
    query_angle = query_positions.astype(F32)[None, :] * frequency[:, None]

    kv, query, upstream_heads = tied((kv, query, upstream_heads))
    upstream = over_fsdp(upstream_heads)
    exponent, out_parts, own_logs, own_top = forward(spot, kv, query, bias)
    stats = over_column(local_stats(spot, upstream, out_parts, own_logs))
    stats, out_parts = tied((stats, out_parts))
    out_slices = over_column(out_parts)
    grads, query_keep, query_send = backward(
        spot, kv, query, upstream, exponent, stats, own_top, tables
    )
    grads, out_slices, query_send = tied((grads, out_slices, query_send))
    key_grad, value_grad = unpack_blocks(over_plane(grads))

    slice_stats = lax.dynamic_slice_in_dim(stats, slice_id * slice_rows, slice_rows, axis=2)
    attn_rows = merge_output(out_slices, slice_stats)
    other_rows = lax.ppermute(attn_rows, "cfg", [(0, 1), (1, 0)])
    mixed = own_weight * attn_rows.astype(F32) + (1.0 - own_weight) * other_rows.astype(F32)
    mixed = mixed.astype(BF16)
    weight_grad = projection_grad(
        spot, [lax.ppermute(mixed, ("seq", "fsdp"), perm) for perm in spread], cotangent
    )

    for bit in (1, 2):
        arrived = z_partner(query_send, bit)
        total = (query_keep.astype(F32) + arrived.astype(F32)).astype(BF16)
        half = total.shape[0] // 2
        query_keep, query_send = total[:half], total[half:]
    arrived = z_partner(query_send, 4)
    query_slice = merge_query_grad(query_keep, arrived, jnp.cos(query_angle), jnp.sin(query_angle))
    query_grad = lax.ppermute(query_slice, ("seq", "fsdp"), back)[None]
    return (query_grad, key_grad, value_grad, weight_grad)


def solution(mesh):
    placed = (
        P("cfg", None, "seq"),
        P("cfg", ("seq", "fsdp"), None),
        P("cfg", ("seq", "fsdp"), None),
        P(None, "fsdp"),
        P("seq", "fsdp"),
        P(),
        P(),
        P(),
    )
    return jax.shard_map(
        per_device,
        mesh=mesh,
        in_specs=placed,
        out_specs=(
            P("cfg", "fsdp", "seq"),
            P("cfg", ("seq", "fsdp"), None),
            P("cfg", ("seq", "fsdp"), None),
            P("seq", "fsdp"),
        ),
        check_vma=False,
    )
```

```python
import math

import jax
import jax.numpy as jnp
from jax import lax
from jax.experimental import pallas as pl
from jax.experimental.pallas import tpu as pltpu
from jax.sharding import PartitionSpec as P

HEAD_DIM = 128
FRAME_TOK = 3600
NEG_LARGE = -1e30
NEG_FLOOR = -1e29
LOSS_SCALE = 128.0
SCALE = 1.0 / math.sqrt(HEAD_DIM)
EXP2_SCALE = SCALE * math.log2(math.e)
BF16 = jnp.bfloat16
F32 = jnp.float32
MIB = 1024 * 1024

PATH = (0, 4, 2, 6, 1, 5, 3, 7)
NT = (((1,), (1,)), ((), ()))
TN = (((0,), (0,)), ((), ()))


def matmul(a, b, dims=(((1,), (0,)), ((), ()))):
    return lax.dot_general(a, b, dims, preferred_element_type=F32)


def params(mib):
    return pltpu.CompilerParams(vmem_limit_bytes=mib * MIB)


def pack_blocks(keys, values, parts):
    rows, width = keys.shape[1], keys.shape[2] // parts
    per = 4

    def kernel(k_ref, v_ref, out_ref):
        for which, ref in enumerate((k_ref, v_ref)):
            for part in range(per):
                out_ref[part, which] = ref[0, :, part * width : (part + 1) * width]

    return pl.pallas_call(
        kernel,
        grid=(parts // per,),
        out_shape=jax.ShapeDtypeStruct((parts, 2, rows, width), keys.dtype),
        in_specs=[pl.BlockSpec((1, rows, per * width), lambda i: (0, 0, i))] * 2,
        out_specs=pl.BlockSpec((per, 2, rows, width), lambda i: (i, 0, 0, 0)),
        compiler_params=params(16),
    )(keys, values)


def unpack_blocks(packed):
    parts, _, rows, width = packed.shape
    per = 4

    def kernel(in_ref, k_ref, v_ref):
        for which, ref in enumerate((k_ref, v_ref)):
            for part in range(per):
                ref[0, :, part * width : (part + 1) * width] = in_ref[part, which]

    shape = jax.ShapeDtypeStruct((1, rows, parts * width), packed.dtype)
    return pl.pallas_call(
        kernel,
        grid=(parts // per,),
        out_shape=(shape, shape),
        in_specs=[pl.BlockSpec((per, 2, rows, width), lambda i: (i, 0, 0, 0))],
        out_specs=(pl.BlockSpec((1, rows, per * width), lambda i: (0, 0, i)),) * 2,
        compiler_params=params(16),
    )(packed)


def forward_kernel(spot_ref, kv_ref, query_ref, bias_ref, exp_ref, out_ref, log_ref, top_ref):
    key_rows = kv_ref.shape[0] * kv_ref.shape[2]
    per, slice_rows = query_ref.shape[0], query_ref.shape[1]
    query_rows = per * slice_rows
    slices = out_ref.shape[0]
    heads = kv_ref.shape[3] // HEAD_DIM
    bias = jnp.concatenate([bias_ref[...]] * (query_rows // 128), axis=1)
    logs, tops = [], []
    for head in range(heads):
        lanes = slice(head * HEAD_DIM, (head + 1) * HEAD_DIM)
        keys = kv_ref[:, 0, :, lanes].reshape(key_rows, HEAD_DIM)
        values = kv_ref[:, 1, :, lanes].reshape(key_rows, HEAD_DIM)
        query = query_ref[:, :, lanes].reshape(query_rows, HEAD_DIM)
        scores = matmul(keys, query, NT) * EXP2_SCALE + bias
        top = jnp.maximum(jnp.max(scores, axis=0, keepdims=True), NEG_FLOOR)
        exponent = jnp.exp2(scores - top)
        total = jnp.sum(exponent, axis=0, keepdims=True)
        exponent_bf = exponent.astype(BF16)
        exp_ref[head] = exponent_bf
        safe = jnp.maximum(total, 1e-30)
        output = (matmul(values, exponent_bf, TN) * (1.0 / safe)).astype(BF16)
        logs.append(jnp.where(total > 0.0, top + jnp.log2(safe), NEG_FLOOR))
        tops.append(top)
        for part in range(per):
            place = lax.rem(pl.program_id(0) * per + part + spot_ref[1], slices)
            out_ref[place, lanes, :] = output[:, part * slice_rows : (part + 1) * slice_rows]
    log_ref[...] = jnp.concatenate(logs, axis=0)
    top_ref[...] = jnp.concatenate(tops, axis=0)


def forward(spot, kv, query, bias):
    blocks, _, block_rows, width = kv.shape
    key_rows = blocks * block_rows
    slices, slice_rows, _ = query.shape
    queries = slices * slice_rows
    heads = width // HEAD_DIM
    step = 256
    per = step // slice_rows
    return pl.pallas_call(
        forward_kernel,
        grid_spec=pltpu.PrefetchScalarGridSpec(
            num_scalar_prefetch=1,
            grid=(queries // step,),
            in_specs=[
                pl.BlockSpec((blocks, 2, block_rows, width), lambda i, s: (0, 0, 0, 0)),
                pl.BlockSpec((per, slice_rows, width), lambda i, s: (i, 0, 0)),
                pl.BlockSpec((key_rows, 128), lambda i, s: (0, 0)),
            ],
            out_specs=(
                pl.BlockSpec((heads, key_rows, step), lambda i, s: (0, 0, i)),
                pl.BlockSpec((slices, width, slice_rows), lambda i, s: (0, 0, 0)),
                pl.BlockSpec((heads, step), lambda i, s: (0, i)),
                pl.BlockSpec((heads, step), lambda i, s: (0, i)),
            ),
        ),
        out_shape=(
            jax.ShapeDtypeStruct((heads, key_rows, queries), BF16),
            jax.ShapeDtypeStruct((slices, width, slice_rows), BF16),
            jax.ShapeDtypeStruct((heads, queries), F32),
            jax.ShapeDtypeStruct((heads, queries), F32),
        ),
        compiler_params=params(60),
        cost_estimate=pl.CostEstimate(
            flops=4 * heads * queries * key_rows * HEAD_DIM,
            bytes_accessed=12 * MIB,
            transcendentals=heads * queries * key_rows,
        ),
    )(spot, kv, query, bias)


def local_stats(spot, upstream, parts, logs):
    slices, slice_rows, width = upstream.shape
    heads = width // HEAD_DIM

    def kernel(spot_ref, up_ref, parts_ref, log_ref, out_ref):
        deltas = []
        for part in range(slices):
            place = lax.rem(part + spot_ref[1], slices)
            product = up_ref[part].astype(F32).T * parts_ref[place].astype(F32)
            deltas.append(
                [
                    jnp.sum(product[head * HEAD_DIM : (head + 1) * HEAD_DIM], axis=0, keepdims=True)
                    for head in range(heads)
                ]
            )
        rows = []
        for head in range(heads):
            rows.append(log_ref[head : head + 1, :])
            rows.append(jnp.concatenate([delta[head] for delta in deltas], axis=1))
        stats = jnp.concatenate(rows, axis=0)
        for copy in range(slices):
            out_ref[copy] = stats

    vmem = pl.BlockSpec(memory_space=pltpu.VMEM)
    return pl.pallas_call(
        kernel,
        out_shape=jax.ShapeDtypeStruct((slices, 2 * heads, slices * slice_rows), F32),
        in_specs=[pl.BlockSpec(memory_space=pltpu.SMEM), vmem, vmem, vmem],
        out_specs=vmem,
        compiler_params=params(16),
    )(spot, upstream, parts, logs)


def merged_stats(stats, head):
    logs = stats[:, 2 * head, :]
    deltas = stats[:, 2 * head + 1, :]
    top = jnp.max(logs, axis=0, keepdims=True)
    shares = jnp.exp2(logs - top)
    total = jnp.sum(shares, axis=0, keepdims=True)
    shares = shares / total
    return top + jnp.log2(total), shares, jnp.sum(deltas * shares, axis=0, keepdims=True)


def backward_kernel(
    spot_ref,
    kv_ref,
    query_ref,
    up_ref,
    exp_ref,
    stats_ref,
    own_ref,
    cos_block,
    sin_block,
    cos_row,
    sin_row,
    grad_ref,
    keep_ref,
    send_ref,
    acc_ref,
):
    step = pl.program_id(0)
    blocks, block_rows = kv_ref.shape[0], kv_ref.shape[2]
    key_rows = blocks * block_rows
    query_rows = query_ref.shape[0] * query_ref.shape[1]
    heads = kv_ref.shape[3] // HEAD_DIM
    stats = stats_ref[...]
    for head in range(heads):
        lanes = slice(head * HEAD_DIM, (head + 1) * HEAD_DIM)
        log_total, _, delta = merged_stats(stats, head)
        factor = jnp.exp2(own_ref[head : head + 1, :] - log_total)
        keys = kv_ref[:, 0, :, lanes].reshape(key_rows, HEAD_DIM)
        values = kv_ref[:, 1, :, lanes].reshape(key_rows, HEAD_DIM)
        query = query_ref[:, :, lanes].reshape(query_rows, HEAD_DIM)
        upstream = up_ref[:, :, lanes].reshape(query_rows, HEAD_DIM)
        probability = exp_ref[head].astype(F32) * factor
        value_grad = matmul(probability.astype(BF16), upstream)
        prob_grad = matmul(values, upstream, NT)
        score_grad = (probability * (prob_grad - delta)).astype(BF16)
        key_grad = matmul(score_grad, query) * SCALE
        query_part = matmul(keys, score_grad, TN)
        for block in range(blocks):
            part = key_grad[block * block_rows : (block + 1) * block_rows, :]
            cos_a = cos_block[block]
            sin_a = sin_block[block]
            cosine = cos_a * cos_row[...] - sin_a * sin_row[...]
            sine = sin_a * cos_row[...] + cos_a * sin_row[...]
            signed = jnp.where(
                lax.broadcasted_iota(jnp.int32, sine.shape, 1) < HEAD_DIM // 2, sine, -sine
            )
            turned = part * cosine + pltpu.roll(part, HEAD_DIM // 2, 1) * signed
            grad_ref[block, 0, :, lanes] = turned.astype(BF16)
            grad_ref[block, 1, :, lanes] = value_grad[
                block * block_rows : (block + 1) * block_rows, :
            ].astype(BF16)

        @pl.when(step == 0)
        def _():
            acc_ref[lanes, :] = query_part

        @pl.when(step > 0)
        def _():
            acc_ref[lanes, :] += query_part

    @pl.when(step == pl.num_programs(0) - 1)
    def _():
        half = keep_ref.shape[0]
        for slot in range(2 * half):
            place = lax.bitwise_xor(spot_ref[0], PATH[slot]) + 2 * half - spot_ref[1]
            first = pl.multiple_of(lax.rem(place, 2 * half) * 128, 128)
            part = (acc_ref[:, pl.ds(first, 128)] * SCALE).astype(BF16)
            if slot < half:
                keep_ref[slot] = part
            else:
                send_ref[slot - half] = part


def backward(spot, kv, query, upstream, exponent, stats, own, tables):
    blocks, _, block_rows, width = kv.shape
    slices, slice_rows, _ = query.shape
    queries = slices * slice_rows
    heads = width // HEAD_DIM
    per = 4
    key_rows = blocks * block_rows
    whole = lambda shape: pl.BlockSpec(shape, lambda i, s: (0,) * len(shape))
    half = jax.ShapeDtypeStruct((slices // 2, width, slice_rows), BF16)
    return pl.pallas_call(
        backward_kernel,
        grid_spec=pltpu.PrefetchScalarGridSpec(
            num_scalar_prefetch=1,
            grid=(blocks // per,),
            in_specs=[
                pl.BlockSpec((per, 2, block_rows, width), lambda i, s: (i, 0, 0, 0)),
                whole(query.shape),
                whole(query.shape),
                pl.BlockSpec((heads, per * block_rows, queries), lambda i, s: (0, i, 0)),
                whole(stats.shape),
                whole(own.shape),
                pl.BlockSpec((per, 1, HEAD_DIM), lambda i, s: (i, 0, 0)),
                pl.BlockSpec((per, 1, HEAD_DIM), lambda i, s: (i, 0, 0)),
                whole((block_rows, HEAD_DIM)),
                whole((block_rows, HEAD_DIM)),
            ],
            out_specs=(
                pl.BlockSpec((per, 2, block_rows, width), lambda i, s: (i, 0, 0, 0)),
                whole(half.shape),
                whole(half.shape),
            ),
            scratch_shapes=[pltpu.VMEM((width, queries), F32)],
        ),
        out_shape=(jax.ShapeDtypeStruct((blocks, 2, block_rows, width), BF16), half, half),
        compiler_params=params(60),
        cost_estimate=pl.CostEstimate(
            flops=8 * heads * queries * key_rows * HEAD_DIM,
            bytes_accessed=14 * MIB,
            transcendentals=0,
        ),
    )(spot, kv, query, upstream, exponent, stats, own, *tables)


def merge_output(parts, stats):
    def kernel(parts_ref, stats_ref, out_ref):
        for head in range(parts_ref.shape[1] // HEAD_DIM):
            lanes = slice(head * HEAD_DIM, (head + 1) * HEAD_DIM)
            _, shares, _ = merged_stats(stats_ref[...], head)
            total = jnp.zeros((HEAD_DIM, parts_ref.shape[2]), F32)
            for block in range(parts_ref.shape[0]):
                total += parts_ref[block, lanes, :].astype(F32) * shares[block : block + 1, :]
            out_ref[lanes, :] = total.astype(BF16)

    return pl.pallas_call(
        kernel, out_shape=jax.ShapeDtypeStruct(parts.shape[1:], BF16), compiler_params=params(8)
    )(parts, stats)


def merge_query_grad(kept, arrived, cosine, sine):
    def kernel(kept_ref, arrived_ref, cos_ref, sin_ref, out_ref):
        total = kept_ref[0].astype(F32) + arrived_ref[0].astype(F32)
        half = HEAD_DIM // 2
        turned = []
        for head in range(total.shape[0] // HEAD_DIM):
            first = total[head * HEAD_DIM : head * HEAD_DIM + half, :]
            second = total[head * HEAD_DIM + half : (head + 1) * HEAD_DIM, :]
            turned.append(first * cos_ref[...] + second * sin_ref[...])
            turned.append(second * cos_ref[...] - first * sin_ref[...])
        out_ref[...] = jnp.concatenate(turned, axis=0).T.astype(BF16)

    return pl.pallas_call(
        kernel,
        out_shape=jax.ShapeDtypeStruct((kept.shape[2], kept.shape[1]), BF16),
        compiler_params=params(8),
    )(kept, arrived, cosine, sine)


def projection_grad(parts, cotangent):
    count, width, _ = parts.shape

    def kernel(parts_ref, cot_ref, out_ref):
        joined = jnp.concatenate([parts_ref[part] for part in range(count)], axis=1)
        out_ref[...] = matmul(joined, cot_ref[...]) * (1.0 / LOSS_SCALE)

    return pl.pallas_call(
        kernel,
        out_shape=jax.ShapeDtypeStruct((width, cotangent.shape[1]), F32),
        compiler_params=params(16),
    )(parts, cotangent)


def own_slice(spot, queries, slice_rows):
    width = queries.shape[2]

    def kernel(spot_ref, in_ref, out_ref):
        out_ref[...] = in_ref[0]

    return pl.pallas_call(
        kernel,
        grid_spec=pltpu.PrefetchScalarGridSpec(
            num_scalar_prefetch=1,
            grid=(1,),
            in_specs=[pl.BlockSpec((1, slice_rows, width), lambda i, s: (0, s[1], 0))],
            out_specs=pl.BlockSpec((slice_rows, width), lambda i, s: (0, 0)),
        ),
        out_shape=jax.ShapeDtypeStruct((slice_rows, width), queries.dtype),
        compiler_params=params(60),
    )(spot, queries)


def assemble(spot, near, far, shifted):
    count = 2 * near.shape[0]

    def kernel(spot_ref, near_ref, far_ref, out_ref):
        for slot in range(count):
            place = lax.bitwise_xor(spot_ref[0], PATH[slot])
            if shifted:
                place = lax.rem(place + count - spot_ref[1], count)
            out_ref[place] = (near_ref if slot < count // 2 else far_ref)[slot % (count // 2)]

    vmem = pl.BlockSpec(memory_space=pltpu.VMEM)
    return pl.pallas_call(
        kernel,
        out_shape=jax.ShapeDtypeStruct((count,) + near.shape[1:], BF16),
        in_specs=[pl.BlockSpec(memory_space=pltpu.SMEM), vmem, vmem],
        out_specs=vmem,
        compiler_params=params(8),
    )(spot, near, far)


def upstream_part(cotangent, out_weight):
    def kernel(cot_ref, weight_ref, out_ref):
        out_ref[...] = matmul(cot_ref[...], weight_ref[...], NT).astype(BF16)

    return pl.pallas_call(
        kernel,
        out_shape=jax.ShapeDtypeStruct((cotangent.shape[0], out_weight.shape[0]), BF16),
        compiler_params=params(60),
    )(cotangent, out_weight)


def per_device(
    queries, key_vectors, value_vectors, cotangent, out_weight, frame_valid, group_offset, guide_index
):
    seq_count, fsdp_count = lax.axis_size("seq"), lax.axis_size("fsdp")
    z_count = fsdp_count
    x_count = seq_count // z_count
    seq_index, fsdp_index = lax.axis_index("seq"), lax.axis_index("fsdp")
    z_index = seq_index % z_count
    cfg_index = lax.axis_index("cfg")
    block_rows = key_vectors.shape[1]
    group_rows, width = queries.shape[1], queries.shape[2]
    slice_rows = group_rows // z_count

    def place(x, z, f):
        return (x * z_count + z) * fsdp_count + f

    spots = [
        (x, z, f) for x in range(x_count) for z in range(z_count) for f in range(fsdp_count)
    ]
    plane_groups = [
        [place(x, z, f) for x in range(x_count) for f in range(fsdp_count)] for z in range(z_count)
    ]
    column_groups = [[x * z_count + z for z in range(z_count)] for x in range(x_count)]
    turn = [(place(x, z, f), place(x, (f + z) % z_count, z)) for x, z, f in spots]
    back = [(d, s) for s, d in turn]

    def over_plane(x):
        return lax.all_to_all(x, ("seq", "fsdp"), 0, 0, axis_index_groups=plane_groups, tiled=True)

    def over_column(x):
        return lax.all_to_all(x, "seq", 0, 0, axis_index_groups=column_groups, tiled=True)

    def over_fsdp(x):
        return lax.all_to_all(x, "fsdp", 0, 0, tiled=True)

    def z_partner(x, bit):
        return lax.ppermute(x, "seq", [(s, s ^ bit) for s in range(seq_count)])

    def doubled(near, bits):
        for bit in bits[:-1]:
            near = jnp.concatenate([near, z_partner(near, bit)])
        return near, z_partner(near, bits[-1])

    tied = lax.optimization_barrier
    spot = jnp.stack([z_index, fsdp_index]).astype(jnp.int32)
    guide = 1.5 + guide_index[0].astype(F32) / 1024.0
    own_weight = jnp.where(cfg_index == 0, guide, 1.0 - guide)

    query_rows = own_slice(spot, queries, slice_rows)
    query_rows, cotangent_first = tied((query_rows, cotangent))
    query_rows = lax.ppermute(query_rows, ("seq", "fsdp"), turn)[None]
    query_rows = jnp.concatenate([query_rows, z_partner(query_rows, 4)])
    partial = upstream_part(cotangent_first, out_weight).reshape(fsdp_count, slice_rows, width)
    partial = over_fsdp(partial)
    packed = pack_blocks(key_vectors, value_vectors, x_count * fsdp_count)
    query_rows, partial, packed = tied((query_rows, partial, packed))

    kv = over_plane(packed)
    summed = jnp.sum(partial.astype(F32), axis=0)
    upstream_rows = (own_weight * summed).astype(BF16)
    query = assemble(spot, *doubled(query_rows, (2, 1)), True)
    upstream_heads = assemble(spot, *doubled(upstream_rows[None], (4, 2, 1)), False)

    block_ids = jnp.arange(x_count * fsdp_count, dtype=jnp.int32)
    block_start = place(block_ids // fsdp_count, z_index, block_ids % fsdp_count) * block_rows
    row_ids = jnp.arange(block_rows, dtype=jnp.int32)
    positions = (block_start[:, None] + row_ids[None, :]).reshape(-1)
    frame_match = (positions // FRAME_TOK)[:, None] == jnp.arange(
        frame_valid.shape[0], dtype=jnp.int32
    )[None, :]
    valid = jnp.sum(jnp.where(frame_match, frame_valid[None, :], 0), axis=1) == 1
    bias = jnp.broadcast_to(
        jnp.where(valid, 0.0, NEG_LARGE).astype(F32)[:, None], (positions.shape[0], 128)
    )
    frequency = 10000.0 ** (-jnp.arange(HEAD_DIM // 2, dtype=F32) / (HEAD_DIM // 2))
    twice = jnp.concatenate([frequency, frequency])
    block_angle = (block_start.astype(F32)[:, None] * twice[None, :])[:, None, :]
    row_angle = row_ids.astype(F32)[:, None] * twice[None, :]
    tables = (jnp.cos(block_angle), jnp.sin(block_angle), jnp.cos(row_angle), jnp.sin(row_angle))
    slice_id = (z_index - fsdp_index) % z_count
    query_positions = (
        group_offset[0] + slice_id * slice_rows + jnp.arange(slice_rows, dtype=jnp.int32)
    )
    query_angle = query_positions.astype(F32)[None, :] * frequency[:, None]

    kv, query, upstream_heads = tied((kv, query, upstream_heads))
    upstream = over_fsdp(upstream_heads)
    exponent, out_parts, own_logs, own_top = forward(spot, kv, query, bias)
    stats = over_column(local_stats(spot, upstream, out_parts, own_logs))
    stats, out_parts = tied((stats, out_parts))
    out_slices = over_column(out_parts)
    grads, query_keep, query_send = backward(
        spot, kv, query, upstream, exponent, stats, own_top, tables
    )
    grads, out_slices, query_send = tied((grads, out_slices, query_send))
    grads = over_plane(grads)

    slice_stats = lax.dynamic_slice_in_dim(stats, slice_id * slice_rows, slice_rows, axis=2)
    attn_rows = merge_output(out_slices, slice_stats)
    other_rows = lax.ppermute(attn_rows, "cfg", [(0, 1), (1, 0)])
    mixed = own_weight * attn_rows.astype(F32) + (1.0 - own_weight) * other_rows.astype(F32)
    mixed = lax.ppermute(mixed.astype(BF16), ("seq", "fsdp"), back)
    mixed = jnp.broadcast_to(mixed[None], (fsdp_count,) + mixed.shape)
    mixed, grads = tied((mixed, grads))
    key_grad, value_grad = unpack_blocks(grads)
    weight_grad = projection_grad(over_fsdp(mixed), cotangent)

    for bit in (1, 2):
        arrived = z_partner(query_send, bit)
        total = (query_keep.astype(F32) + arrived.astype(F32)).astype(BF16)
        half = total.shape[0] // 2
        query_keep, query_send = total[:half], total[half:]
    arrived = z_partner(query_send, 4)
    query_slice = merge_query_grad(query_keep, arrived, jnp.cos(query_angle), jnp.sin(query_angle))
    query_grad = lax.ppermute(query_slice, ("seq", "fsdp"), back)[None]
    return (query_grad, key_grad, value_grad, weight_grad)


def solution(mesh):
    placed = (
        P("cfg", None, "seq"),
        P("cfg", ("seq", "fsdp"), None),
        P("cfg", ("seq", "fsdp"), None),
        P(None, "fsdp"),
        P("seq", "fsdp"),
        P(),
        P(),
        P(),
    )
    return jax.shard_map(
        per_device,
        mesh=mesh,
        in_specs=placed,
        out_specs=(
            P("cfg", "fsdp", "seq"),
            P("cfg", ("seq", "fsdp"), None),
            P("cfg", ("seq", "fsdp"), None),
            P("seq", "fsdp"),
        ),
        check_vma=False,
    )
```

```python
import math

import jax
import jax.numpy as jnp
from jax import lax
from jax.experimental import pallas as pl
from jax.experimental.pallas import tpu as pltpu
from jax.sharding import PartitionSpec as P

HEAD_DIM = 128
FRAME_TOK = 3600
NEG_LARGE = -1e30
NEG_FLOOR = -1e29
LOSS_SCALE = 128.0
SCALE = 1.0 / math.sqrt(HEAD_DIM)
EXP2_SCALE = SCALE * math.log2(math.e)
BF16 = jnp.bfloat16
F32 = jnp.float32
MIB = 1024 * 1024

PATH = (0, 4, 2, 6, 1, 5, 3, 7)
NT = (((1,), (1,)), ((), ()))
TN = (((0,), (0,)), ((), ()))


def matmul(a, b, dims=(((1,), (0,)), ((), ()))):
    return lax.dot_general(a, b, dims, preferred_element_type=F32)


def params(mib):
    return pltpu.CompilerParams(vmem_limit_bytes=mib * MIB)


def pack_blocks(keys, values, parts):
    rows, width = keys.shape[1], keys.shape[2] // parts
    per = 4

    def kernel(k_ref, v_ref, out_ref):
        for which, ref in enumerate((k_ref, v_ref)):
            for part in range(per):
                out_ref[part, which] = ref[0, :, part * width : (part + 1) * width]

    return pl.pallas_call(
        kernel,
        grid=(parts // per,),
        out_shape=jax.ShapeDtypeStruct((parts, 2, rows, width), keys.dtype),
        in_specs=[pl.BlockSpec((1, rows, per * width), lambda i: (0, 0, i))] * 2,
        out_specs=pl.BlockSpec((per, 2, rows, width), lambda i: (i, 0, 0, 0)),
        compiler_params=params(16),
    )(keys, values)


def unpack_blocks(packed):
    parts, _, rows, width = packed.shape
    per = 4

    def kernel(in_ref, k_ref, v_ref):
        for which, ref in enumerate((k_ref, v_ref)):
            for part in range(per):
                ref[0, :, part * width : (part + 1) * width] = in_ref[part, which]

    shape = jax.ShapeDtypeStruct((1, rows, parts * width), packed.dtype)
    return pl.pallas_call(
        kernel,
        grid=(parts // per,),
        out_shape=(shape, shape),
        in_specs=[pl.BlockSpec((per, 2, rows, width), lambda i: (i, 0, 0, 0))],
        out_specs=(pl.BlockSpec((1, rows, per * width), lambda i: (0, 0, i)),) * 2,
        compiler_params=params(16),
    )(packed)


def forward_kernel(kv_ref, query_ref, up_ref, bias_ref, exp_ref, out_ref, stat_ref, top_ref):
    key_rows = kv_ref.shape[0] * kv_ref.shape[2]
    per, slice_rows = query_ref.shape[0], query_ref.shape[1]
    query_rows = per * slice_rows
    heads = kv_ref.shape[3] // HEAD_DIM
    bias = jnp.concatenate([bias_ref[...]] * (query_rows // 128), axis=1)
    rows, tops = [], []
    for head in range(heads):
        lanes = slice(head * HEAD_DIM, (head + 1) * HEAD_DIM)
        keys = kv_ref[:, 0, :, lanes].reshape(key_rows, HEAD_DIM)
        values = kv_ref[:, 1, :, lanes].reshape(key_rows, HEAD_DIM)
        query = query_ref[:, :, lanes].reshape(query_rows, HEAD_DIM)
        scores = matmul(keys, query, NT) * EXP2_SCALE + bias
        top = jnp.maximum(jnp.max(scores, axis=0, keepdims=True), NEG_FLOOR)
        exponent = jnp.exp2(scores - top)
        total = jnp.sum(exponent, axis=0, keepdims=True)
        exponent_bf = exponent.astype(BF16)
        exp_ref[head] = exponent_bf
        safe = jnp.maximum(total, 1e-30)
        output = matmul(values, exponent_bf, TN) * (1.0 / safe)
        upstream = up_ref[:, :, lanes].reshape(query_rows, HEAD_DIM).astype(F32)
        rows.append(jnp.where(total > 0.0, top + jnp.log2(safe), NEG_FLOOR))
        rows.append(jnp.sum(upstream.T * output, axis=0, keepdims=True))
        tops.append(top)
        for part in range(per):
            out_ref[part, lanes, :] = output[
                :, part * slice_rows : (part + 1) * slice_rows
            ].astype(BF16)
    stats = jnp.concatenate(rows, axis=0)
    for copy in range(stat_ref.shape[0]):
        stat_ref[copy] = stats
    top_ref[...] = jnp.concatenate(tops, axis=0)


def forward(kv, query, upstream, bias):
    blocks, _, block_rows, width = kv.shape
    key_rows = blocks * block_rows
    slices, slice_rows, _ = query.shape
    queries = slices * slice_rows
    heads = width // HEAD_DIM
    step = 256
    per = step // slice_rows
    return pl.pallas_call(
        forward_kernel,
        grid=(queries // step,),
        in_specs=[
            pl.BlockSpec((blocks, 2, block_rows, width), lambda i: (0, 0, 0, 0)),
            pl.BlockSpec((per, slice_rows, width), lambda i: (i, 0, 0)),
            pl.BlockSpec((per, slice_rows, width), lambda i: (i, 0, 0)),
            pl.BlockSpec((key_rows, 128), lambda i: (0, 0)),
        ],
        out_specs=(
            pl.BlockSpec((heads, key_rows, step), lambda i: (0, 0, i)),
            pl.BlockSpec((per, width, slice_rows), lambda i: (i, 0, 0)),
            pl.BlockSpec((slices, 2 * heads, step), lambda i: (0, 0, i)),
            pl.BlockSpec((heads, step), lambda i: (0, i)),
        ),
        out_shape=(
            jax.ShapeDtypeStruct((heads, key_rows, queries), BF16),
            jax.ShapeDtypeStruct((slices, width, slice_rows), BF16),
            jax.ShapeDtypeStruct((slices, 2 * heads, queries), F32),
            jax.ShapeDtypeStruct((heads, queries), F32),
        ),
        compiler_params=params(48),
        cost_estimate=pl.CostEstimate(
            flops=4 * heads * queries * key_rows * HEAD_DIM,
            bytes_accessed=12 * MIB,
            transcendentals=heads * queries * key_rows,
        ),
    )(kv, query, upstream, bias)


def merged_stats(stats, head):
    logs = stats[:, 2 * head, :]
    deltas = stats[:, 2 * head + 1, :]
    top = jnp.max(logs, axis=0, keepdims=True)
    shares = jnp.exp2(logs - top)
    total = jnp.sum(shares, axis=0, keepdims=True)
    shares = shares / total
    return top + jnp.log2(total), shares, jnp.sum(deltas * shares, axis=0, keepdims=True)


def backward_kernel(
    spot_ref,
    kv_ref,
    query_ref,
    up_ref,
    exp_ref,
    stats_ref,
    own_ref,
    cos_block,
    sin_block,
    cos_row,
    sin_row,
    grad_ref,
    keep_ref,
    send_ref,
    acc_ref,
):
    step = pl.program_id(0)
    blocks, block_rows = kv_ref.shape[0], kv_ref.shape[2]
    key_rows = blocks * block_rows
    query_rows = query_ref.shape[0] * query_ref.shape[1]
    heads = kv_ref.shape[3] // HEAD_DIM
    stats = stats_ref[...]
    for head in range(heads):
        lanes = slice(head * HEAD_DIM, (head + 1) * HEAD_DIM)
        log_total, _, delta = merged_stats(stats, head)
        factor = jnp.exp2(own_ref[head : head + 1, :] - log_total)
        keys = kv_ref[:, 0, :, lanes].reshape(key_rows, HEAD_DIM)
        values = kv_ref[:, 1, :, lanes].reshape(key_rows, HEAD_DIM)
        query = query_ref[:, :, lanes].reshape(query_rows, HEAD_DIM)
        upstream = up_ref[:, :, lanes].reshape(query_rows, HEAD_DIM)
        probability = exp_ref[head].astype(F32) * factor
        value_grad = matmul(probability.astype(BF16), upstream)
        prob_grad = matmul(values, upstream, NT)
        score_grad = (probability * (prob_grad - delta)).astype(BF16)
        key_grad = matmul(score_grad, query) * SCALE
        query_part = matmul(keys, score_grad, TN)
        for block in range(blocks):
            part = key_grad[block * block_rows : (block + 1) * block_rows, :]
            cos_a = cos_block[block]
            sin_a = sin_block[block]
            cosine = cos_a * cos_row[...] - sin_a * sin_row[...]
            sine = sin_a * cos_row[...] + cos_a * sin_row[...]
            signed = jnp.where(
                lax.broadcasted_iota(jnp.int32, sine.shape, 1) < HEAD_DIM // 2, sine, -sine
            )
            turned = part * cosine + pltpu.roll(part, HEAD_DIM // 2, 1) * signed
            grad_ref[block, 0, :, lanes] = turned.astype(BF16)
            grad_ref[block, 1, :, lanes] = value_grad[
                block * block_rows : (block + 1) * block_rows, :
            ].astype(BF16)

        @pl.when(step == 0)
        def _():
            acc_ref[lanes, :] = query_part

        @pl.when(step > 0)
        def _():
            acc_ref[lanes, :] += query_part

    @pl.when(step == pl.num_programs(0) - 1)
    def _():
        half = keep_ref.shape[0]
        for slot in range(2 * half):
            first = pl.multiple_of(lax.bitwise_xor(spot_ref[0], PATH[slot]) * 128, 128)
            part = (acc_ref[:, pl.ds(first, 128)] * SCALE).astype(BF16)
            if slot < half:
                keep_ref[slot] = part
            else:
                send_ref[slot - half] = part


def backward(spot, kv, query, upstream, exponent, stats, own, tables):
    blocks, _, block_rows, width = kv.shape
    slices, slice_rows, _ = query.shape
    queries = slices * slice_rows
    heads = width // HEAD_DIM
    per = 4
    key_rows = blocks * block_rows
    whole = lambda shape: pl.BlockSpec(shape, lambda i, s: (0,) * len(shape))
    half = jax.ShapeDtypeStruct((slices // 2, width, slice_rows), BF16)
    return pl.pallas_call(
        backward_kernel,
        grid_spec=pltpu.PrefetchScalarGridSpec(
            num_scalar_prefetch=1,
            grid=(blocks // per,),
            in_specs=[
                pl.BlockSpec((per, 2, block_rows, width), lambda i, s: (i, 0, 0, 0)),
                whole(query.shape),
                whole(query.shape),
                pl.BlockSpec((heads, per * block_rows, queries), lambda i, s: (0, i, 0)),
                whole(stats.shape),
                whole(own.shape),
                pl.BlockSpec((per, 1, HEAD_DIM), lambda i, s: (i, 0, 0)),
                pl.BlockSpec((per, 1, HEAD_DIM), lambda i, s: (i, 0, 0)),
                whole((block_rows, HEAD_DIM)),
                whole((block_rows, HEAD_DIM)),
            ],
            out_specs=(
                pl.BlockSpec((per, 2, block_rows, width), lambda i, s: (i, 0, 0, 0)),
                whole(half.shape),
                whole(half.shape),
            ),
            scratch_shapes=[pltpu.VMEM((width, queries), F32)],
        ),
        out_shape=(jax.ShapeDtypeStruct((blocks, 2, block_rows, width), BF16), half, half),
        compiler_params=params(60),
        cost_estimate=pl.CostEstimate(
            flops=8 * heads * queries * key_rows * HEAD_DIM,
            bytes_accessed=14 * MIB,
            transcendentals=0,
        ),
    )(spot, kv, query, upstream, exponent, stats, own, *tables)


def merge_output(parts, stats):
    def kernel(parts_ref, stats_ref, out_ref):
        for head in range(parts_ref.shape[1] // HEAD_DIM):
            lanes = slice(head * HEAD_DIM, (head + 1) * HEAD_DIM)
            _, shares, _ = merged_stats(stats_ref[...], head)
            total = jnp.zeros((HEAD_DIM, parts_ref.shape[2]), F32)
            for block in range(parts_ref.shape[0]):
                total += parts_ref[block, lanes, :].astype(F32) * shares[block : block + 1, :]
            out_ref[lanes, :] = total.astype(BF16)

    return pl.pallas_call(
        kernel, out_shape=jax.ShapeDtypeStruct(parts.shape[1:], BF16), compiler_params=params(8)
    )(parts, stats)


def merge_query_grad(kept, arrived, cosine, sine):
    def kernel(kept_ref, arrived_ref, cos_ref, sin_ref, out_ref):
        total = kept_ref[0].astype(F32) + arrived_ref[0].astype(F32)
        half = HEAD_DIM // 2
        turned = []
        for head in range(total.shape[0] // HEAD_DIM):
            first = total[head * HEAD_DIM : head * HEAD_DIM + half, :]
            second = total[head * HEAD_DIM + half : (head + 1) * HEAD_DIM, :]
            turned.append(first * cos_ref[...] + second * sin_ref[...])
            turned.append(second * cos_ref[...] - first * sin_ref[...])
        out_ref[...] = jnp.concatenate(turned, axis=0).T.astype(BF16)

    return pl.pallas_call(
        kernel,
        out_shape=jax.ShapeDtypeStruct((kept.shape[2], kept.shape[1]), BF16),
        compiler_params=params(8),
    )(kept, arrived, cosine, sine)


def projection_grad(parts, cotangent):
    count, width, _ = parts.shape

    def kernel(parts_ref, cot_ref, out_ref):
        joined = jnp.concatenate([parts_ref[part] for part in range(count)], axis=1)
        out_ref[...] = matmul(joined, cot_ref[...]) * (1.0 / LOSS_SCALE)

    return pl.pallas_call(
        kernel,
        out_shape=jax.ShapeDtypeStruct((width, cotangent.shape[1]), F32),
        compiler_params=params(16),
    )(parts, cotangent)


def assemble(spot, near, far):
    count = 2 * near.shape[0]

    def kernel(spot_ref, near_ref, far_ref, out_ref):
        for slot in range(count):
            place = lax.bitwise_xor(spot_ref[0], PATH[slot])
            out_ref[place] = (near_ref if slot < count // 2 else far_ref)[slot % (count // 2)]

    vmem = pl.BlockSpec(memory_space=pltpu.VMEM)
    return pl.pallas_call(
        kernel,
        out_shape=jax.ShapeDtypeStruct((count,) + near.shape[1:], BF16),
        in_specs=[pl.BlockSpec(memory_space=pltpu.SMEM), vmem, vmem],
        out_specs=vmem,
        compiler_params=params(8),
    )(spot, near, far)


def upstream_part(spot, cotangent, out_weight, slices):
    slice_rows = cotangent.shape[0] // slices

    def kernel(spot_ref, cot_ref, weight_ref, keep_ref, send_ref):
        for slot in range(slices):
            first = pl.multiple_of(lax.bitwise_xor(spot_ref[0], PATH[slot]) * slice_rows, slice_rows)
            part = matmul(cot_ref[pl.ds(first, slice_rows), :], weight_ref[...], NT).astype(BF16)
            if slot < slices // 2:
                keep_ref[slot] = part
            else:
                send_ref[slot - slices // 2] = part

    vmem = pl.BlockSpec(memory_space=pltpu.VMEM)
    half = jax.ShapeDtypeStruct((slices // 2, slice_rows, out_weight.shape[0]), BF16)
    return pl.pallas_call(
        kernel,
        out_shape=(half, half),
        in_specs=[pl.BlockSpec(memory_space=pltpu.SMEM), vmem, vmem],
        out_specs=(vmem, vmem),
        compiler_params=params(16),
    )(spot, cotangent, out_weight)


def per_device(
    queries, key_vectors, value_vectors, cotangent, out_weight, frame_valid, group_offset, guide_index
):
    seq_count, fsdp_count = lax.axis_size("seq"), lax.axis_size("fsdp")
    fsdp_index = lax.axis_index("fsdp")
    block_rows = key_vectors.shape[1]
    group_rows, width = queries.shape[1], queries.shape[2]
    slice_rows = group_rows // fsdp_count
    tied = lax.optimization_barrier

    def over_seq(x):
        return lax.all_to_all(x, "seq", 0, 0, tiled=True)

    def over_fsdp(x):
        return lax.all_to_all(x, "fsdp", 0, 0, tiled=True)

    def partner(x, bit):
        return lax.ppermute(x, "fsdp", [(s, s ^ bit) for s in range(fsdp_count)])

    def halved(keep, send):
        for bit in (1, 2):
            total = (keep.astype(F32) + partner(send, bit).astype(F32)).astype(BF16)
            half = total.shape[0] // 2
            keep, send = total[:half], total[half:]
        return keep, partner(send, 4)

    def doubled(block):
        near = block[None]
        for bit in (4, 2):
            near = jnp.concatenate([near, partner(near, bit)])
        return assemble(spot, near, partner(near, 1))

    spot = fsdp_index.astype(jnp.int32)[None]
    guide = 1.5 + guide_index[0].astype(F32) / 1024.0
    own_weight = jnp.where(lax.axis_index("cfg") == 0, guide, 1.0 - guide)

    packed = pack_blocks(key_vectors, value_vectors, seq_count)
    packed, cotangent_after = tied((packed, cotangent))
    kv = over_seq(packed)

    keep, arrived = halved(*upstream_part(spot, cotangent_after, out_weight, fsdp_count))
    upstream = own_weight * (keep[0].astype(F32) + arrived[0].astype(F32))
    upstream = doubled(upstream.astype(BF16))
    query = queries.reshape(fsdp_count, slice_rows, width)

    block_ids = jnp.arange(seq_count, dtype=jnp.int32)
    block_start = (block_ids * fsdp_count + fsdp_index) * block_rows
    row_ids = jnp.arange(block_rows, dtype=jnp.int32)
    positions = (block_start[:, None] + row_ids[None, :]).reshape(-1)
    frame_match = (positions // FRAME_TOK)[:, None] == jnp.arange(
        frame_valid.shape[0], dtype=jnp.int32
    )[None, :]
    valid = jnp.sum(jnp.where(frame_match, frame_valid[None, :], 0), axis=1) == 1
    bias = jnp.broadcast_to(
        jnp.where(valid, 0.0, NEG_LARGE).astype(F32)[:, None], (positions.shape[0], 128)
    )
    frequency = 10000.0 ** (-jnp.arange(HEAD_DIM // 2, dtype=F32) / (HEAD_DIM // 2))
    twice = jnp.concatenate([frequency, frequency])
    block_angle = (block_start.astype(F32)[:, None] * twice[None, :])[:, None, :]
    row_angle = row_ids.astype(F32)[:, None] * twice[None, :]
    tables = (jnp.cos(block_angle), jnp.sin(block_angle), jnp.cos(row_angle), jnp.sin(row_angle))
    query_positions = (
        group_offset[0] + fsdp_index * slice_rows + jnp.arange(slice_rows, dtype=jnp.int32)
    )
    query_angle = query_positions.astype(F32)[None, :] * frequency[:, None]
    query_tables = (jnp.cos(query_angle), jnp.sin(query_angle))
    kv, upstream, bias, tables, query_tables = tied((kv, upstream, bias, tables, query_tables))

    exponent, out_parts, own_stats, own_top = forward(kv, query, upstream, bias)
    stats = over_fsdp(own_stats)
    stats, out_parts = tied((stats, out_parts))
    out_slices = over_fsdp(out_parts)
    grads, query_keep, query_send = backward(
        spot, kv, query, upstream, exponent, stats, own_top, tables
    )
    grads, out_slices, query_send = tied((grads, out_slices, query_send))
    key_grad, value_grad = unpack_blocks(over_seq(grads))

    query_slice = merge_query_grad(*halved(query_keep, query_send), *query_tables)
    query_grad = query_slice[None]

    slice_stats = lax.dynamic_slice_in_dim(stats, fsdp_index * slice_rows, slice_rows, axis=2)
    attn_rows = merge_output(out_slices, slice_stats)
    other_rows = lax.ppermute(attn_rows, "cfg", [(0, 1), (1, 0)])
    mixed = own_weight * attn_rows.astype(F32) + (1.0 - own_weight) * other_rows.astype(F32)
    weight_grad = projection_grad(doubled(mixed.astype(BF16)), cotangent)
    return (query_grad, key_grad, value_grad, weight_grad)


def solution(mesh):
    placed = (
        P("cfg", None, "seq"),
        P("cfg", ("seq", "fsdp"), None),
        P("cfg", ("seq", "fsdp"), None),
        P(None, "fsdp"),
        P("seq", "fsdp"),
        P(),
        P(),
        P(),
    )
    return jax.shard_map(
        per_device,
        mesh=mesh,
        in_specs=placed,
        out_specs=(
            P("cfg", "fsdp", "seq"),
            P("cfg", ("seq", "fsdp"), None),
            P("cfg", ("seq", "fsdp"), None),
            P("seq", "fsdp"),
        ),
        check_vma=False,
    )
```

```python
import math

import jax
import jax.numpy as jnp
from jax import lax
from jax.experimental import pallas as pl
from jax.experimental.pallas import tpu as pltpu
from jax.sharding import PartitionSpec as P

HEAD_DIM = 128
FRAME_TOK = 3600
NEG_LARGE = -1e30
NEG_FLOOR = -1e29
LOSS_SCALE = 128.0
SCALE = 1.0 / math.sqrt(HEAD_DIM)
EXP2_SCALE = SCALE * math.log2(math.e)
BF16 = jnp.bfloat16
F32 = jnp.float32
MIB = 1024 * 1024
GRANT = 44

PATH = (0, 1, 4, 5, 2, 3, 6, 7)
NT = (((1,), (1,)), ((), ()))
TN = (((0,), (0,)), ((), ()))


def matmul(a, b, dims=(((1,), (0,)), ((), ()))):
    return lax.dot_general(a, b, dims, preferred_element_type=F32)


def params(mib):
    return pltpu.CompilerParams(vmem_limit_bytes=mib * MIB)


def pack_blocks(keys, values, parts):
    rows, width = keys.shape[1], keys.shape[2] // parts
    per = 4

    def kernel(k_ref, v_ref, out_ref):
        for which, ref in enumerate((k_ref, v_ref)):
            for part in range(per):
                out_ref[part, which] = ref[0, :, part * width : (part + 1) * width]

    return pl.pallas_call(
        kernel,
        grid=(parts // per,),
        out_shape=pltpu.HBM((parts, 2, rows, width), keys.dtype),
        in_specs=[pl.BlockSpec((1, rows, per * width), lambda i: (0, 0, i))] * 2,
        out_specs=pl.BlockSpec((per, 2, rows, width), lambda i: (i, 0, 0, 0)),
        compiler_params=params(60),
    )(keys, values)


def unpack_blocks(packed):
    parts, _, rows, width = packed.shape
    per = 4

    def kernel(in_ref, k_ref, v_ref):
        for which, ref in enumerate((k_ref, v_ref)):
            for part in range(per):
                ref[0, :, part * width : (part + 1) * width] = in_ref[part, which]

    shape = jax.ShapeDtypeStruct((1, rows, parts * width), packed.dtype)
    return pl.pallas_call(
        kernel,
        grid=(parts // per,),
        out_shape=(shape, shape),
        in_specs=[pl.BlockSpec((per, 2, rows, width), lambda i: (i, 0, 0, 0))],
        out_specs=(pl.BlockSpec((1, rows, per * width), lambda i: (0, 0, i)),) * 2,
        compiler_params=params(16),
    )(packed)


def forward_kernel(kv_ref, query_ref, up_ref, bias_ref, exp_ref, out_ref, stat_ref, top_ref):
    key_rows = kv_ref.shape[0] * kv_ref.shape[2]
    per, slice_rows = query_ref.shape[0], query_ref.shape[1]
    query_rows = per * slice_rows
    heads = kv_ref.shape[3] // HEAD_DIM
    bias = jnp.concatenate([bias_ref[...]] * (query_rows // 128), axis=1)
    rows, tops = [], []
    for head in range(heads):
        lanes = slice(head * HEAD_DIM, (head + 1) * HEAD_DIM)
        keys = kv_ref[:, 0, :, lanes].reshape(key_rows, HEAD_DIM)
        values = kv_ref[:, 1, :, lanes].reshape(key_rows, HEAD_DIM)
        query = query_ref[:, :, lanes].reshape(query_rows, HEAD_DIM)
        scores = matmul(keys, query, NT) * EXP2_SCALE + bias
        top = jnp.maximum(jnp.max(scores, axis=0, keepdims=True), NEG_FLOOR)
        exponent = jnp.exp2(scores - top)
        total = jnp.sum(exponent, axis=0, keepdims=True)
        exponent_bf = exponent.astype(BF16)
        exp_ref[head] = exponent_bf
        safe = jnp.maximum(total, 1e-30)
        output = matmul(values, exponent_bf, TN) * (1.0 / safe)
        upstream = up_ref[:, :, lanes].reshape(query_rows, HEAD_DIM).astype(F32)
        rows.append(jnp.where(total > 0.0, top + jnp.log2(safe), NEG_FLOOR))
        rows.append(jnp.sum(upstream.T * output, axis=0, keepdims=True))
        tops.append(top)
        for part in range(per):
            out_ref[part, lanes, :] = output[
                :, part * slice_rows : (part + 1) * slice_rows
            ].astype(BF16)
    stats = jnp.concatenate(rows, axis=0)
    for copy in range(stat_ref.shape[0]):
        stat_ref[copy] = stats
    top_ref[...] = jnp.concatenate(tops, axis=0)


def forward(kv, query, upstream, bias):
    blocks, _, block_rows, width = kv.shape
    key_rows = blocks * block_rows
    slices, slice_rows, _ = query.shape
    queries = slices * slice_rows
    heads = width // HEAD_DIM
    step = 256
    per = step // slice_rows
    return pl.pallas_call(
        forward_kernel,
        grid=(queries // step,),
        in_specs=[
            pl.BlockSpec((blocks, 2, block_rows, width), lambda i: (0, 0, 0, 0)),
            pl.BlockSpec((per, slice_rows, width), lambda i: (i, 0, 0)),
            pl.BlockSpec((per, slice_rows, width), lambda i: (i, 0, 0)),
            pl.BlockSpec((key_rows, 128), lambda i: (0, 0)),
        ],
        out_specs=(
            pl.BlockSpec((heads, key_rows, step), lambda i: (0, 0, i)),
            pl.BlockSpec((per, width, slice_rows), lambda i: (i, 0, 0)),
            pl.BlockSpec((slices, 2 * heads, step), lambda i: (0, 0, i)),
            pl.BlockSpec((heads, step), lambda i: (0, i)),
        ),
        out_shape=(
            jax.ShapeDtypeStruct((heads, key_rows, queries), BF16),
            pltpu.HBM((slices, width, slice_rows), BF16),
            pltpu.HBM((slices, 2 * heads, queries), F32),
            jax.ShapeDtypeStruct((heads, queries), F32),
        ),
        compiler_params=params(GRANT),
        cost_estimate=pl.CostEstimate(
            flops=4 * heads * queries * key_rows * HEAD_DIM,
            bytes_accessed=12 * MIB,
            transcendentals=heads * queries * key_rows,
        ),
    )(kv, query, upstream, bias)


def merged_stats(stats, head):
    logs = stats[:, 2 * head, :]
    deltas = stats[:, 2 * head + 1, :]
    top = jnp.max(logs, axis=0, keepdims=True)
    shares = jnp.exp2(logs - top)
    total = jnp.sum(shares, axis=0, keepdims=True)
    shares = shares / total
    return top + jnp.log2(total), shares, jnp.sum(deltas * shares, axis=0, keepdims=True)


def backward_kernel(
    spot_ref,
    kv_ref,
    query_ref,
    up_ref,
    exp_ref,
    stats_ref,
    own_ref,
    cos_block,
    sin_block,
    cos_row,
    sin_row,
    grad_ref,
    keep_ref,
    send_ref,
    acc_ref,
):
    step = pl.program_id(0)
    blocks, block_rows = kv_ref.shape[0], kv_ref.shape[2]
    key_rows = blocks * block_rows
    query_rows = query_ref.shape[0] * query_ref.shape[1]
    heads = kv_ref.shape[3] // HEAD_DIM
    stats = stats_ref[...]
    for head in range(heads):
        lanes = slice(head * HEAD_DIM, (head + 1) * HEAD_DIM)
        log_total, _, delta = merged_stats(stats, head)
        factor = jnp.exp2(own_ref[head : head + 1, :] - log_total)
        keys = kv_ref[:, 0, :, lanes].reshape(key_rows, HEAD_DIM)
        values = kv_ref[:, 1, :, lanes].reshape(key_rows, HEAD_DIM)
        query = query_ref[:, :, lanes].reshape(query_rows, HEAD_DIM)
        upstream = up_ref[:, :, lanes].reshape(query_rows, HEAD_DIM)
        probability = exp_ref[head].astype(F32) * factor
        value_grad = matmul(probability.astype(BF16), upstream)
        prob_grad = matmul(values, upstream, NT)
        score_grad = (probability * (prob_grad - delta)).astype(BF16)
        key_grad = matmul(score_grad, query) * SCALE
        query_part = matmul(keys, score_grad, TN)
        for block in range(blocks):
            part = key_grad[block * block_rows : (block + 1) * block_rows, :]
            cos_a = cos_block[block]
            sin_a = sin_block[block]
            cosine = cos_a * cos_row[...] - sin_a * sin_row[...]
            sine = sin_a * cos_row[...] + cos_a * sin_row[...]
            signed = jnp.where(
                lax.broadcasted_iota(jnp.int32, sine.shape, 1) < HEAD_DIM // 2, sine, -sine
            )
            turned = part * cosine + pltpu.roll(part, HEAD_DIM // 2, 1) * signed
            grad_ref[block, 0, :, lanes] = turned.astype(BF16)
            grad_ref[block, 1, :, lanes] = value_grad[
                block * block_rows : (block + 1) * block_rows, :
            ].astype(BF16)

        @pl.when(step == 0)
        def _():
            acc_ref[lanes, :] = query_part

        @pl.when(step > 0)
        def _():
            acc_ref[lanes, :] += query_part

    @pl.when(step == pl.num_programs(0) - 1)
    def _():
        half = keep_ref.shape[0]
        for slot in range(2 * half):
            first = pl.multiple_of(lax.bitwise_xor(spot_ref[0], PATH[slot]) * 128, 128)
            part = (acc_ref[:, pl.ds(first, 128)] * SCALE).astype(BF16)
            if slot < half:
                keep_ref[slot] = part
            else:
                send_ref[slot - half] = part


def backward(spot, kv, query, upstream, exponent, stats, own, tables):
    blocks, _, block_rows, width = kv.shape
    slices, slice_rows, _ = query.shape
    queries = slices * slice_rows
    heads = width // HEAD_DIM
    per = 4
    key_rows = blocks * block_rows
    whole = lambda shape: pl.BlockSpec(shape, lambda i, s: (0,) * len(shape))
    half = pltpu.HBM((slices // 2, width, slice_rows), BF16)
    return pl.pallas_call(
        backward_kernel,
        grid_spec=pltpu.PrefetchScalarGridSpec(
            num_scalar_prefetch=1,
            grid=(blocks // per,),
            in_specs=[
                pl.BlockSpec((per, 2, block_rows, width), lambda i, s: (i, 0, 0, 0)),
                whole(query.shape),
                whole(query.shape),
                pl.BlockSpec((heads, per * block_rows, queries), lambda i, s: (0, i, 0)),
                whole(stats.shape),
                whole(own.shape),
                pl.BlockSpec((per, 1, HEAD_DIM), lambda i, s: (i, 0, 0)),
                pl.BlockSpec((per, 1, HEAD_DIM), lambda i, s: (i, 0, 0)),
                whole((block_rows, HEAD_DIM)),
                whole((block_rows, HEAD_DIM)),
            ],
            out_specs=(
                pl.BlockSpec((per, 2, block_rows, width), lambda i, s: (i, 0, 0, 0)),
                whole((slices // 2, width, slice_rows)),
                whole((slices // 2, width, slice_rows)),
            ),
            scratch_shapes=[pltpu.VMEM((width, queries), F32)],
        ),
        out_shape=(pltpu.HBM((blocks, 2, block_rows, width), BF16), half, half),
        compiler_params=params(GRANT),
        cost_estimate=pl.CostEstimate(
            flops=8 * heads * queries * key_rows * HEAD_DIM,
            bytes_accessed=14 * MIB,
            transcendentals=0,
        ),
    )(spot, kv, query, upstream, exponent, stats, own, *tables)


def merge_output(parts, stats):
    def kernel(parts_ref, stats_ref, out_ref):
        for head in range(parts_ref.shape[1] // HEAD_DIM):
            lanes = slice(head * HEAD_DIM, (head + 1) * HEAD_DIM)
            _, shares, _ = merged_stats(stats_ref[...], head)
            total = jnp.zeros((HEAD_DIM, parts_ref.shape[2]), F32)
            for block in range(parts_ref.shape[0]):
                total += parts_ref[block, lanes, :].astype(F32) * shares[block : block + 1, :]
            out_ref[lanes, :] = total.astype(BF16)

    return pl.pallas_call(
        kernel, out_shape=jax.ShapeDtypeStruct(parts.shape[1:], BF16), compiler_params=params(8)
    )(parts, stats)


def merge_query_grad(kept, arrived, cosine, sine):
    def kernel(kept_ref, arrived_ref, cos_ref, sin_ref, out_ref):
        total = kept_ref[0].astype(F32) + arrived_ref[0].astype(F32)
        half = HEAD_DIM // 2
        turned = []
        for head in range(total.shape[0] // HEAD_DIM):
            first = total[head * HEAD_DIM : head * HEAD_DIM + half, :]
            second = total[head * HEAD_DIM + half : (head + 1) * HEAD_DIM, :]
            turned.append(first * cos_ref[...] + second * sin_ref[...])
            turned.append(second * cos_ref[...] - first * sin_ref[...])
        out_ref[...] = jnp.concatenate(turned, axis=0).T.astype(BF16)

    return pl.pallas_call(
        kernel,
        out_shape=jax.ShapeDtypeStruct((kept.shape[2], kept.shape[1]), BF16),
        compiler_params=params(8),
    )(kept, arrived, cosine, sine)


def projection_grad(parts, cotangent):
    count, width, _ = parts.shape

    def kernel(parts_ref, cot_ref, out_ref):
        joined = jnp.concatenate([parts_ref[part] for part in range(count)], axis=1)
        out_ref[...] = matmul(joined, cot_ref[...]) * (1.0 / LOSS_SCALE)

    return pl.pallas_call(
        kernel,
        out_shape=jax.ShapeDtypeStruct((width, cotangent.shape[1]), F32),
        compiler_params=params(16),
    )(parts, cotangent)


def assemble(spot, near, far):
    count = 2 * near.shape[0]

    def kernel(spot_ref, near_ref, far_ref, out_ref):
        for slot in range(count):
            place = lax.bitwise_xor(spot_ref[0], PATH[slot])
            out_ref[place] = (near_ref if slot < count // 2 else far_ref)[slot % (count // 2)]

    vmem = pl.BlockSpec(memory_space=pltpu.VMEM)
    return pl.pallas_call(
        kernel,
        out_shape=pltpu.HBM((count,) + near.shape[1:], BF16),
        in_specs=[pl.BlockSpec(memory_space=pltpu.SMEM), vmem, vmem],
        out_specs=vmem,
        compiler_params=params(8),
    )(spot, near, far)


def upstream_part(spot, cotangent, out_weight, slices):
    slice_rows = cotangent.shape[0] // slices

    def kernel(spot_ref, cot_ref, weight_ref, keep_ref, send_ref):
        for slot in range(slices):
            first = pl.multiple_of(lax.bitwise_xor(spot_ref[0], PATH[slot]) * slice_rows, slice_rows)
            part = matmul(cot_ref[pl.ds(first, slice_rows), :], weight_ref[...], NT).astype(BF16)
            if slot < slices // 2:
                keep_ref[slot] = part
            else:
                send_ref[slot - slices // 2] = part

    vmem = pl.BlockSpec(memory_space=pltpu.VMEM)
    half = jax.ShapeDtypeStruct((slices // 2, slice_rows, out_weight.shape[0]), BF16)
    return pl.pallas_call(
        kernel,
        out_shape=(half, half),
        in_specs=[pl.BlockSpec(memory_space=pltpu.SMEM), vmem, vmem],
        out_specs=(vmem, vmem),
        compiler_params=params(16),
    )(spot, cotangent, out_weight)


def per_device(
    queries, key_vectors, value_vectors, cotangent, out_weight, frame_valid, group_offset, guide_index
):
    seq_count, fsdp_count = lax.axis_size("seq"), lax.axis_size("fsdp")
    fsdp_index = lax.axis_index("fsdp")
    block_rows = key_vectors.shape[1]
    group_rows, width = queries.shape[1], queries.shape[2]
    slice_rows = group_rows // fsdp_count
    tied = lax.optimization_barrier

    def over_seq(x):
        return lax.all_to_all(x, "seq", 0, 0, tiled=True)

    def over_fsdp(x):
        return lax.all_to_all(x, "fsdp", 0, 0, tiled=True)

    def partner(x, bit):
        return lax.ppermute(x, "fsdp", [(s, s ^ bit) for s in range(fsdp_count)])

    def halved(keep, send):
        for bit in (2, 4):
            total = (keep.astype(F32) + partner(send, bit).astype(F32)).astype(BF16)
            half = total.shape[0] // 2
            keep, send = total[:half], total[half:]
        return keep, partner(send, 1)

    def doubled(block):
        near = block[None]
        for bit in (1, 4):
            near = jnp.concatenate([near, partner(near, bit)])
        return assemble(spot, near, partner(near, 2))

    spot = fsdp_index.astype(jnp.int32)[None]
    guide = 1.5 + guide_index[0].astype(F32) / 1024.0
    own_weight = jnp.where(lax.axis_index("cfg") == 0, guide, 1.0 - guide)

    packed = pack_blocks(key_vectors, value_vectors, seq_count)
    packed, cotangent_after = tied((packed, cotangent))
    kv = over_seq(packed)

    keep, arrived = halved(*upstream_part(spot, cotangent_after, out_weight, fsdp_count))
    upstream = own_weight * (keep[0].astype(F32) + arrived[0].astype(F32))
    query = queries.reshape(fsdp_count, slice_rows, width)

    block_ids = jnp.arange(seq_count, dtype=jnp.int32)
    block_start = (block_ids * fsdp_count + fsdp_index) * block_rows
    row_ids = jnp.arange(block_rows, dtype=jnp.int32)
    positions = (block_start[:, None] + row_ids[None, :]).reshape(-1)
    frame_match = (positions // FRAME_TOK)[:, None] == jnp.arange(
        frame_valid.shape[0], dtype=jnp.int32
    )[None, :]
    valid = jnp.sum(jnp.where(frame_match, frame_valid[None, :], 0), axis=1) == 1
    bias = jnp.broadcast_to(
        jnp.where(valid, 0.0, NEG_LARGE).astype(F32)[:, None], (positions.shape[0], 128)
    )
    frequency = 10000.0 ** (-jnp.arange(HEAD_DIM // 2, dtype=F32) / (HEAD_DIM // 2))
    twice = jnp.concatenate([frequency, frequency])
    block_angle = (block_start.astype(F32)[:, None] * twice[None, :])[:, None, :]
    row_angle = row_ids.astype(F32)[:, None] * twice[None, :]
    tables = (jnp.cos(block_angle), jnp.sin(block_angle), jnp.cos(row_angle), jnp.sin(row_angle))
    query_positions = (
        group_offset[0] + fsdp_index * slice_rows + jnp.arange(slice_rows, dtype=jnp.int32)
    )
    query_angle = query_positions.astype(F32)[None, :] * frequency[:, None]
    query_tables = (jnp.cos(query_angle), jnp.sin(query_angle))
    upstream, bias, tables, query_tables = tied(
        (upstream.astype(BF16), bias, tables, query_tables)
    )
    upstream = doubled(upstream)

    exponent, out_parts, own_stats, own_top = forward(kv, query, upstream, bias)
    stats = over_fsdp(own_stats)
    stats, out_parts = tied((stats, out_parts))
    out_slices = over_fsdp(out_parts)
    grads, query_keep, query_send = backward(
        spot, kv, query, upstream, exponent, stats, own_top, tables
    )
    grads, out_slices, query_send = tied((grads, out_slices, query_send))
    key_grad, value_grad = unpack_blocks(over_seq(grads))

    query_slice = merge_query_grad(*halved(query_keep, query_send), *query_tables)
    query_grad = query_slice[None]

    slice_stats = lax.dynamic_slice_in_dim(stats, fsdp_index * slice_rows, slice_rows, axis=2)
    attn_rows = merge_output(out_slices, slice_stats)
    other_rows = lax.ppermute(attn_rows, "cfg", [(0, 1), (1, 0)])
    mixed = own_weight * attn_rows.astype(F32) + (1.0 - own_weight) * other_rows.astype(F32)
    weight_grad = projection_grad(doubled(mixed.astype(BF16)), cotangent)
    return (query_grad, key_grad, value_grad, weight_grad)


def solution(mesh):
    placed = (
        P("cfg", None, "seq"),
        P("cfg", ("seq", "fsdp"), None),
        P("cfg", ("seq", "fsdp"), None),
        P(None, "fsdp"),
        P("seq", "fsdp"),
        P(),
        P(),
        P(),
    )
    return jax.shard_map(
        per_device,
        mesh=mesh,
        in_specs=placed,
        out_specs=(
            P("cfg", "fsdp", "seq"),
            P("cfg", ("seq", "fsdp"), None),
            P("cfg", ("seq", "fsdp"), None),
            P("seq", "fsdp"),
        ),
        check_vma=False,
    )
```

```python
import math

import jax
import jax.numpy as jnp
from jax import lax
from jax.experimental import pallas as pl
from jax.experimental.pallas import tpu as pltpu
from jax.sharding import PartitionSpec as P

HEAD_DIM = 128
FRAME_TOK = 3600
NEG_LARGE = -1e30
NEG_FLOOR = -1e29
LOSS_SCALE = 128.0
SCALE = 1.0 / math.sqrt(HEAD_DIM)
EXP2_SCALE = SCALE * math.log2(math.e)
BF16 = jnp.bfloat16
F32 = jnp.float32
MIB = 1024 * 1024

HALVING = (0, 1, 4, 5, 2, 3, 6, 7)
DOUBLING = (0, 4, 2, 6, 1, 5, 3, 7)
NT = (((1,), (1,)), ((), ()))
TN = (((0,), (0,)), ((), ()))


def matmul(a, b, dims=(((1,), (0,)), ((), ()))):
    return lax.dot_general(a, b, dims, preferred_element_type=F32)


def params(mib):
    return pltpu.CompilerParams(vmem_limit_bytes=mib * MIB)


def pack_blocks(keys, values, parts):
    rows, width = keys.shape[1], keys.shape[2] // parts
    per = 4

    def kernel(k_ref, v_ref, out_ref):
        for which, ref in enumerate((k_ref, v_ref)):
            for part in range(per):
                out_ref[part, which] = ref[0, :, part * width : (part + 1) * width]

    return pl.pallas_call(
        kernel,
        grid=(parts // per,),
        out_shape=pltpu.HBM((parts, 2, rows, width), keys.dtype),
        in_specs=[pl.BlockSpec((1, rows, per * width), lambda i: (0, 0, i))] * 2,
        out_specs=pl.BlockSpec((per, 2, rows, width), lambda i: (i, 0, 0, 0)),
        compiler_params=params(60),
    )(keys, values)


def unpack_blocks(packed):
    parts, _, rows, width = packed.shape
    per = 4

    def kernel(in_ref, k_ref, v_ref):
        for which, ref in enumerate((k_ref, v_ref)):
            for part in range(per):
                ref[0, :, part * width : (part + 1) * width] = in_ref[part, which]

    shape = jax.ShapeDtypeStruct((1, rows, parts * width), packed.dtype)
    return pl.pallas_call(
        kernel,
        grid=(parts // per,),
        out_shape=(shape, shape),
        in_specs=[pl.BlockSpec((per, 2, rows, width), lambda i: (i, 0, 0, 0))],
        out_specs=(pl.BlockSpec((1, rows, per * width), lambda i: (0, 0, i)),) * 2,
        compiler_params=params(16),
    )(packed)


def forward_kernel(kv_ref, query_ref, up_ref, bias_ref, exp_ref, out_ref, stat_ref, top_ref):
    key_rows = kv_ref.shape[0] * kv_ref.shape[2]
    per, slice_rows = query_ref.shape[0], query_ref.shape[1]
    query_rows = per * slice_rows
    heads = kv_ref.shape[3] // HEAD_DIM
    bias = jnp.concatenate([bias_ref[...]] * (query_rows // 128), axis=1)
    rows, tops = [], []
    for head in range(heads):
        lanes = slice(head * HEAD_DIM, (head + 1) * HEAD_DIM)
        keys = kv_ref[:, 0, :, lanes].reshape(key_rows, HEAD_DIM)
        values = kv_ref[:, 1, :, lanes].reshape(key_rows, HEAD_DIM)
        query = query_ref[:, :, lanes].reshape(query_rows, HEAD_DIM)
        scores = matmul(keys, query, NT) * EXP2_SCALE + bias
        top = jnp.maximum(jnp.max(scores, axis=0, keepdims=True), NEG_FLOOR)
        exponent = jnp.exp2(scores - top)
        total = jnp.sum(exponent, axis=0, keepdims=True)
        exponent_bf = exponent.astype(BF16)
        exp_ref[head] = exponent_bf
        safe = jnp.maximum(total, 1e-30)
        output = matmul(values, exponent_bf, TN) * (1.0 / safe)
        upstream = up_ref[:, :, lanes].reshape(query_rows, HEAD_DIM).astype(F32)
        rows.append(jnp.where(total > 0.0, top + jnp.log2(safe), NEG_FLOOR))
        rows.append(jnp.sum(upstream.T * output, axis=0, keepdims=True))
        tops.append(top)
        for part in range(per):
            out_ref[part, lanes, :] = output[
                :, part * slice_rows : (part + 1) * slice_rows
            ].astype(BF16)
    stats = jnp.concatenate(rows, axis=0)
    for copy in range(stat_ref.shape[0]):
        stat_ref[copy] = stats
    top_ref[...] = jnp.concatenate(tops, axis=0)


def forward(kv, query, upstream, bias):
    blocks, _, block_rows, width = kv.shape
    key_rows = blocks * block_rows
    slices, slice_rows, _ = query.shape
    queries = slices * slice_rows
    heads = width // HEAD_DIM
    step = 256
    per = step // slice_rows
    return pl.pallas_call(
        forward_kernel,
        grid=(queries // step,),
        in_specs=[
            pl.BlockSpec((blocks, 2, block_rows, width), lambda i: (0, 0, 0, 0)),
            pl.BlockSpec((per, slice_rows, width), lambda i: (i, 0, 0)),
            pl.BlockSpec((per, slice_rows, width), lambda i: (i, 0, 0)),
            pl.BlockSpec((key_rows, 128), lambda i: (0, 0)),
        ],
        out_specs=(
            pl.BlockSpec((heads, key_rows, step), lambda i: (0, 0, i)),
            pl.BlockSpec((per, width, slice_rows), lambda i: (i, 0, 0)),
            pl.BlockSpec((slices, 2 * heads, step), lambda i: (0, 0, i)),
            pl.BlockSpec((heads, step), lambda i: (0, i)),
        ),
        out_shape=(
            jax.ShapeDtypeStruct((heads, key_rows, queries), BF16),
            pltpu.HBM((slices, width, slice_rows), BF16),
            pltpu.HBM((slices, 2 * heads, queries), F32),
            jax.ShapeDtypeStruct((heads, queries), F32),
        ),
        compiler_params=pltpu.CompilerParams(vmem_limit_bytes=61_300_000),
        cost_estimate=pl.CostEstimate(
            flops=4 * heads * queries * key_rows * HEAD_DIM,
            bytes_accessed=12 * MIB,
            transcendentals=heads * queries * key_rows,
        ),
    )(kv, query, upstream, bias)


def merged_stats(stats, head):
    logs = stats[:, 2 * head, :]
    deltas = stats[:, 2 * head + 1, :]
    top = jnp.max(logs, axis=0, keepdims=True)
    shares = jnp.exp2(logs - top)
    total = jnp.sum(shares, axis=0, keepdims=True)
    return top + jnp.log2(total), jnp.sum(deltas * shares, axis=0, keepdims=True) / total


def backward_kernel(
    spot_ref,
    kv_ref,
    query_ref,
    up_ref,
    exp_ref,
    stats_ref,
    log_ref,
    own_ref,
    parts_ref,
    cos_block,
    sin_block,
    cos_row,
    sin_row,
    grad_ref,
    keep_ref,
    send_ref,
    acc_ref,
):
    step = pl.program_id(0)
    blocks, block_rows = kv_ref.shape[0], kv_ref.shape[2]
    key_rows = blocks * block_rows
    query_rows = query_ref.shape[0] * query_ref.shape[1]
    heads = kv_ref.shape[3] // HEAD_DIM
    stats = stats_ref[...]
    for head in range(heads):
        lanes = slice(head * HEAD_DIM, (head + 1) * HEAD_DIM)
        log_total, delta = merged_stats(stats, head)
        factor = jnp.exp2(own_ref[head : head + 1, :] - log_total)
        keys = kv_ref[:, 0, :, lanes].reshape(key_rows, HEAD_DIM)
        values = kv_ref[:, 1, :, lanes].reshape(key_rows, HEAD_DIM)
        query = query_ref[:, :, lanes].reshape(query_rows, HEAD_DIM)
        upstream = up_ref[:, :, lanes].reshape(query_rows, HEAD_DIM)
        probability = exp_ref[head].astype(F32) * factor
        value_grad = matmul(probability.astype(BF16), upstream)
        prob_grad = matmul(values, upstream, NT)
        score_grad = (probability * (prob_grad - delta)).astype(BF16)
        key_grad = matmul(score_grad, query) * SCALE
        query_part = matmul(keys, score_grad, TN)
        for block in range(blocks):
            part = key_grad[block * block_rows : (block + 1) * block_rows, :]
            cos_a = cos_block[block]
            sin_a = sin_block[block]
            cosine = cos_a * cos_row[...] - sin_a * sin_row[...]
            sine = sin_a * cos_row[...] + cos_a * sin_row[...]
            signed = jnp.where(
                lax.broadcasted_iota(jnp.int32, sine.shape, 1) < HEAD_DIM // 2, sine, -sine
            )
            turned = part * cosine + pltpu.roll(part, HEAD_DIM // 2, 1) * signed
            grad_ref[block, 0, :, lanes] = turned.astype(BF16)
            grad_ref[block, 1, :, lanes] = value_grad[
                block * block_rows : (block + 1) * block_rows, :
            ].astype(BF16)

        @pl.when(step == 0)
        def _():
            acc_ref[lanes, :] = query_part

        @pl.when(step > 0)
        def _():
            acc_ref[lanes, :] += query_part

    @pl.when(step == pl.num_programs(0) - 1)
    def _():
        half = keep_ref.shape[0]
        for slot in range(2 * half):
            place = lax.bitwise_xor(spot_ref[0], HALVING[slot])
            spread = pl.ds(pl.multiple_of(place * 128, 128), 128)
            query_part = (acc_ref[:, spread] * SCALE).astype(BF16)
            part = parts_ref[place].astype(F32)
            weighted = []
            for head in range(heads):
                log_total, _ = merged_stats(stats_ref[:, :, spread], head)
                share = jnp.exp2(log_ref[0, 2 * head : 2 * head + 1, spread] - log_total)
                weighted.append(part[head * HEAD_DIM : (head + 1) * HEAD_DIM, :] * share)
            ref = keep_ref if slot < half else send_ref
            width = query_part.shape[0]
            ref[slot % half, :width] = jnp.concatenate(weighted, axis=0).astype(BF16)
            ref[slot % half, width:] = query_part


def backward(spot, kv, query, upstream, exponent, stats, own_stats, own_top, out_parts, tables):
    blocks, _, block_rows, width = kv.shape
    slices, slice_rows, _ = query.shape
    queries = slices * slice_rows
    heads = width // HEAD_DIM
    per = 4
    key_rows = blocks * block_rows
    whole = lambda shape: pl.BlockSpec(shape, lambda i, s: (0,) * len(shape))
    half = pltpu.HBM((slices // 2, 2 * width, slice_rows), BF16)
    return pl.pallas_call(
        backward_kernel,
        grid_spec=pltpu.PrefetchScalarGridSpec(
            num_scalar_prefetch=1,
            grid=(blocks // per,),
            in_specs=[
                pl.BlockSpec((per, 2, block_rows, width), lambda i, s: (i, 0, 0, 0)),
                whole(query.shape),
                whole(query.shape),
                pl.BlockSpec((heads, per * block_rows, queries), lambda i, s: (0, i, 0)),
                whole(stats.shape),
                whole((1,) + own_stats.shape[1:]),
                whole(own_top.shape),
                whole(out_parts.shape),
                pl.BlockSpec((per, 1, HEAD_DIM), lambda i, s: (i, 0, 0)),
                pl.BlockSpec((per, 1, HEAD_DIM), lambda i, s: (i, 0, 0)),
                whole((block_rows, HEAD_DIM)),
                whole((block_rows, HEAD_DIM)),
            ],
            out_specs=(
                pl.BlockSpec((per, 2, block_rows, width), lambda i, s: (i, 0, 0, 0)),
            )
            + (whole((slices // 2, 2 * width, slice_rows)),) * 2,
            scratch_shapes=[pltpu.VMEM((width, queries), F32)],
        ),
        out_shape=(pltpu.HBM((blocks, 2, block_rows, width), BF16), half, half),
        compiler_params=params(60),
        cost_estimate=pl.CostEstimate(
            flops=8 * heads * queries * key_rows * HEAD_DIM,
            bytes_accessed=14 * MIB,
            transcendentals=0,
        ),
    )(spot, kv, query, upstream, exponent, stats, own_stats, own_top, out_parts, *tables)


def merge_query_grad(kept, arrived, cosine, sine):
    width = kept.shape[1] // 2

    def kernel(kept_ref, arrived_ref, cos_ref, sin_ref, out_ref):
        total = kept_ref[0, width:].astype(F32) + arrived_ref[0, width:].astype(F32)
        half = HEAD_DIM // 2
        turned = []
        for head in range(total.shape[0] // HEAD_DIM):
            first = total[head * HEAD_DIM : head * HEAD_DIM + half, :]
            second = total[head * HEAD_DIM + half : (head + 1) * HEAD_DIM, :]
            turned.append(first * cos_ref[...] + second * sin_ref[...])
            turned.append(second * cos_ref[...] - first * sin_ref[...])
        out_ref[...] = jnp.concatenate(turned, axis=0).T.astype(BF16)

    return pl.pallas_call(
        kernel,
        out_shape=jax.ShapeDtypeStruct((kept.shape[2], width), BF16),
        compiler_params=params(8),
    )(kept, arrived, cosine, sine)


def projection_grad(parts, cotangent):
    count, width, _ = parts.shape

    def kernel(parts_ref, cot_ref, out_ref):
        joined = jnp.concatenate([parts_ref[part] for part in range(count)], axis=1)
        out_ref[...] = matmul(joined, cot_ref[...]) * (1.0 / LOSS_SCALE)

    return pl.pallas_call(
        kernel,
        out_shape=jax.ShapeDtypeStruct((width, cotangent.shape[1]), F32),
        compiler_params=params(16),
    )(parts, cotangent)


def assemble(spot, near, far):
    count = 2 * near.shape[0]

    def kernel(spot_ref, near_ref, far_ref, out_ref):
        for slot in range(count):
            place = lax.bitwise_xor(spot_ref[0], DOUBLING[slot])
            out_ref[place] = (near_ref if slot < count // 2 else far_ref)[slot % (count // 2)]

    vmem = pl.BlockSpec(memory_space=pltpu.VMEM)
    return pl.pallas_call(
        kernel,
        out_shape=pltpu.HBM((count,) + near.shape[1:], BF16),
        in_specs=[pl.BlockSpec(memory_space=pltpu.SMEM), vmem, vmem],
        out_specs=vmem,
        compiler_params=params(8),
    )(spot, near, far)


def upstream_part(spot, cotangent, out_weight, slices):
    slice_rows = cotangent.shape[0] // slices

    def kernel(spot_ref, cot_ref, weight_ref, keep_ref, send_ref):
        for slot in range(slices):
            first = pl.multiple_of(lax.bitwise_xor(spot_ref[0], HALVING[slot]) * slice_rows, slice_rows)
            part = matmul(cot_ref[pl.ds(first, slice_rows), :], weight_ref[...], NT).astype(BF16)
            if slot < slices // 2:
                keep_ref[slot] = part
            else:
                send_ref[slot - slices // 2] = part

    vmem = pl.BlockSpec(memory_space=pltpu.VMEM)
    half = jax.ShapeDtypeStruct((slices // 2, slice_rows, out_weight.shape[0]), BF16)
    return pl.pallas_call(
        kernel,
        out_shape=(half, half),
        in_specs=[pl.BlockSpec(memory_space=pltpu.SMEM), vmem, vmem],
        out_specs=(vmem, vmem),
        compiler_params=params(16),
    )(spot, cotangent, out_weight)


def per_device(
    queries, key_vectors, value_vectors, cotangent, out_weight, frame_valid, group_offset, guide_index
):
    seq_count, fsdp_count = lax.axis_size("seq"), lax.axis_size("fsdp")
    fsdp_index = lax.axis_index("fsdp")
    block_rows = key_vectors.shape[1]
    group_rows, width = queries.shape[1], queries.shape[2]
    slice_rows = group_rows // fsdp_count
    tied = lax.optimization_barrier

    def over_seq(x):
        return lax.all_to_all(x, "seq", 0, 0, tiled=True)

    def over_fsdp(x):
        return lax.all_to_all(x, "fsdp", 0, 0, tiled=True)

    def partner(x, bit):
        return lax.ppermute(x, "fsdp", [(s, s ^ bit) for s in range(fsdp_count)])

    def halved(keep, send):
        for bit in (2, 4):
            total = (keep.astype(F32) + partner(send, bit).astype(F32)).astype(BF16)
            half = total.shape[0] // 2
            keep, send = total[:half], total[half:]
        return keep, partner(send, 1)

    def doubled(block):
        near = block[None]
        for bit in (4, 2):
            near = jnp.concatenate([near, partner(near, bit)])
        return assemble(spot, near, partner(near, 1))

    spot = fsdp_index.astype(jnp.int32)[None]
    guide = 1.5 + guide_index[0].astype(F32) / 1024.0
    own_weight = jnp.where(lax.axis_index("cfg") == 0, guide, 1.0 - guide)

    packed = pack_blocks(key_vectors, value_vectors, seq_count)
    packed, cotangent_after = tied((packed, cotangent))
    kv = over_seq(packed)

    keep, arrived = halved(*upstream_part(spot, cotangent_after, out_weight, fsdp_count))
    upstream = own_weight * (keep[0].astype(F32) + arrived[0].astype(F32))
    query = queries.reshape(fsdp_count, slice_rows, width)

    block_ids = jnp.arange(seq_count, dtype=jnp.int32)
    block_start = (block_ids * fsdp_count + fsdp_index) * block_rows
    row_ids = jnp.arange(block_rows, dtype=jnp.int32)
    positions = (block_start[:, None] + row_ids[None, :]).reshape(-1)
    frame_match = (positions // FRAME_TOK)[:, None] == jnp.arange(
        frame_valid.shape[0], dtype=jnp.int32
    )[None, :]
    valid = jnp.sum(jnp.where(frame_match, frame_valid[None, :], 0), axis=1) == 1
    bias = jnp.broadcast_to(
        jnp.where(valid, 0.0, NEG_LARGE).astype(F32)[:, None], (positions.shape[0], 128)
    )
    frequency = 10000.0 ** (-jnp.arange(HEAD_DIM // 2, dtype=F32) / (HEAD_DIM // 2))
    twice = jnp.concatenate([frequency, frequency])
    block_angle = (block_start.astype(F32)[:, None] * twice[None, :])[:, None, :]
    row_angle = row_ids.astype(F32)[:, None] * twice[None, :]
    tables = (jnp.cos(block_angle), jnp.sin(block_angle), jnp.cos(row_angle), jnp.sin(row_angle))
    query_positions = (
        group_offset[0] + fsdp_index * slice_rows + jnp.arange(slice_rows, dtype=jnp.int32)
    )
    query_angle = query_positions.astype(F32)[None, :] * frequency[:, None]
    query_tables = (jnp.cos(query_angle), jnp.sin(query_angle))
    upstream, bias, tables, query_tables = tied(
        (upstream.astype(BF16), bias, tables, query_tables)
    )
    upstream = doubled(upstream)

    exponent, out_parts, own_stats, own_top = forward(kv, query, upstream, bias)
    stats = over_fsdp(own_stats)
    grads, keep, send = backward(
        spot, kv, query, upstream, exponent, stats, own_stats, own_top, out_parts, tables
    )
    key_grad, value_grad = unpack_blocks(over_seq(grads))

    keep, arrived = halved(keep, send)
    query_grad = merge_query_grad(keep, arrived, *query_tables)[None]
    attn_rows = keep[0, :width].astype(F32) + arrived[0, :width].astype(F32)
    attn_rows = attn_rows.astype(BF16)
    other_rows = lax.ppermute(attn_rows, "cfg", [(0, 1), (1, 0)])
    mixed = own_weight * attn_rows.astype(F32) + (1.0 - own_weight) * other_rows.astype(F32)
    weight_grad = projection_grad(doubled(mixed.astype(BF16)), cotangent)
    return (query_grad, key_grad, value_grad, weight_grad)


def solution(mesh):
    placed = (
        P("cfg", None, "seq"),
        P("cfg", ("seq", "fsdp"), None),
        P("cfg", ("seq", "fsdp"), None),
        P(None, "fsdp"),
        P("seq", "fsdp"),
        P(),
        P(),
        P(),
    )
    return jax.shard_map(
        per_device,
        mesh=mesh,
        in_specs=placed,
        out_specs=(
            P("cfg", "fsdp", "seq"),
            P("cfg", ("seq", "fsdp"), None),
            P("cfg", ("seq", "fsdp"), None),
            P("seq", "fsdp"),
        ),
        check_vma=False,
    )
```

```python
import math

import jax
import jax.numpy as jnp
from jax import lax
from jax.experimental import pallas as pl
from jax.experimental.pallas import tpu as pltpu
from jax.sharding import PartitionSpec as P

HEAD_DIM = 128
FRAME_TOK = 3600
NEG_LARGE = -1e30
NEG_FLOOR = -1e29
LOSS_SCALE = 128.0
SCALE = 1.0 / math.sqrt(HEAD_DIM)
EXP2_SCALE = SCALE * math.log2(math.e)
BF16 = jnp.bfloat16
F32 = jnp.float32
MIB = 1024 * 1024

HALVING = (0, 1, 4, 5, 2, 3, 6, 7)
DOUBLING = (0, 4, 2, 6, 1, 5, 3, 7)
NT = (((1,), (1,)), ((), ()))
TN = (((0,), (0,)), ((), ()))


def matmul(a, b, dims=(((1,), (0,)), ((), ()))):
    return lax.dot_general(a, b, dims, preferred_element_type=F32)


def params(mib):
    return pltpu.CompilerParams(vmem_limit_bytes=mib * MIB)


def pack_blocks(keys, values, parts):
    rows, width = keys.shape[1], keys.shape[2] // parts
    per = 4

    def kernel(k_ref, v_ref, out_ref):
        for which, ref in enumerate((k_ref, v_ref)):
            for part in range(per):
                out_ref[part, which] = ref[0, :, part * width : (part + 1) * width]

    return pl.pallas_call(
        kernel,
        grid=(parts // per,),
        out_shape=pltpu.HBM((parts, 2, rows, width), keys.dtype),
        in_specs=[pl.BlockSpec((1, rows, per * width), lambda i: (0, 0, i))] * 2,
        out_specs=pl.BlockSpec((per, 2, rows, width), lambda i: (i, 0, 0, 0)),
        compiler_params=params(60),
    )(keys, values)


def unpack_blocks(packed):
    parts, _, rows, width = packed.shape
    per = 4

    def kernel(in_ref, k_ref, v_ref):
        for which, ref in enumerate((k_ref, v_ref)):
            for part in range(per):
                ref[0, :, part * width : (part + 1) * width] = in_ref[part, which]

    shape = jax.ShapeDtypeStruct((1, rows, parts * width), packed.dtype)
    return pl.pallas_call(
        kernel,
        grid=(parts // per,),
        out_shape=(shape, shape),
        in_specs=[pl.BlockSpec((per, 2, rows, width), lambda i: (i, 0, 0, 0))],
        out_specs=(pl.BlockSpec((1, rows, per * width), lambda i: (0, 0, i)),) * 2,
        compiler_params=params(16),
    )(packed)


def forward_kernel(kv_ref, query_ref, up_ref, bias_ref, exp_ref, out_ref, stat_ref, top_ref):
    key_rows = kv_ref.shape[0] * kv_ref.shape[2]
    per, slice_rows = query_ref.shape[0], query_ref.shape[1]
    query_rows = per * slice_rows
    heads = kv_ref.shape[3] // HEAD_DIM
    bias = jnp.concatenate([bias_ref[...]] * (query_rows // 128), axis=1)
    rows, tops = [], []
    for head in range(heads):
        lanes = slice(head * HEAD_DIM, (head + 1) * HEAD_DIM)
        keys = kv_ref[:, 0, :, lanes].reshape(key_rows, HEAD_DIM)
        values = kv_ref[:, 1, :, lanes].reshape(key_rows, HEAD_DIM)
        query = query_ref[:, :, lanes].reshape(query_rows, HEAD_DIM)
        scores = matmul(keys, query, NT) * EXP2_SCALE + bias
        top = jnp.maximum(jnp.max(scores, axis=0, keepdims=True), NEG_FLOOR)
        exponent = jnp.exp2(scores - top)
        total = jnp.sum(exponent, axis=0, keepdims=True)
        exponent_bf = exponent.astype(BF16)
        exp_ref[head] = exponent_bf
        safe = jnp.maximum(total, 1e-30)
        output = matmul(values, exponent_bf, TN) * (1.0 / safe)
        upstream = up_ref[:, :, lanes].reshape(query_rows, HEAD_DIM).astype(F32)
        rows.append(jnp.where(total > 0.0, top + jnp.log2(safe), NEG_FLOOR))
        rows.append(jnp.sum(upstream.T * output, axis=0, keepdims=True))
        tops.append(top)
        for part in range(per):
            out_ref[part, lanes, :] = output[
                :, part * slice_rows : (part + 1) * slice_rows
            ].astype(BF16)
    stats = jnp.concatenate(rows, axis=0)
    for copy in range(stat_ref.shape[0]):
        stat_ref[copy] = stats
    top_ref[...] = jnp.concatenate(tops, axis=0)


def forward(kv, query, upstream, bias):
    blocks, _, block_rows, width = kv.shape
    key_rows = blocks * block_rows
    slices, slice_rows, _ = query.shape
    queries = slices * slice_rows
    heads = width // HEAD_DIM
    step = 256
    per = step // slice_rows
    return pl.pallas_call(
        forward_kernel,
        grid=(queries // step,),
        in_specs=[
            pl.BlockSpec((blocks, 2, block_rows, width), lambda i: (0, 0, 0, 0)),
            pl.BlockSpec((per, slice_rows, width), lambda i: (i, 0, 0)),
            pl.BlockSpec((per, slice_rows, width), lambda i: (i, 0, 0)),
            pl.BlockSpec((key_rows, 128), lambda i: (0, 0)),
        ],
        out_specs=(
            pl.BlockSpec((heads, key_rows, step), lambda i: (0, 0, i)),
            pl.BlockSpec((per, width, slice_rows), lambda i: (i, 0, 0)),
            pl.BlockSpec((slices, 2 * heads, step), lambda i: (0, 0, i)),
            pl.BlockSpec((heads, step), lambda i: (0, i)),
        ),
        out_shape=(
            jax.ShapeDtypeStruct((heads, key_rows, queries), BF16),
            pltpu.HBM((slices, width, slice_rows), BF16),
            pltpu.HBM((slices, 2 * heads, queries), F32),
            jax.ShapeDtypeStruct((heads, queries), F32),
        ),
        compiler_params=pltpu.CompilerParams(vmem_limit_bytes=61_300_000),
        cost_estimate=pl.CostEstimate(
            flops=4 * heads * queries * key_rows * HEAD_DIM,
            bytes_accessed=12 * MIB,
            transcendentals=heads * queries * key_rows,
        ),
    )(kv, query, upstream, bias)


def merged_stats(stats, head):
    logs = stats[:, 2 * head, :]
    deltas = stats[:, 2 * head + 1, :]
    top = jnp.max(logs, axis=0, keepdims=True)
    shares = jnp.exp2(logs - top)
    total = jnp.sum(shares, axis=0, keepdims=True)
    return top + jnp.log2(total), jnp.sum(deltas * shares, axis=0, keepdims=True) / total


def backward_kernel(
    spot_ref,
    kv_ref,
    query_ref,
    up_ref,
    exp_ref,
    stats_ref,
    log_ref,
    own_ref,
    parts_ref,
    cos_block,
    sin_block,
    cos_row,
    sin_row,
    grad_ref,
    keep_ref,
    send_ref,
    out_keep_ref,
    out_send_ref,
    acc_ref,
):
    step = pl.program_id(0)
    blocks, block_rows = kv_ref.shape[0], kv_ref.shape[2]
    key_rows = blocks * block_rows
    query_rows = query_ref.shape[0] * query_ref.shape[1]
    heads = kv_ref.shape[3] // HEAD_DIM
    stats = stats_ref[...]
    for head in range(heads):
        lanes = slice(head * HEAD_DIM, (head + 1) * HEAD_DIM)
        log_total, delta = merged_stats(stats, head)
        factor = jnp.exp2(own_ref[head : head + 1, :] - log_total)
        keys = kv_ref[:, 0, :, lanes].reshape(key_rows, HEAD_DIM)
        values = kv_ref[:, 1, :, lanes].reshape(key_rows, HEAD_DIM)
        query = query_ref[:, :, lanes].reshape(query_rows, HEAD_DIM)
        upstream = up_ref[:, :, lanes].reshape(query_rows, HEAD_DIM)
        probability = exp_ref[head].astype(F32) * factor
        value_grad = matmul(probability.astype(BF16), upstream)
        prob_grad = matmul(values, upstream, NT)
        score_grad = (probability * (prob_grad - delta)).astype(BF16)
        key_grad = matmul(score_grad, query) * SCALE
        query_part = matmul(keys, score_grad, TN)
        for block in range(blocks):
            part = key_grad[block * block_rows : (block + 1) * block_rows, :]
            cos_a = cos_block[block]
            sin_a = sin_block[block]
            cosine = cos_a * cos_row[...] - sin_a * sin_row[...]
            sine = sin_a * cos_row[...] + cos_a * sin_row[...]
            signed = jnp.where(
                lax.broadcasted_iota(jnp.int32, sine.shape, 1) < HEAD_DIM // 2, sine, -sine
            )
            turned = part * cosine + pltpu.roll(part, HEAD_DIM // 2, 1) * signed
            grad_ref[block, 0, :, lanes] = turned.astype(BF16)
            grad_ref[block, 1, :, lanes] = value_grad[
                block * block_rows : (block + 1) * block_rows, :
            ].astype(BF16)

        @pl.when(step == 0)
        def _():
            acc_ref[lanes, :] = query_part

        @pl.when(step > 0)
        def _():
            acc_ref[lanes, :] += query_part

    @pl.when(step == pl.num_programs(0) - 1)
    def _():
        half = keep_ref.shape[0]
        for slot in range(2 * half):
            place = lax.bitwise_xor(spot_ref[0], HALVING[slot])
            spread = pl.ds(pl.multiple_of(place * 128, 128), 128)
            query_part = (acc_ref[:, spread] * SCALE).astype(BF16)
            part = parts_ref[place].astype(F32)
            weighted = []
            for head in range(heads):
                log_total, _ = merged_stats(stats_ref[:, :, spread], head)
                share = jnp.exp2(log_ref[0, 2 * head : 2 * head + 1, spread] - log_total)
                weighted.append(part[head * HEAD_DIM : (head + 1) * HEAD_DIM, :] * share)
            out_part = jnp.concatenate(weighted, axis=0).astype(BF16)
            if slot < half:
                keep_ref[slot] = query_part
                out_keep_ref[slot] = out_part
            else:
                send_ref[slot - half] = query_part
                out_send_ref[slot - half] = out_part


def backward(spot, kv, query, upstream, exponent, stats, own_stats, own_top, out_parts, tables):
    blocks, _, block_rows, width = kv.shape
    slices, slice_rows, _ = query.shape
    queries = slices * slice_rows
    heads = width // HEAD_DIM
    per = 4
    key_rows = blocks * block_rows
    whole = lambda shape: pl.BlockSpec(shape, lambda i, s: (0,) * len(shape))
    half = pltpu.HBM((slices // 2, width, slice_rows), BF16)
    return pl.pallas_call(
        backward_kernel,
        grid_spec=pltpu.PrefetchScalarGridSpec(
            num_scalar_prefetch=1,
            grid=(blocks // per,),
            in_specs=[
                pl.BlockSpec((per, 2, block_rows, width), lambda i, s: (i, 0, 0, 0)),
                whole(query.shape),
                whole(query.shape),
                pl.BlockSpec((heads, per * block_rows, queries), lambda i, s: (0, i, 0)),
                whole(stats.shape),
                whole((1,) + own_stats.shape[1:]),
                whole(own_top.shape),
                whole(out_parts.shape),
                pl.BlockSpec((per, 1, HEAD_DIM), lambda i, s: (i, 0, 0)),
                pl.BlockSpec((per, 1, HEAD_DIM), lambda i, s: (i, 0, 0)),
                whole((block_rows, HEAD_DIM)),
                whole((block_rows, HEAD_DIM)),
            ],
            out_specs=(
                pl.BlockSpec((per, 2, block_rows, width), lambda i, s: (i, 0, 0, 0)),
            )
            + (whole((slices // 2, width, slice_rows)),) * 4,
            scratch_shapes=[pltpu.VMEM((width, queries), F32)],
        ),
        out_shape=(pltpu.HBM((blocks, 2, block_rows, width), BF16), half, half, half, half),
        compiler_params=params(60),
        cost_estimate=pl.CostEstimate(
            flops=8 * heads * queries * key_rows * HEAD_DIM,
            bytes_accessed=14 * MIB,
            transcendentals=0,
        ),
    )(spot, kv, query, upstream, exponent, stats, own_stats, own_top, out_parts, *tables)


def merge_query_grad(kept, arrived, cosine, sine):
    def kernel(kept_ref, arrived_ref, cos_ref, sin_ref, out_ref):
        total = kept_ref[0].astype(F32) + arrived_ref[0].astype(F32)
        half = HEAD_DIM // 2
        turned = []
        for head in range(total.shape[0] // HEAD_DIM):
            first = total[head * HEAD_DIM : head * HEAD_DIM + half, :]
            second = total[head * HEAD_DIM + half : (head + 1) * HEAD_DIM, :]
            turned.append(first * cos_ref[...] + second * sin_ref[...])
            turned.append(second * cos_ref[...] - first * sin_ref[...])
        out_ref[...] = jnp.concatenate(turned, axis=0).T.astype(BF16)

    return pl.pallas_call(
        kernel,
        out_shape=jax.ShapeDtypeStruct((kept.shape[2], kept.shape[1]), BF16),
        compiler_params=params(8),
    )(kept, arrived, cosine, sine)


def projection_grad(spot, near, far, cotangent):
    half, width, _ = near.shape

    def kernel(spot_ref, near_ref, far_ref, cot_ref, out_ref, joined_ref):
        for slot in range(2 * half):
            first = pl.multiple_of(lax.bitwise_xor(spot_ref[0], DOUBLING[slot]) * 128, 128)
            ref = near_ref if slot < half else far_ref
            joined_ref[:, pl.ds(first, 128)] = ref[slot % half]
        out_ref[...] = matmul(joined_ref[...], cot_ref[...]) * (1.0 / LOSS_SCALE)

    vmem = pl.BlockSpec(memory_space=pltpu.VMEM)
    return pl.pallas_call(
        kernel,
        out_shape=jax.ShapeDtypeStruct((width, cotangent.shape[1]), F32),
        in_specs=[pl.BlockSpec(memory_space=pltpu.SMEM), vmem, vmem, vmem],
        out_specs=vmem,
        scratch_shapes=[pltpu.VMEM((width, 2 * half * 128), BF16)],
        compiler_params=params(16),
    )(spot, near, far, cotangent)


def assemble(spot, near, far):
    count = 2 * near.shape[0]

    def kernel(spot_ref, near_ref, far_ref, out_ref):
        for slot in range(count):
            place = lax.bitwise_xor(spot_ref[0], DOUBLING[slot])
            out_ref[place] = (near_ref if slot < count // 2 else far_ref)[slot % (count // 2)]

    vmem = pl.BlockSpec(memory_space=pltpu.VMEM)
    return pl.pallas_call(
        kernel,
        out_shape=pltpu.HBM((count,) + near.shape[1:], BF16),
        in_specs=[pl.BlockSpec(memory_space=pltpu.SMEM), vmem, vmem],
        out_specs=vmem,
        compiler_params=params(8),
    )(spot, near, far)


def upstream_part(spot, cotangent, out_weight, slices):
    slice_rows = cotangent.shape[0] // slices

    def kernel(spot_ref, cot_ref, weight_ref, keep_ref, send_ref):
        for slot in range(slices):
            first = pl.multiple_of(lax.bitwise_xor(spot_ref[0], HALVING[slot]) * slice_rows, slice_rows)
            part = matmul(cot_ref[pl.ds(first, slice_rows), :], weight_ref[...], NT).astype(BF16)
            if slot < slices // 2:
                keep_ref[slot] = part
            else:
                send_ref[slot - slices // 2] = part

    vmem = pl.BlockSpec(memory_space=pltpu.VMEM)
    half = jax.ShapeDtypeStruct((slices // 2, slice_rows, out_weight.shape[0]), BF16)
    return pl.pallas_call(
        kernel,
        out_shape=(half, half),
        in_specs=[pl.BlockSpec(memory_space=pltpu.SMEM), vmem, vmem],
        out_specs=(vmem, vmem),
        compiler_params=params(16),
    )(spot, cotangent, out_weight)


def per_device(
    queries, key_vectors, value_vectors, cotangent, out_weight, frame_valid, group_offset, guide_index
):
    seq_count, fsdp_count = lax.axis_size("seq"), lax.axis_size("fsdp")
    fsdp_index = lax.axis_index("fsdp")
    block_rows = key_vectors.shape[1]
    group_rows, width = queries.shape[1], queries.shape[2]
    slice_rows = group_rows // fsdp_count
    tied = lax.optimization_barrier

    def over_seq(x):
        return lax.all_to_all(x, "seq", 0, 0, tiled=True)

    def over_fsdp(x):
        return lax.all_to_all(x, "fsdp", 0, 0, tiled=True)

    def partner(x, bit):
        return lax.ppermute(x, "fsdp", [(s, s ^ bit) for s in range(fsdp_count)])

    def halved(keep, send):
        for bit in (2, 4):
            total = (keep.astype(F32) + partner(send, bit).astype(F32)).astype(BF16)
            half = total.shape[0] // 2
            keep, send = total[:half], total[half:]
        return keep, partner(send, 1)

    def doubled(block):
        near = block[None]
        for bit in (4, 2):
            near = jnp.concatenate([near, partner(near, bit)])
        return near, partner(near, 1)

    spot = fsdp_index.astype(jnp.int32)[None]
    guide = 1.5 + guide_index[0].astype(F32) / 1024.0
    own_weight = jnp.where(lax.axis_index("cfg") == 0, guide, 1.0 - guide)

    packed = pack_blocks(key_vectors, value_vectors, seq_count)
    packed, cotangent_after = tied((packed, cotangent))
    kv = over_seq(packed)

    keep, arrived = halved(*upstream_part(spot, cotangent_after, out_weight, fsdp_count))
    upstream = own_weight * (keep[0].astype(F32) + arrived[0].astype(F32))
    query = queries.reshape(fsdp_count, slice_rows, width)

    block_ids = jnp.arange(seq_count, dtype=jnp.int32)
    block_start = (block_ids * fsdp_count + fsdp_index) * block_rows
    row_ids = jnp.arange(block_rows, dtype=jnp.int32)
    positions = (block_start[:, None] + row_ids[None, :]).reshape(-1)
    frame_match = (positions // FRAME_TOK)[:, None] == jnp.arange(
        frame_valid.shape[0], dtype=jnp.int32
    )[None, :]
    valid = jnp.sum(jnp.where(frame_match, frame_valid[None, :], 0), axis=1) == 1
    bias = jnp.broadcast_to(
        jnp.where(valid, 0.0, NEG_LARGE).astype(F32)[:, None], (positions.shape[0], 128)
    )
    frequency = 10000.0 ** (-jnp.arange(HEAD_DIM // 2, dtype=F32) / (HEAD_DIM // 2))
    twice = jnp.concatenate([frequency, frequency])
    block_angle = (block_start.astype(F32)[:, None] * twice[None, :])[:, None, :]
    row_angle = row_ids.astype(F32)[:, None] * twice[None, :]
    tables = (jnp.cos(block_angle), jnp.sin(block_angle), jnp.cos(row_angle), jnp.sin(row_angle))
    query_positions = (
        group_offset[0] + fsdp_index * slice_rows + jnp.arange(slice_rows, dtype=jnp.int32)
    )
    query_angle = query_positions.astype(F32)[None, :] * frequency[:, None]
    query_tables = (jnp.cos(query_angle), jnp.sin(query_angle))
    upstream, bias, tables = tied((upstream.astype(BF16), bias, tables))
    upstream = assemble(spot, *doubled(upstream))

    exponent, out_parts, own_stats, own_top = forward(kv, query, upstream, bias)
    stats = over_fsdp(own_stats)
    grads, query_keep, query_send, out_keep, out_send = backward(
        spot, kv, query, upstream, exponent, stats, own_stats, own_top, out_parts, tables
    )
    key_grad, value_grad = unpack_blocks(over_seq(grads))

    query_slice = merge_query_grad(*halved(query_keep, query_send), *query_tables)
    query_grad = query_slice[None]

    out_keep, arrived = halved(out_keep, out_send)
    attn_rows = (out_keep[0].astype(F32) + arrived[0].astype(F32)).astype(BF16)
    other_rows = lax.ppermute(attn_rows, "cfg", [(0, 1), (1, 0)])
    mixed = own_weight * attn_rows.astype(F32) + (1.0 - own_weight) * other_rows.astype(F32)
    weight_grad = projection_grad(spot, *doubled(mixed.astype(BF16)), cotangent)
    return (query_grad, key_grad, value_grad, weight_grad)


def solution(mesh):
    placed = (
        P("cfg", None, "seq"),
        P("cfg", ("seq", "fsdp"), None),
        P("cfg", ("seq", "fsdp"), None),
        P(None, "fsdp"),
        P("seq", "fsdp"),
        P(),
        P(),
        P(),
    )
    return jax.shard_map(
        per_device,
        mesh=mesh,
        in_specs=placed,
        out_specs=(
            P("cfg", "fsdp", "seq"),
            P("cfg", ("seq", "fsdp"), None),
            P("cfg", ("seq", "fsdp"), None),
            P("seq", "fsdp"),
        ),
        check_vma=False,
    )
```

```python
import math

import jax
import jax.numpy as jnp
from jax import lax
from jax.experimental import pallas as pl
from jax.experimental.pallas import tpu as pltpu
from jax.sharding import PartitionSpec as P

HEAD_DIM = 128
FRAME_TOK = 3600
NEG_LARGE = -1e30
NEG_FLOOR = -1e29
LOSS_SCALE = 128.0
SCALE = 1.0 / math.sqrt(HEAD_DIM)
EXP2_SCALE = SCALE * math.log2(math.e)
BF16 = jnp.bfloat16
F32 = jnp.float32
MIB = 1024 * 1024

HALVING = (0, 1, 4, 5, 2, 3, 6, 7)
DOUBLING = (0, 4, 2, 6, 1, 5, 3, 7)
NT = (((1,), (1,)), ((), ()))
TN = (((0,), (0,)), ((), ()))


def matmul(a, b, dims=(((1,), (0,)), ((), ()))):
    return lax.dot_general(a, b, dims, preferred_element_type=F32)


def params(mib):
    return pltpu.CompilerParams(vmem_limit_bytes=mib * MIB)


def pack_blocks(keys, values, parts):
    rows, width = keys.shape[1], keys.shape[2] // parts
    per = 4

    def kernel(k_ref, v_ref, out_ref):
        for which, ref in enumerate((k_ref, v_ref)):
            for part in range(per):
                out_ref[part, which] = ref[0, :, part * width : (part + 1) * width]

    return pl.pallas_call(
        kernel,
        grid=(parts // per,),
        out_shape=pltpu.HBM((parts, 2, rows, width), keys.dtype),
        in_specs=[pl.BlockSpec((1, rows, per * width), lambda i: (0, 0, i))] * 2,
        out_specs=pl.BlockSpec((per, 2, rows, width), lambda i: (i, 0, 0, 0)),
        compiler_params=params(60),
    )(keys, values)


def unpack_blocks(packed):
    parts, _, rows, width = packed.shape
    per = 4

    def kernel(in_ref, k_ref, v_ref):
        for which, ref in enumerate((k_ref, v_ref)):
            for part in range(per):
                ref[0, :, part * width : (part + 1) * width] = in_ref[part, which]

    shape = jax.ShapeDtypeStruct((1, rows, parts * width), packed.dtype)
    return pl.pallas_call(
        kernel,
        grid=(parts // per,),
        out_shape=(shape, shape),
        in_specs=[pl.BlockSpec((per, 2, rows, width), lambda i: (i, 0, 0, 0))],
        out_specs=(pl.BlockSpec((1, rows, per * width), lambda i: (0, 0, i)),) * 2,
        compiler_params=params(16),
    )(packed)


def forward_kernel(kv_ref, query_ref, up_ref, bias_ref, exp_ref, out_ref, stat_ref, top_ref):
    key_rows = kv_ref.shape[0] * kv_ref.shape[2]
    per, slice_rows = query_ref.shape[0], query_ref.shape[1]
    query_rows = per * slice_rows
    heads = kv_ref.shape[3] // HEAD_DIM
    bias = jnp.concatenate([bias_ref[...]] * (query_rows // 128), axis=1)
    rows, tops = [], []
    for head in range(heads):
        lanes = slice(head * HEAD_DIM, (head + 1) * HEAD_DIM)
        keys = kv_ref[:, 0, :, lanes].reshape(key_rows, HEAD_DIM)
        values = kv_ref[:, 1, :, lanes].reshape(key_rows, HEAD_DIM)
        query = query_ref[:, :, lanes].reshape(query_rows, HEAD_DIM)
        scores = matmul(keys, query, NT) * EXP2_SCALE + bias
        top = jnp.maximum(jnp.max(scores, axis=0, keepdims=True), NEG_FLOOR)
        exponent = jnp.exp2(scores - top)
        total = jnp.sum(exponent, axis=0, keepdims=True)
        exponent_bf = exponent.astype(BF16)
        exp_ref[head] = exponent_bf
        safe = jnp.maximum(total, 1e-30)
        output = matmul(values, exponent_bf, TN) * (1.0 / safe)
        upstream = up_ref[:, :, lanes].reshape(query_rows, HEAD_DIM).astype(F32)
        rows.append(jnp.where(total > 0.0, top + jnp.log2(safe), NEG_FLOOR))
        rows.append(jnp.sum(upstream.T * output, axis=0, keepdims=True))
        tops.append(top)
        for part in range(per):
            out_ref[part, lanes, :] = output[
                :, part * slice_rows : (part + 1) * slice_rows
            ].astype(BF16)
    stats = jnp.concatenate(rows, axis=0)
    for copy in range(stat_ref.shape[0]):
        stat_ref[copy] = stats
    top_ref[...] = jnp.concatenate(tops, axis=0)


def forward(kv, query, upstream, bias):
    blocks, _, block_rows, width = kv.shape
    key_rows = blocks * block_rows
    slices, slice_rows, _ = query.shape
    queries = slices * slice_rows
    heads = width // HEAD_DIM
    step = 512
    per = step // slice_rows
    return pl.pallas_call(
        forward_kernel,
        grid=(queries // step,),
        in_specs=[
            pl.BlockSpec((blocks, 2, block_rows, width), lambda i: (0, 0, 0, 0)),
            pl.BlockSpec((per, slice_rows, width), lambda i: (i, 0, 0)),
            pl.BlockSpec((per, slice_rows, width), lambda i: (i, 0, 0)),
            pl.BlockSpec((key_rows, 128), lambda i: (0, 0)),
        ],
        out_specs=(
            pl.BlockSpec((heads, key_rows, step), lambda i: (0, 0, i)),
            pl.BlockSpec((per, width, slice_rows), lambda i: (i, 0, 0)),
            pl.BlockSpec((slices, 2 * heads, step), lambda i: (0, 0, i)),
            pl.BlockSpec((heads, step), lambda i: (0, i)),
        ),
        out_shape=(
            jax.ShapeDtypeStruct((heads, key_rows, queries), BF16),
            pltpu.HBM((slices, width, slice_rows), BF16),
            pltpu.HBM((slices, 2 * heads, queries), F32),
            jax.ShapeDtypeStruct((heads, queries), F32),
        ),
        compiler_params=pltpu.CompilerParams(vmem_limit_bytes=61_300_000),
        cost_estimate=pl.CostEstimate(
            flops=4 * heads * queries * key_rows * HEAD_DIM,
            bytes_accessed=12 * MIB,
            transcendentals=heads * queries * key_rows,
        ),
    )(kv, query, upstream, bias)


def merged_stats(stats, head):
    logs = stats[:, 2 * head, :]
    deltas = stats[:, 2 * head + 1, :]
    top = jnp.max(logs, axis=0, keepdims=True)
    shares = jnp.exp2(logs - top)
    total = jnp.sum(shares, axis=0, keepdims=True)
    return top + jnp.log2(total), jnp.sum(deltas * shares, axis=0, keepdims=True) / total


def backward_kernel(
    spot_ref,
    kv_ref,
    query_ref,
    up_ref,
    exp_ref,
    stats_ref,
    log_ref,
    own_ref,
    parts_ref,
    cos_block,
    sin_block,
    cos_row,
    sin_row,
    grad_ref,
    keep_ref,
    send_ref,
    out_keep_ref,
    out_send_ref,
    acc_ref,
):
    step = pl.program_id(0)
    blocks, block_rows = kv_ref.shape[0], kv_ref.shape[2]
    key_rows = blocks * block_rows
    query_rows = query_ref.shape[0] * query_ref.shape[1]
    heads = kv_ref.shape[3] // HEAD_DIM
    stats = stats_ref[...]
    for head in range(heads):
        lanes = slice(head * HEAD_DIM, (head + 1) * HEAD_DIM)
        log_total, delta = merged_stats(stats, head)
        factor = jnp.exp2(own_ref[head : head + 1, :] - log_total)
        keys = kv_ref[:, 0, :, lanes].reshape(key_rows, HEAD_DIM)
        values = kv_ref[:, 1, :, lanes].reshape(key_rows, HEAD_DIM)
        query = query_ref[:, :, lanes].reshape(query_rows, HEAD_DIM)
        upstream = up_ref[:, :, lanes].reshape(query_rows, HEAD_DIM)
        probability = exp_ref[head].astype(F32) * factor
        value_grad = matmul(probability.astype(BF16), upstream)
        prob_grad = matmul(values, upstream, NT)
        score_grad = (probability * (prob_grad - delta)).astype(BF16)
        key_grad = matmul(score_grad, query) * SCALE
        query_part = matmul(keys, score_grad, TN)
        for block in range(blocks):
            part = key_grad[block * block_rows : (block + 1) * block_rows, :]
            cos_a = cos_block[block]
            sin_a = sin_block[block]
            cosine = cos_a * cos_row[...] - sin_a * sin_row[...]
            sine = sin_a * cos_row[...] + cos_a * sin_row[...]
            signed = jnp.where(
                lax.broadcasted_iota(jnp.int32, sine.shape, 1) < HEAD_DIM // 2, sine, -sine
            )
            turned = part * cosine + pltpu.roll(part, HEAD_DIM // 2, 1) * signed
            grad_ref[block, 0, :, lanes] = turned.astype(BF16)
            grad_ref[block, 1, :, lanes] = value_grad[
                block * block_rows : (block + 1) * block_rows, :
            ].astype(BF16)

        @pl.when(step == 0)
        def _():
            acc_ref[lanes, :] = query_part

        @pl.when(step > 0)
        def _():
            acc_ref[lanes, :] += query_part

    @pl.when(step == pl.num_programs(0) - 1)
    def _():
        half = keep_ref.shape[0]
        for slot in range(2 * half):
            place = lax.bitwise_xor(spot_ref[0], HALVING[slot])
            spread = pl.ds(pl.multiple_of(place * 128, 128), 128)
            query_part = (acc_ref[:, spread] * SCALE).astype(BF16)
            part = parts_ref[place].astype(F32)
            weighted = []
            for head in range(heads):
                log_total, _ = merged_stats(stats_ref[:, :, spread], head)
                share = jnp.exp2(log_ref[0, 2 * head : 2 * head + 1, spread] - log_total)
                weighted.append(part[head * HEAD_DIM : (head + 1) * HEAD_DIM, :] * share)
            out_part = jnp.concatenate(weighted, axis=0).astype(BF16)
            if slot < half:
                keep_ref[slot] = query_part
                out_keep_ref[slot] = out_part
            else:
                send_ref[slot - half] = query_part
                out_send_ref[slot - half] = out_part


def backward(spot, kv, query, upstream, exponent, stats, own_stats, own_top, out_parts, tables):
    blocks, _, block_rows, width = kv.shape
    slices, slice_rows, _ = query.shape
    queries = slices * slice_rows
    heads = width // HEAD_DIM
    per = 4
    key_rows = blocks * block_rows
    whole = lambda shape: pl.BlockSpec(shape, lambda i, s: (0,) * len(shape))
    half = pltpu.HBM((slices // 2, width, slice_rows), BF16)
    return pl.pallas_call(
        backward_kernel,
        grid_spec=pltpu.PrefetchScalarGridSpec(
            num_scalar_prefetch=1,
            grid=(blocks // per,),
            in_specs=[
                pl.BlockSpec((per, 2, block_rows, width), lambda i, s: (i, 0, 0, 0)),
                whole(query.shape),
                whole(query.shape),
                pl.BlockSpec((heads, per * block_rows, queries), lambda i, s: (0, i, 0)),
                whole(stats.shape),
                whole((1,) + own_stats.shape[1:]),
                whole(own_top.shape),
                whole(out_parts.shape),
                pl.BlockSpec((per, 1, HEAD_DIM), lambda i, s: (i, 0, 0)),
                pl.BlockSpec((per, 1, HEAD_DIM), lambda i, s: (i, 0, 0)),
                whole((block_rows, HEAD_DIM)),
                whole((block_rows, HEAD_DIM)),
            ],
            out_specs=(
                pl.BlockSpec((per, 2, block_rows, width), lambda i, s: (i, 0, 0, 0)),
            )
            + (whole((slices // 2, width, slice_rows)),) * 4,
            scratch_shapes=[pltpu.VMEM((width, queries), F32)],
        ),
        out_shape=(pltpu.HBM((blocks, 2, block_rows, width), BF16), half, half, half, half),
        compiler_params=params(60),
        cost_estimate=pl.CostEstimate(
            flops=8 * heads * queries * key_rows * HEAD_DIM,
            bytes_accessed=14 * MIB,
            transcendentals=0,
        ),
    )(spot, kv, query, upstream, exponent, stats, own_stats, own_top, out_parts, *tables)


def merge_query_grad(kept, arrived, cosine, sine):
    def kernel(kept_ref, arrived_ref, cos_ref, sin_ref, out_ref):
        total = kept_ref[0].astype(F32) + arrived_ref[0].astype(F32)
        half = HEAD_DIM // 2
        turned = []
        for head in range(total.shape[0] // HEAD_DIM):
            first = total[head * HEAD_DIM : head * HEAD_DIM + half, :]
            second = total[head * HEAD_DIM + half : (head + 1) * HEAD_DIM, :]
            turned.append(first * cos_ref[...] + second * sin_ref[...])
            turned.append(second * cos_ref[...] - first * sin_ref[...])
        out_ref[...] = jnp.concatenate(turned, axis=0).T.astype(BF16)

    return pl.pallas_call(
        kernel,
        out_shape=jax.ShapeDtypeStruct((kept.shape[2], kept.shape[1]), BF16),
        compiler_params=params(8),
    )(kept, arrived, cosine, sine)


def projection_grad(spot, near, far, cotangent):
    half, width, _ = near.shape

    def kernel(spot_ref, near_ref, far_ref, cot_ref, out_ref, joined_ref):
        for slot in range(2 * half):
            first = pl.multiple_of(lax.bitwise_xor(spot_ref[0], DOUBLING[slot]) * 128, 128)
            ref = near_ref if slot < half else far_ref
            joined_ref[:, pl.ds(first, 128)] = ref[slot % half]
        out_ref[...] = matmul(joined_ref[...], cot_ref[...]) * (1.0 / LOSS_SCALE)

    vmem = pl.BlockSpec(memory_space=pltpu.VMEM)
    return pl.pallas_call(
        kernel,
        out_shape=jax.ShapeDtypeStruct((width, cotangent.shape[1]), F32),
        in_specs=[pl.BlockSpec(memory_space=pltpu.SMEM), vmem, vmem, vmem],
        out_specs=vmem,
        scratch_shapes=[pltpu.VMEM((width, 2 * half * 128), BF16)],
        compiler_params=params(16),
    )(spot, near, far, cotangent)


def assemble(spot, near, far):
    count = 2 * near.shape[0]

    def kernel(spot_ref, near_ref, far_ref, out_ref):
        for slot in range(count):
            place = lax.bitwise_xor(spot_ref[0], DOUBLING[slot])
            out_ref[place] = (near_ref if slot < count // 2 else far_ref)[slot % (count // 2)]

    vmem = pl.BlockSpec(memory_space=pltpu.VMEM)
    return pl.pallas_call(
        kernel,
        out_shape=pltpu.HBM((count,) + near.shape[1:], BF16),
        in_specs=[pl.BlockSpec(memory_space=pltpu.SMEM), vmem, vmem],
        out_specs=vmem,
        compiler_params=params(8),
    )(spot, near, far)


def upstream_part(spot, cotangent, out_weight, slices):
    slice_rows = cotangent.shape[0] // slices

    def kernel(spot_ref, cot_ref, weight_ref, keep_ref, send_ref):
        for slot in range(slices):
            first = pl.multiple_of(lax.bitwise_xor(spot_ref[0], HALVING[slot]) * slice_rows, slice_rows)
            part = matmul(cot_ref[pl.ds(first, slice_rows), :], weight_ref[...], NT).astype(BF16)
            if slot < slices // 2:
                keep_ref[slot] = part
            else:
                send_ref[slot - slices // 2] = part

    vmem = pl.BlockSpec(memory_space=pltpu.VMEM)
    half = jax.ShapeDtypeStruct((slices // 2, slice_rows, out_weight.shape[0]), BF16)
    return pl.pallas_call(
        kernel,
        out_shape=(half, half),
        in_specs=[pl.BlockSpec(memory_space=pltpu.SMEM), vmem, vmem],
        out_specs=(vmem, vmem),
        compiler_params=params(16),
    )(spot, cotangent, out_weight)


def per_device(
    queries, key_vectors, value_vectors, cotangent, out_weight, frame_valid, group_offset, guide_index
):
    seq_count, fsdp_count = lax.axis_size("seq"), lax.axis_size("fsdp")
    fsdp_index = lax.axis_index("fsdp")
    block_rows = key_vectors.shape[1]
    group_rows, width = queries.shape[1], queries.shape[2]
    slice_rows = group_rows // fsdp_count
    tied = lax.optimization_barrier

    def over_seq(x):
        return lax.all_to_all(x, "seq", 0, 0, tiled=True)

    def over_fsdp(x):
        return lax.all_to_all(x, "fsdp", 0, 0, tiled=True)

    def partner(x, bit):
        return lax.ppermute(x, "fsdp", [(s, s ^ bit) for s in range(fsdp_count)])

    def halved(keep, send):
        for bit in (2, 4):
            total = (keep.astype(F32) + partner(send, bit).astype(F32)).astype(BF16)
            half = total.shape[0] // 2
            keep, send = total[:half], total[half:]
        return keep, partner(send, 1)

    def doubled(block):
        near = block[None]
        for bit in (4, 2):
            near = jnp.concatenate([near, partner(near, bit)])
        return near, partner(near, 1)

    spot = fsdp_index.astype(jnp.int32)[None]
    guide = 1.5 + guide_index[0].astype(F32) / 1024.0
    own_weight = jnp.where(lax.axis_index("cfg") == 0, guide, 1.0 - guide)

    packed = pack_blocks(key_vectors, value_vectors, seq_count)
    packed, cotangent_after = tied((packed, cotangent))
    kv = over_seq(packed)

    keep, arrived = halved(*upstream_part(spot, cotangent_after, out_weight, fsdp_count))
    upstream = own_weight * (keep[0].astype(F32) + arrived[0].astype(F32))
    query = queries.reshape(fsdp_count, slice_rows, width)

    block_ids = jnp.arange(seq_count, dtype=jnp.int32)
    block_start = (block_ids * fsdp_count + fsdp_index) * block_rows
    row_ids = jnp.arange(block_rows, dtype=jnp.int32)
    positions = (block_start[:, None] + row_ids[None, :]).reshape(-1)
    frame_match = (positions // FRAME_TOK)[:, None] == jnp.arange(
        frame_valid.shape[0], dtype=jnp.int32
    )[None, :]
    valid = jnp.sum(jnp.where(frame_match, frame_valid[None, :], 0), axis=1) == 1
    bias = jnp.broadcast_to(
        jnp.where(valid, 0.0, NEG_LARGE).astype(F32)[:, None], (positions.shape[0], 128)
    )
    frequency = 10000.0 ** (-jnp.arange(HEAD_DIM // 2, dtype=F32) / (HEAD_DIM // 2))
    twice = jnp.concatenate([frequency, frequency])
    block_angle = (block_start.astype(F32)[:, None] * twice[None, :])[:, None, :]
    row_angle = row_ids.astype(F32)[:, None] * twice[None, :]
    tables = (jnp.cos(block_angle), jnp.sin(block_angle), jnp.cos(row_angle), jnp.sin(row_angle))
    query_positions = (
        group_offset[0] + fsdp_index * slice_rows + jnp.arange(slice_rows, dtype=jnp.int32)
    )
    query_angle = query_positions.astype(F32)[None, :] * frequency[:, None]
    query_tables = (jnp.cos(query_angle), jnp.sin(query_angle))
    upstream, bias, tables = tied((upstream.astype(BF16), bias, tables))
    upstream = assemble(spot, *doubled(upstream))

    exponent, out_parts, own_stats, own_top = forward(kv, query, upstream, bias)
    stats = over_fsdp(own_stats)
    grads, query_keep, query_send, out_keep, out_send = backward(
        spot, kv, query, upstream, exponent, stats, own_stats, own_top, out_parts, tables
    )
    key_grad, value_grad = unpack_blocks(over_seq(grads))

    query_slice = merge_query_grad(*halved(query_keep, query_send), *query_tables)
    query_grad = query_slice[None]

    out_keep, arrived = halved(out_keep, out_send)
    attn_rows = (out_keep[0].astype(F32) + arrived[0].astype(F32)).astype(BF16)
    other_rows = lax.ppermute(attn_rows, "cfg", [(0, 1), (1, 0)])
    mixed = own_weight * attn_rows.astype(F32) + (1.0 - own_weight) * other_rows.astype(F32)
    weight_grad = projection_grad(spot, *doubled(mixed.astype(BF16)), cotangent)
    return (query_grad, key_grad, value_grad, weight_grad)


def solution(mesh):
    placed = (
        P("cfg", None, "seq"),
        P("cfg", ("seq", "fsdp"), None),
        P("cfg", ("seq", "fsdp"), None),
        P(None, "fsdp"),
        P("seq", "fsdp"),
        P(),
        P(),
        P(),
    )
    return jax.shard_map(
        per_device,
        mesh=mesh,
        in_specs=placed,
        out_specs=(
            P("cfg", "fsdp", "seq"),
            P("cfg", ("seq", "fsdp"), None),
            P("cfg", ("seq", "fsdp"), None),
            P("seq", "fsdp"),
        ),
        check_vma=False,
    )
```

```python
import math

import jax
import jax.numpy as jnp
from jax import lax
from jax.experimental import pallas as pl
from jax.experimental.pallas import tpu as pltpu
from jax.sharding import PartitionSpec as P

HEAD_DIM = 128
FRAME_TOK = 3600
NEG_LARGE = -1e30
NEG_FLOOR = -1e29
LOSS_SCALE = 128.0
SCALE = 1.0 / math.sqrt(HEAD_DIM)
EXP2_SCALE = SCALE * math.log2(math.e)
BF16 = jnp.bfloat16
F32 = jnp.float32
MIB = 1024 * 1024

HALVING = (0, 1, 4, 5, 2, 3, 6, 7)
DOUBLING = (0, 4, 2, 6, 1, 5, 3, 7)
NT = (((1,), (1,)), ((), ()))
TN = (((0,), (0,)), ((), ()))


def matmul(a, b, dims=(((1,), (0,)), ((), ()))):
    return lax.dot_general(a, b, dims, preferred_element_type=F32)


def params(mib):
    return pltpu.CompilerParams(vmem_limit_bytes=mib * MIB)


def pack_blocks(keys, values, parts):
    rows, width = keys.shape[1], keys.shape[2] // parts
    per = 8

    def kernel(k_ref, v_ref, out_ref):
        for which, ref in enumerate((k_ref, v_ref)):
            for part in range(per):
                out_ref[part, which] = ref[0, :, part * width : (part + 1) * width]

    return pl.pallas_call(
        kernel,
        grid=(parts // per,),
        out_shape=pltpu.HBM((parts, 2, rows, width), keys.dtype),
        in_specs=[pl.BlockSpec((1, rows, per * width), lambda i: (0, 0, i))] * 2,
        out_specs=pl.BlockSpec((per, 2, rows, width), lambda i: (i, 0, 0, 0)),
        compiler_params=params(60),
    )(keys, values)


def unpack_blocks(packed):
    parts, _, rows, width = packed.shape
    per = 4

    def kernel(in_ref, k_ref, v_ref):
        for which, ref in enumerate((k_ref, v_ref)):
            for part in range(per):
                ref[0, :, part * width : (part + 1) * width] = in_ref[part, which]

    shape = jax.ShapeDtypeStruct((1, rows, parts * width), packed.dtype)
    return pl.pallas_call(
        kernel,
        grid=(parts // per,),
        out_shape=(shape, shape),
        in_specs=[pl.BlockSpec((per, 2, rows, width), lambda i: (i, 0, 0, 0))],
        out_specs=(pl.BlockSpec((1, rows, per * width), lambda i: (0, 0, i)),) * 2,
        compiler_params=params(16),
    )(packed)


def forward_kernel(kv_ref, query_ref, up_ref, bias_ref, exp_ref, out_ref, stat_ref, top_ref):
    key_rows = kv_ref.shape[0] * kv_ref.shape[2]
    per, slice_rows = query_ref.shape[0], query_ref.shape[1]
    query_rows = per * slice_rows
    heads = kv_ref.shape[3] // HEAD_DIM
    bias = jnp.concatenate([bias_ref[...]] * (query_rows // 128), axis=1)
    rows, tops = [], []
    for head in range(heads):
        lanes = slice(head * HEAD_DIM, (head + 1) * HEAD_DIM)
        keys = kv_ref[:, 0, :, lanes].reshape(key_rows, HEAD_DIM)
        values = kv_ref[:, 1, :, lanes].reshape(key_rows, HEAD_DIM)
        query = query_ref[:, :, lanes].reshape(query_rows, HEAD_DIM)
        scores = matmul(keys, query, NT) * EXP2_SCALE + bias
        top = jnp.maximum(jnp.max(scores, axis=0, keepdims=True), NEG_FLOOR)
        exponent = jnp.exp2(scores - top)
        total = jnp.sum(exponent, axis=0, keepdims=True)
        exponent_bf = exponent.astype(BF16)
        exp_ref[head] = exponent_bf
        safe = jnp.maximum(total, 1e-30)
        output = matmul(values, exponent_bf, TN) * (1.0 / safe)
        upstream = up_ref[:, :, lanes].reshape(query_rows, HEAD_DIM).astype(F32)
        rows.append(jnp.where(total > 0.0, top + jnp.log2(safe), NEG_FLOOR))
        rows.append(jnp.sum(upstream.T * output, axis=0, keepdims=True))
        tops.append(top)
        for part in range(per):
            out_ref[part, lanes, :] = output[
                :, part * slice_rows : (part + 1) * slice_rows
            ].astype(BF16)
    stats = jnp.concatenate(rows, axis=0)
    for copy in range(stat_ref.shape[0]):
        stat_ref[copy] = stats
    top_ref[...] = jnp.concatenate(tops, axis=0)


def forward(kv, query, upstream, bias):
    blocks, _, block_rows, width = kv.shape
    key_rows = blocks * block_rows
    slices, slice_rows, _ = query.shape
    queries = slices * slice_rows
    heads = width // HEAD_DIM
    step = 512
    per = step // slice_rows
    return pl.pallas_call(
        forward_kernel,
        grid=(queries // step,),
        in_specs=[
            pl.BlockSpec((blocks, 2, block_rows, width), lambda i: (0, 0, 0, 0)),
            pl.BlockSpec((per, slice_rows, width), lambda i: (i, 0, 0)),
            pl.BlockSpec((per, slice_rows, width), lambda i: (i, 0, 0)),
            pl.BlockSpec((key_rows, 128), lambda i: (0, 0)),
        ],
        out_specs=(
            pl.BlockSpec((heads, key_rows, step), lambda i: (0, 0, i)),
            pl.BlockSpec((per, width, slice_rows), lambda i: (i, 0, 0)),
            pl.BlockSpec((slices, 2 * heads, step), lambda i: (0, 0, i)),
            pl.BlockSpec((heads, step), lambda i: (0, i)),
        ),
        out_shape=(
            jax.ShapeDtypeStruct((heads, key_rows, queries), BF16),
            pltpu.HBM((slices, width, slice_rows), BF16),
            pltpu.HBM((slices, 2 * heads, queries), F32),
            jax.ShapeDtypeStruct((heads, queries), F32),
        ),
        compiler_params=pltpu.CompilerParams(vmem_limit_bytes=61_300_000),
        cost_estimate=pl.CostEstimate(
            flops=4 * heads * queries * key_rows * HEAD_DIM,
            bytes_accessed=12 * MIB,
            transcendentals=heads * queries * key_rows,
        ),
    )(kv, query, upstream, bias)


def merged_stats(stats, head):
    logs = stats[:, 2 * head, :]
    deltas = stats[:, 2 * head + 1, :]
    top = jnp.max(logs, axis=0, keepdims=True)
    shares = jnp.exp2(logs - top)
    total = jnp.sum(shares, axis=0, keepdims=True)
    return top + jnp.log2(total), jnp.sum(deltas * shares, axis=0, keepdims=True) / total


def backward_kernel(
    spot_ref,
    kv_ref,
    query_ref,
    up_ref,
    exp_ref,
    stats_ref,
    log_ref,
    own_ref,
    parts_ref,
    cos_block,
    sin_block,
    cos_row,
    sin_row,
    grad_ref,
    keep_ref,
    send_ref,
    out_keep_ref,
    out_send_ref,
    acc_ref,
):
    step = pl.program_id(0)
    blocks, block_rows = kv_ref.shape[0], kv_ref.shape[2]
    key_rows = blocks * block_rows
    query_rows = query_ref.shape[0] * query_ref.shape[1]
    heads = kv_ref.shape[3] // HEAD_DIM
    stats = stats_ref[...]
    for head in range(heads):
        lanes = slice(head * HEAD_DIM, (head + 1) * HEAD_DIM)
        log_total, delta = merged_stats(stats, head)
        factor = jnp.exp2(own_ref[head : head + 1, :] - log_total)
        keys = kv_ref[:, 0, :, lanes].reshape(key_rows, HEAD_DIM)
        values = kv_ref[:, 1, :, lanes].reshape(key_rows, HEAD_DIM)
        query = query_ref[:, :, lanes].reshape(query_rows, HEAD_DIM)
        upstream = up_ref[:, :, lanes].reshape(query_rows, HEAD_DIM)
        probability = exp_ref[head].astype(F32) * factor
        value_grad = matmul(probability.astype(BF16), upstream)
        prob_grad = matmul(values, upstream, NT)
        score_grad = (probability * (prob_grad - delta)).astype(BF16)
        key_grad = matmul(score_grad, query) * SCALE
        query_part = matmul(keys, score_grad, TN)
        for block in range(blocks):
            part = key_grad[block * block_rows : (block + 1) * block_rows, :]
            cos_a = cos_block[block]
            sin_a = sin_block[block]
            cosine = cos_a * cos_row[...] - sin_a * sin_row[...]
            sine = sin_a * cos_row[...] + cos_a * sin_row[...]
            signed = jnp.where(
                lax.broadcasted_iota(jnp.int32, sine.shape, 1) < HEAD_DIM // 2, sine, -sine
            )
            turned = part * cosine + pltpu.roll(part, HEAD_DIM // 2, 1) * signed
            grad_ref[block, 0, :, lanes] = turned.astype(BF16)
            grad_ref[block, 1, :, lanes] = value_grad[
                block * block_rows : (block + 1) * block_rows, :
            ].astype(BF16)

        @pl.when(step == 0)
        def _():
            acc_ref[lanes, :] = query_part

        @pl.when(step > 0)
        def _():
            acc_ref[lanes, :] += query_part

    @pl.when(step == pl.num_programs(0) - 1)
    def _():
        half = keep_ref.shape[0]
        for slot in range(2 * half):
            place = lax.bitwise_xor(spot_ref[0], HALVING[slot])
            spread = pl.ds(pl.multiple_of(place * 128, 128), 128)
            query_part = (acc_ref[:, spread] * SCALE).astype(BF16)
            part = parts_ref[place].astype(F32)
            weighted = []
            for head in range(heads):
                log_total, _ = merged_stats(stats_ref[:, :, spread], head)
                share = jnp.exp2(log_ref[0, 2 * head : 2 * head + 1, spread] - log_total)
                weighted.append(part[head * HEAD_DIM : (head + 1) * HEAD_DIM, :] * share)
            out_part = jnp.concatenate(weighted, axis=0).astype(BF16)
            if slot < half:
                keep_ref[slot] = query_part
                out_keep_ref[slot] = out_part
            else:
                send_ref[slot - half] = query_part
                out_send_ref[slot - half] = out_part


def backward(spot, kv, query, upstream, exponent, stats, own_stats, own_top, out_parts, tables):
    blocks, _, block_rows, width = kv.shape
    slices, slice_rows, _ = query.shape
    queries = slices * slice_rows
    heads = width // HEAD_DIM
    per = 4
    key_rows = blocks * block_rows
    whole = lambda shape: pl.BlockSpec(shape, lambda i, s: (0,) * len(shape))
    half = pltpu.HBM((slices // 2, width, slice_rows), BF16)
    return pl.pallas_call(
        backward_kernel,
        grid_spec=pltpu.PrefetchScalarGridSpec(
            num_scalar_prefetch=1,
            grid=(blocks // per,),
            in_specs=[
                pl.BlockSpec((per, 2, block_rows, width), lambda i, s: (i, 0, 0, 0)),
                whole(query.shape),
                whole(query.shape),
                pl.BlockSpec((heads, per * block_rows, queries), lambda i, s: (0, i, 0)),
                whole(stats.shape),
                whole((1,) + own_stats.shape[1:]),
                whole(own_top.shape),
                whole(out_parts.shape),
                pl.BlockSpec((per, 1, HEAD_DIM), lambda i, s: (i, 0, 0)),
                pl.BlockSpec((per, 1, HEAD_DIM), lambda i, s: (i, 0, 0)),
                whole((block_rows, HEAD_DIM)),
                whole((block_rows, HEAD_DIM)),
            ],
            out_specs=(
                pl.BlockSpec((per, 2, block_rows, width), lambda i, s: (i, 0, 0, 0)),
            )
            + (whole((slices // 2, width, slice_rows)),) * 4,
            scratch_shapes=[pltpu.VMEM((width, queries), F32)],
        ),
        out_shape=(pltpu.HBM((blocks, 2, block_rows, width), BF16), half, half, half, half),
        compiler_params=params(60),
        cost_estimate=pl.CostEstimate(
            flops=8 * heads * queries * key_rows * HEAD_DIM,
            bytes_accessed=14 * MIB,
            transcendentals=0,
        ),
    )(spot, kv, query, upstream, exponent, stats, own_stats, own_top, out_parts, *tables)


def merge_query_grad(kept, arrived, cosine, sine):
    def kernel(kept_ref, arrived_ref, cos_ref, sin_ref, out_ref):
        total = kept_ref[0].astype(F32) + arrived_ref[0].astype(F32)
        half = HEAD_DIM // 2
        turned = []
        for head in range(total.shape[0] // HEAD_DIM):
            first = total[head * HEAD_DIM : head * HEAD_DIM + half, :]
            second = total[head * HEAD_DIM + half : (head + 1) * HEAD_DIM, :]
            turned.append(first * cos_ref[...] + second * sin_ref[...])
            turned.append(second * cos_ref[...] - first * sin_ref[...])
        out_ref[...] = jnp.concatenate(turned, axis=0).T.astype(BF16)

    return pl.pallas_call(
        kernel,
        out_shape=jax.ShapeDtypeStruct((kept.shape[2], kept.shape[1]), BF16),
        compiler_params=params(8),
    )(kept, arrived, cosine, sine)


def projection_grad(spot, near, far, cotangent):
    half, width, _ = near.shape

    def kernel(spot_ref, near_ref, far_ref, cot_ref, out_ref, joined_ref):
        for slot in range(2 * half):
            first = pl.multiple_of(lax.bitwise_xor(spot_ref[0], DOUBLING[slot]) * 128, 128)
            ref = near_ref if slot < half else far_ref
            joined_ref[:, pl.ds(first, 128)] = ref[slot % half]
        out_ref[...] = matmul(joined_ref[...], cot_ref[...]) * (1.0 / LOSS_SCALE)

    vmem = pl.BlockSpec(memory_space=pltpu.VMEM)
    return pl.pallas_call(
        kernel,
        out_shape=jax.ShapeDtypeStruct((width, cotangent.shape[1]), F32),
        in_specs=[pl.BlockSpec(memory_space=pltpu.SMEM), vmem, vmem, vmem],
        out_specs=vmem,
        scratch_shapes=[pltpu.VMEM((width, 2 * half * 128), BF16)],
        compiler_params=params(16),
    )(spot, near, far, cotangent)


def assemble(spot, near, far):
    count = 2 * near.shape[0]

    def kernel(spot_ref, near_ref, far_ref, out_ref):
        for slot in range(count):
            place = lax.bitwise_xor(spot_ref[0], DOUBLING[slot])
            out_ref[place] = (near_ref if slot < count // 2 else far_ref)[slot % (count // 2)]

    vmem = pl.BlockSpec(memory_space=pltpu.VMEM)
    return pl.pallas_call(
        kernel,
        out_shape=pltpu.HBM((count,) + near.shape[1:], BF16),
        in_specs=[pl.BlockSpec(memory_space=pltpu.SMEM), vmem, vmem],
        out_specs=vmem,
        compiler_params=params(8),
    )(spot, near, far)


def upstream_part(spot, cotangent, out_weight, slices):
    slice_rows = cotangent.shape[0] // slices

    def kernel(spot_ref, cot_ref, weight_ref, keep_ref, send_ref):
        for slot in range(slices):
            first = pl.multiple_of(lax.bitwise_xor(spot_ref[0], HALVING[slot]) * slice_rows, slice_rows)
            part = matmul(cot_ref[pl.ds(first, slice_rows), :], weight_ref[...], NT).astype(BF16)
            if slot < slices // 2:
                keep_ref[slot] = part
            else:
                send_ref[slot - slices // 2] = part

    vmem = pl.BlockSpec(memory_space=pltpu.VMEM)
    half = jax.ShapeDtypeStruct((slices // 2, slice_rows, out_weight.shape[0]), BF16)
    return pl.pallas_call(
        kernel,
        out_shape=(half, half),
        in_specs=[pl.BlockSpec(memory_space=pltpu.SMEM), vmem, vmem],
        out_specs=(vmem, vmem),
        compiler_params=params(16),
    )(spot, cotangent, out_weight)


def per_device(
    queries, key_vectors, value_vectors, cotangent, out_weight, frame_valid, group_offset, guide_index
):
    seq_count, fsdp_count = lax.axis_size("seq"), lax.axis_size("fsdp")
    fsdp_index = lax.axis_index("fsdp")
    block_rows = key_vectors.shape[1]
    group_rows, width = queries.shape[1], queries.shape[2]
    slice_rows = group_rows // fsdp_count
    tied = lax.optimization_barrier

    def over_seq(x):
        return lax.all_to_all(x, "seq", 0, 0, tiled=True)

    def over_fsdp(x):
        return lax.all_to_all(x, "fsdp", 0, 0, tiled=True)

    def partner(x, bit):
        return lax.ppermute(x, "fsdp", [(s, s ^ bit) for s in range(fsdp_count)])

    def halved(keep, send):
        for bit in (2, 4):
            total = (keep.astype(F32) + partner(send, bit).astype(F32)).astype(BF16)
            half = total.shape[0] // 2
            keep, send = total[:half], total[half:]
        return keep, partner(send, 1)

    def doubled(block):
        near = block[None]
        for bit in (4, 2):
            near = jnp.concatenate([near, partner(near, bit)])
        return near, partner(near, 1)

    spot = fsdp_index.astype(jnp.int32)[None]
    guide = 1.5 + guide_index[0].astype(F32) / 1024.0
    own_weight = jnp.where(lax.axis_index("cfg") == 0, guide, 1.0 - guide)

    packed = pack_blocks(key_vectors, value_vectors, seq_count)
    packed, cotangent_after = tied((packed, cotangent))
    kv = over_seq(packed)

    keep, arrived = halved(*upstream_part(spot, cotangent_after, out_weight, fsdp_count))
    upstream = own_weight * (keep[0].astype(F32) + arrived[0].astype(F32))
    query = queries.reshape(fsdp_count, slice_rows, width)

    block_ids = jnp.arange(seq_count, dtype=jnp.int32)
    block_start = (block_ids * fsdp_count + fsdp_index) * block_rows
    row_ids = jnp.arange(block_rows, dtype=jnp.int32)
    positions = (block_start[:, None] + row_ids[None, :]).reshape(-1)
    frame_match = (positions // FRAME_TOK)[:, None] == jnp.arange(
        frame_valid.shape[0], dtype=jnp.int32
    )[None, :]
    valid = jnp.sum(jnp.where(frame_match, frame_valid[None, :], 0), axis=1) == 1
    bias = jnp.broadcast_to(
        jnp.where(valid, 0.0, NEG_LARGE).astype(F32)[:, None], (positions.shape[0], 128)
    )
    frequency = 10000.0 ** (-jnp.arange(HEAD_DIM // 2, dtype=F32) / (HEAD_DIM // 2))
    twice = jnp.concatenate([frequency, frequency])
    block_angle = (block_start.astype(F32)[:, None] * twice[None, :])[:, None, :]
    row_angle = row_ids.astype(F32)[:, None] * twice[None, :]
    tables = (jnp.cos(block_angle), jnp.sin(block_angle), jnp.cos(row_angle), jnp.sin(row_angle))
    query_positions = (
        group_offset[0] + fsdp_index * slice_rows + jnp.arange(slice_rows, dtype=jnp.int32)
    )
    query_angle = query_positions.astype(F32)[None, :] * frequency[:, None]
    query_tables = (jnp.cos(query_angle), jnp.sin(query_angle))
    upstream, bias, tables = tied((upstream.astype(BF16), bias, tables))
    upstream = assemble(spot, *doubled(upstream))

    exponent, out_parts, own_stats, own_top = forward(kv, query, upstream, bias)
    stats = over_fsdp(own_stats)
    grads, query_keep, query_send, out_keep, out_send = backward(
        spot, kv, query, upstream, exponent, stats, own_stats, own_top, out_parts, tables
    )
    key_grad, value_grad = unpack_blocks(over_seq(grads))

    query_slice = merge_query_grad(*halved(query_keep, query_send), *query_tables)
    query_grad = query_slice[None]

    out_keep, arrived = halved(out_keep, out_send)
    attn_rows = (out_keep[0].astype(F32) + arrived[0].astype(F32)).astype(BF16)
    other_rows = lax.ppermute(attn_rows, "cfg", [(0, 1), (1, 0)])
    mixed = own_weight * attn_rows.astype(F32) + (1.0 - own_weight) * other_rows.astype(F32)
    weight_grad = projection_grad(spot, *doubled(mixed.astype(BF16)), cotangent)
    return (query_grad, key_grad, value_grad, weight_grad)


def solution(mesh):
    placed = (
        P("cfg", None, "seq"),
        P("cfg", ("seq", "fsdp"), None),
        P("cfg", ("seq", "fsdp"), None),
        P(None, "fsdp"),
        P("seq", "fsdp"),
        P(),
        P(),
        P(),
    )
    return jax.shard_map(
        per_device,
        mesh=mesh,
        in_specs=placed,
        out_specs=(
            P("cfg", "fsdp", "seq"),
            P("cfg", ("seq", "fsdp"), None),
            P("cfg", ("seq", "fsdp"), None),
            P("seq", "fsdp"),
        ),
        check_vma=False,
    )
```
